32 devices in a mesh: dp: 4 (over y, x), seq: 8 (over z, core).
Axes of the slice: x: 2, y: 2, z: 4, core: 2. Of those that a mesh axis runs over, the one named last changes fastest.
Arguments:
- tokens: bfloat16 [8, 512, 512], P('dp', 'seq'), may hold values from -6 to 6
- memory: bfloat16 [8, 20, 512], P('dp'), may hold values from -6 to 6
- lengths: int32 [8], P('dp'), may hold values from 128 to 512, as said below
- w_qkv: bfloat16 [512, 1536], P(('dp', 'seq')), may hold values from -0.25 to 0.25
- b_query: bfloat16 [512], P(('dp', 'seq')), may hold values from -0.59765625 to 0.59765625
- b_value: bfloat16 [512], P(('dp', 'seq')), may hold values from -0.29882812 to 0.29882812
- w_out: bfloat16 [512, 512], P(('dp', 'seq')), may hold values from -1 to 1
- b_out: bfloat16 [512], P(('dp', 'seq')), may hold values from -3 to 3
- gain_one: bfloat16 [512], P(('dp', 'seq')), may hold values from 0.25 to 1.75
- shift_one: bfloat16 [512], P(('dp', 'seq')), may hold values from -3 to 3
- w_up: bfloat16 [512, 2048], P(('dp', 'seq')), may hold values from -0.25 to 0.25
- b_up: bfloat16 [2048], P(('dp', 'seq')), may hold values from -1.5 to 1.5
- w_down: bfloat16 [2048, 512], P(('dp', 'seq')), may hold values from -0.25 to 0.25
- b_down: bfloat16 [512], P(('dp', 'seq')), may hold values from -3 to 3
- gain_two: bfloat16 [512], P(('dp', 'seq')), may hold values from 0.25 to 1.75
- shift_two: bfloat16 [512], P(('dp', 'seq')), may hold values from -3 to 3
- cot_tokens: bfloat16 [8, 512, 512], P('dp', 'seq'), may hold values from -6 to 6
- cot_memory: bfloat16 [8, 20, 512], P('dp'), may hold values from -6 to 6
Outputs:
- layer_tokens: bfloat16 [8, 512, 512], P('dp', 'seq')
- layer_memory: bfloat16 [8, 20, 512], P('dp')
- input_grad_tokens: bfloat16 [8, 512, 512], P('dp', 'seq')
- input_grad_memory: bfloat16 [8, 20, 512], P('dp')
- grad_w_qkv: float32 [512, 1536], P(('dp', 'seq'))
- grad_b_query: float32 [512], P(('dp', 'seq'))
- grad_b_value: float32 [512], P(('dp', 'seq'))
- grad_w_out: float32 [512, 512], P(('dp', 'seq'))
- grad_b_out: float32 [512], P(('dp', 'seq'))
- grad_gain_one: float32 [512], P(('dp', 'seq'))
- grad_shift_one: float32 [512], P(('dp', 'seq'))
- grad_w_up: float32 [512, 2048], P(('dp', 'seq'))
- grad_b_up: float32 [2048], P(('dp', 'seq'))
- grad_w_down: float32 [2048, 512], P(('dp', 'seq'))
- grad_b_down: float32 [512], P(('dp', 'seq'))
- grad_gain_two: float32 [512], P(('dp', 'seq'))
- grad_shift_two: float32 [512], P(('dp', 'seq'))
- token_rms: float32 [8, 512], P('dp')
The draws below stay inside these ranges and needn't reach their ends.
Inputs may be any that keep to these rules, and one draw needn't show every extreme that they name: `lengths`: token positions below a slot's length are valid, the rest padding. Some slot has length 512 and some 512 // 4.
All inputs are finite; a program needn't handle non-finite values.
Results may differ from the reference program's by a relative error of at most 0.025.
Values may be sent and summed in bfloat16 or wider, within the bound.
No kernel may reach another device: no remote copies, remote signals or barrier semaphores. Data moves between devices by JAX's collectives and lax.ppermute only.
A program may use at most 128 MiB of HBM per device.

```python
import jax
import jax.numpy as jnp
from jax import lax

D = 512
HEADS = 8
HEAD_DIM = 64
FF = 2048
MEM = 20
SLOT_LEN = 512
SLOTS = 8


def draw_lengths(key, part):
    draw_values = jax.random.randint(key, (SLOTS,), SLOT_LEN // 4, SLOT_LEN + 1, dtype=jnp.int32)
    slot_order = jax.random.permutation(jax.random.fold_in(key, 7), SLOTS)
    draw_values = draw_values.at[slot_order[0]].set(SLOT_LEN)
    return draw_values.at[slot_order[1]].set(SLOT_LEN // 4)


def level_of(rng, extent, shards, least, largest):
    gain = 1.0
    for axis_at, blocks in shards:
        steps = jax.random.uniform(jax.random.fold_in(jax.random.fold_in(rng, 6), axis_at), (blocks,), jnp.float32, least / len(shards), largest / len(shards))
        gain = gain * jnp.repeat(jnp.exp(steps), extent[axis_at] // blocks).reshape((-1,) + (1,) * (len(extent) - 1 - axis_at))
    return gain


def normal_values(rng, dims, width, bound, pieces=(), held_as=jnp.bfloat16):
    level = level_of(rng, dims, pieces, -0.22, 0.18) if pieces else 1.0
    values = jax.random.normal(rng, dims, jnp.float32) * width * level
    return jnp.minimum(jnp.maximum(values, -bound), bound).astype(held_as)


def setup_inputs(seed: int = 0) -> dict:
    arg_keys = jax.random.split(jax.random.key(seed), 19)
    tokens = normal_values(arg_keys[0], (SLOTS, SLOT_LEN, D), 1.0, 6.0, ((0, 4), (1, 8)))
    memory = normal_values(arg_keys[1], (SLOTS, MEM, D), 1.0, 6.0, ((0, 4),))
    lengths = draw_lengths(jax.random.fold_in(arg_keys[18], 71), 0)
    w_qkv = normal_values(arg_keys[3], (D, 3 * D), D ** -0.5, 0.25, ((0, 32),))
    b_query = normal_values(arg_keys[4], (D,), 0.1, 0.59765625, ((0, 32),))
    b_value = normal_values(arg_keys[5], (D,), 0.05, 0.29882812, ((0, 32),))
    w_out = normal_values(arg_keys[6], (D, D), (D // 16) ** -0.5, 1.0, ((0, 32),))
    b_out = normal_values(arg_keys[7], (D,), 0.5, 3.0, ((0, 32),))
    gain_one = jnp.clip(1.0 + 0.15 * jax.random.normal(arg_keys[8], (D,), jnp.float32), 0.25, 1.75).astype(jnp.bfloat16)
    shift_one = normal_values(arg_keys[9], (D,), 0.5, 3.0, ((0, 32),))
    w_up = normal_values(arg_keys[10], (D, FF), D ** -0.5, 0.25, ((0, 32),))
    b_up = normal_values(arg_keys[11], (FF,), 0.25, 1.5, ((0, 32),))
    w_down = normal_values(arg_keys[12], (FF, D), (FF // 4) ** -0.5, 0.25, ((0, 32),))
    b_down = normal_values(arg_keys[13], (D,), 0.5, 3.0, ((0, 32),))
    gain_two = jnp.clip(1.0 + 0.15 * jax.random.normal(arg_keys[14], (D,), jnp.float32), 0.25, 1.75).astype(jnp.bfloat16)
    shift_two = normal_values(arg_keys[15], (D,), 0.5, 3.0, ((0, 32),))
    cot_tokens = normal_values(arg_keys[16], (SLOTS, SLOT_LEN, D), 1.0, 6.0, ((0, 4), (1, 8)))
    cot_memory = normal_values(arg_keys[17], (SLOTS, MEM, D), 1.0, 6.0, ((0, 4),))
    return {"tokens": tokens, "memory": memory, "lengths": lengths, "w_qkv": w_qkv, "b_query": b_query, "b_value": b_value, "w_out": w_out, "b_out": b_out, "gain_one": gain_one, "shift_one": shift_one, "w_up": w_up, "b_up": b_up, "w_down": w_down, "b_down": b_down, "gain_two": gain_two, "shift_two": shift_two, "cot_tokens": cot_tokens, "cot_memory": cot_memory}


@jax.custom_vjp
def low(v):
    return lax.optimization_barrier(v.astype(jnp.bfloat16)).astype(jnp.float32)

@jax.custom_vjp
def low_back(v):
    return v

def low_keep(v):
    return (low(v), None)

def low_pass(kept, grad):
    return (grad,)

def back_keep(v):
    return (v, None)

def back_low(kept, grad):
    return (low(grad),)
low.defvjp(low_keep, low_pass)
low_back.defvjp(back_keep, back_low)

def matmul(left_side, right_side):
    return jnp.dot(left_side, right_side, precision=lax.Precision.HIGHEST, preferred_element_type=jnp.float32)

def smooth_unit(values):
    return 0.5 * values * (1.0 + jnp.tanh(0.7978845608 * (values + 0.044715 * values * values * values)))

def layer_norm(hidden, scale_gain, offset):
    center = hidden - lax.optimization_barrier(jnp.mean(hidden, axis=-1, keepdims=True))
    variance = lax.optimization_barrier(jnp.mean(center * center, axis=-1, keepdims=True))
    return center * lax.rsqrt(variance + 1e-05) * scale_gain + offset

def split_heads(matrix):
    return jnp.transpose(matrix.reshape(matrix.shape[0], HEADS, HEAD_DIM), (1, 0, 2))

def slot_forward(param_set, memory_part, tokens_part, valid_rows):
    w_qkv, b_query, b_value, w_out, b_out, gain_one, shift_one, w_up, b_up, w_down, b_down, gain_two, shift_two = param_set
    model_width = w_qkv.shape[0]
    stacked = jnp.concatenate([memory_part, tokens_part], axis=0)
    bias_all = jnp.concatenate([b_query, jnp.zeros_like(b_query), b_value])
    packed = low_back(low(matmul(stacked, w_qkv) + bias_all))
    query_heads = split_heads(packed[:, :model_width])
    key_heads = split_heads(packed[:, model_width:2 * model_width])
    value_heads = split_heads(packed[:, 2 * model_width:])
    keep_mask = valid_rows > 0.5

    def one_head(triple):
        head_query, head_key, head_value = triple
        scores = low_back(jnp.einsum('qd,kd->qk', head_query, head_key, precision=lax.Precision.HIGHEST) * 0.125)
        scores = jnp.where(keep_mask[None, :], scores, -1e+30)
        shifted = scores - lax.optimization_barrier(jnp.max(scores, axis=-1, keepdims=True))
        expos = jnp.exp(shifted)
        weights = expos / lax.optimization_barrier(jnp.sum(expos, axis=-1, keepdims=True))
        return matmul(low(weights), head_value)
    heads_out = lax.map(jax.checkpoint(one_head), (query_heads, key_heads, value_heads))
    attn = low_back(low(jnp.transpose(heads_out, (1, 0, 2)).reshape(stacked.shape[0], model_width)))
    branch = low_back(matmul(attn, w_out) + b_out)
    normed_one = layer_norm(stacked + branch, gain_one, shift_one)
    up_linear = low_back(matmul(low(normed_one), w_up) + b_up)
    hidden = low(smooth_unit(up_linear))
    feed_branch = low_back(matmul(hidden, w_down) + b_down)
    result = layer_norm(normed_one + feed_branch, gain_two, shift_two) * valid_rows[:, None]
    return (result, feed_branch)

def reference(tokens, memory, lengths, w_qkv, b_query, b_value, w_out, b_out, gain_one, shift_one, w_up, b_up, w_down, b_down, gain_two, shift_two, cot_tokens, cot_memory):
    params = tuple((item.astype(jnp.float32) for item in (w_qkv, b_query, b_value, w_out, b_out, gain_one, shift_one, w_up, b_up, w_down, b_down, gain_two, shift_two)))
    positions = jnp.arange(SLOT_LEN, dtype=jnp.int32)

    def per_slot(summed, inputs):
        memory_in, tokens_in, length, cot_tok_in, cot_mem_in = inputs
        valid_rows = jnp.concatenate([jnp.ones((MEM,), jnp.float32), (positions < length).astype(jnp.float32)])

        def forward(param_set, memory_part, tokens_part):
            return slot_forward(param_set, memory_part, tokens_part, valid_rows)
        result, backward, feed_branch = jax.vjp(forward, params, memory_in, tokens_in, has_aux=True)
        grad_params, grad_memory_in, grad_tokens_in = backward(jnp.concatenate([cot_mem_in, cot_tok_in], axis=0))
        summed = jax.tree.map(lambda running, update: running + update, summed, grad_params)
        token_part = feed_branch[MEM:]
        squares = lax.optimization_barrier(jnp.sum(token_part * token_part * valid_rows[MEM:, None], axis=0))
        root_mean = jnp.sqrt(squares / length.astype(jnp.float32))
        return (summed, (result[MEM:].astype(jnp.bfloat16), result[:MEM].astype(jnp.bfloat16), grad_tokens_in.astype(jnp.bfloat16), grad_memory_in.astype(jnp.bfloat16), root_mean))
    initial = tuple((jnp.zeros_like(item) for item in params))
    summed, emitted = lax.scan(per_slot, initial, (memory.astype(jnp.float32), tokens.astype(jnp.float32), lengths, cot_tokens.astype(jnp.float32), cot_memory.astype(jnp.float32)))
    return (emitted[0], emitted[1], emitted[2], emitted[3], summed[0], summed[1], summed[2], summed[3], summed[4], summed[5], summed[6], summed[7], summed[8], summed[9], summed[10], summed[11], summed[12], emitted[4])
```

```python
import functools

import jax
import jax.numpy as jnp
from jax import lax
from jax.experimental import pallas as pl
from jax.experimental.pallas import tpu as pltpu
from jax.sharding import PartitionSpec as P

HEADS = 8
HEAD_DIM = 64
WIDTH = 512
FF = 2048
BLOCKS = 32
ROWS = 128
MEM_PAD = 32
OWN = ROWS + MEM_PAD
MEM_KEYS = 128
LANES = 128
MIB = 1 << 20

BF = jnp.bfloat16
F32 = jnp.float32
NN = (((1,), (0,)), ((), ()))
NT = (((1,), (1,)), ((), ()))
TN = (((0,), (0,)), ((), ()))

GATHER_QKV = (2, 3, 4, 1, 0)
GATHER_UP = (2, 4, 1, 3, 0)
GATHER_DOWN = (2, 1, 3, 4, 0)
REDUCE_UP = (0, 1, 4, 3, 2)
REDUCE_DOWN = (0, 3, 1, 4, 2)
REDUCE_QKV = (0, 4, 3, 1, 2)


def dot(a, b, dims=NN):
    return lax.dot_general(a, b, dims, preferred_element_type=F32)


def low(v):
    return v.astype(BF)


def high(v):
    return v.astype(F32)


def split_three(v):
    first = high(low(v))
    second = high(low(v - first))
    return first, second, high(low(v - first - second))


def aligned(index, size):
    return pl.ds(pl.multiple_of(index * size, size), size)


class Layout:
    def __init__(self, mesh):
        self.dp = mesh.shape["dp"]
        self.seq = mesh.shape["seq"]
        self.devices = self.dp * self.seq
        self.low_bits = (self.devices // BLOCKS).bit_length() - 1
        self.group = self.seq // 2
        self.seq_bits = self.seq.bit_length() - 1

    def dim(self, bit):
        if bit < self.seq_bits:
            return "seq", 1 << bit
        return "dp", 1 << (bit - self.seq_bits)

    def swap(self, x, bit):
        axis, mask = self.dim(bit)
        size = self.seq if axis == "seq" else self.dp
        return lax.ppermute(x, axis, [(i, i ^ mask) for i in range(size)])

    def block_swap(self, x, bit):
        return self.swap(x, bit + self.low_bits)

    def device(self):
        return lax.axis_index("dp") * self.seq + lax.axis_index("seq")

    def block(self):
        return self.device() >> self.low_bits

    def join_low(self, x, axis):
        for bit in range(self.low_bits):
            other = self.swap(x, bit)
            first = (self.device() >> bit) % 2 == 0
            x = jnp.where(
                first, jnp.concatenate([x, other], axis), jnp.concatenate([other, x], axis)
            )
        return x

    def reduce_low(self, x, axis):
        for bit in reversed(range(self.low_bits)):
            first = (self.device() >> bit) % 2 == 0
            lower, upper = jnp.split(x, 2, axis)
            other = self.swap(jnp.where(first, upper, lower), bit)
            x = jnp.where(first, lower, upper) + other
        return x

    def gather(self, x, order):
        held = x
        for bit in order[:3]:
            held = jnp.concatenate([held, self.block_swap(held, bit)], 0)
        last = self.block_swap(held, order[3])
        return held, last, self.block_swap(held, order[4]), self.block_swap(last, order[4])

    def reduce(self, keep, send, order, fold):
        other = self.block_swap(send, order[0])
        for bit in order[1:]:
            keep, send = fold(keep, other)
            other = self.block_swap(send, bit)
        return keep, other

    def gather_group(self, x):
        near = x
        mask = self.group // 2
        while mask > 1:
            near = jnp.concatenate([near, self.swap(near, mask.bit_length() - 1)], 0)
            mask //= 2
        return near, self.swap(near, 0)

    def group_masks(self):
        near = [0]
        mask = self.group // 2
        while mask > 1:
            near += [m ^ mask for m in near]
            mask //= 2
        return near, [m ^ 1 for m in near]


def gather_masks(order):
    held = [0]
    for bit in order[:3]:
        held = held + [m ^ (1 << bit) for m in held]
    last = [m ^ (1 << order[3]) for m in held]
    swapped = [[m ^ (1 << order[4]) for m in part] for part in (held, last)]
    return held, last, swapped[0], swapped[1]


def reduce_masks(order):
    return [
        sum(((place >> (4 - k)) & 1) << bit for k, bit in enumerate(order))
        for place in range(BLOCKS)
    ]


def place_blocks(target, parts, order, block, unit, lanes):
    for part, masks in zip(parts, gather_masks(order)):
        for place, mask in enumerate(masks):
            target[aligned(block ^ mask, unit), :] = part[place, :, lanes]


def emit_blocks(source, keep, send, order, block, unit, at, lanes):
    for place, mask in enumerate(reduce_masks(order)):
        target = keep if place < BLOCKS // 2 else send
        target[place % (BLOCKS // 2), at, lanes] = source[aligned(block ^ mask, unit), :]


def roll_lanes(v, shift):
    return pltpu.roll(v, shift % LANES, 1) if shift % LANES else v


def lane_index(shape):
    return lax.broadcasted_iota(jnp.int32, shape, 1)


def normalize(hidden):
    center = hidden - jnp.mean(hidden, axis=-1, keepdims=True)
    inverse = lax.rsqrt(jnp.mean(center * center, axis=-1, keepdims=True) + 1e-05)
    return center * inverse, inverse


def norm_back(grad_normed, normed, inverse):
    mean_grad = jnp.mean(grad_normed, axis=-1, keepdims=True)
    mean_cross = jnp.mean(grad_normed * normed, axis=-1, keepdims=True)
    return inverse * (grad_normed - mean_grad - normed * mean_cross)


def half_masks():
    first = lane_index((1, LANES)) < HEAD_DIM
    return low(jnp.where(first, 1.0, 0.0)), low(jnp.where(first, 0.0, 1.0))


def both_heads(pair, scale=1.0):
    first, second = half_masks()
    return jnp.concatenate([pair * (first * scale), pair * (second * scale)], 0)


def join_heads(pair):
    half = pair.shape[0] // 2
    return jnp.where(lane_index((half, LANES)) < HEAD_DIM, pair[:half], pair[half:])


def head_column(columns, pair):
    lanes = lane_index(columns.shape)
    picked = [
        jnp.sum(jnp.where(lanes == 2 * pair + k, columns, 0.0), axis=1, keepdims=True)
        for k in range(2)
    ]
    return jnp.concatenate(picked, 0)


def key_valid(shape, axis, slot, group, length, slot_len, mem_rows):
    place = lax.broadcasted_iota(jnp.int32, shape, axis)
    half = (place >> 6) & 1
    position = ((half ^ slot) * group + (place >> 7)) * HEAD_DIM + (place & 63)
    token = jnp.logical_and(place < slot_len, position < length)
    mem = jnp.logical_and(place >= slot_len, place < slot_len + mem_rows)
    return jnp.logical_or(token, mem)


def own_valid(shape, slot, group, rank, length, mem_rows):
    place = lax.broadcasted_iota(jnp.int32, shape, 0)
    half = (place >> 6) & 1
    position = ((half ^ slot) * group + rank) * HEAD_DIM + (place & 63)
    token = jnp.logical_and(place < ROWS, position < length)
    mem = jnp.logical_and(place >= ROWS, place < ROWS + mem_rows)
    return jnp.logical_or(token, mem)


def forward_kernel(layout, mem_rows, slot_len, *refs):
    lengths, near, far, memory, w0, w1, w2, w3 = refs[:8]
    qkv, attn, lse_col, vectors, up_bias = refs[8:13]
    rows, weight, extra = refs[13:]
    group = layout.group
    place = lax.axis_index("seq")
    slot, rank = place // group, place % group
    block = layout.block()
    length = lengths[slot]
    parts = (w0, w1, w2, w3)
    place_blocks(weight, parts, GATHER_QKV, block, 16, slice(0, 3 * WIDTH))
    place_blocks(extra, parts, GATHER_QKV, block, 16, slice(4 * WIDTH, 4 * WIDTH + LANES))
    for part, masks in zip((near, far), layout.group_masks()):
        for k, mask in enumerate(masks):
            rows[aligned(rank ^ mask, ROWS), :] = part[k]
    rows[slot_len : slot_len + MEM_PAD, :] = memory[slot]

    pieces, ups = [], []
    for g in range(4):
        total = jnp.zeros((8, LANES), F32)
        for p in range(8):
            total += roll_lanes(high(extra[(8 * g + p) * 16 : (8 * g + p + 1) * 16, :])[:8], 16 * p)
        pieces.append(total)
    for g in range(16):
        total = jnp.zeros((8, LANES), F32)
        for p in range(2):
            at = (2 * g + p) * 16
            total += roll_lanes(high(extra[at : at + 16, :])[8:], 64 * p)
        ups.append(total)
    vector_rows = jnp.concatenate(pieces, 1)
    vectors[...] = vector_rows
    up_bias[...] = jnp.concatenate(ups, 1)

    key_rows = slot_len + MEM_KEYS
    filled = slot_len + MEM_PAD
    qkv[filled:key_rows, :] = jnp.zeros((key_rows - filled, 3 * WIDTH), BF)
    shifts = (vector_rows[0:1], None, vector_rows[1:2])
    step = 544 if filled == 544 else 512
    for start in range(0, filled, step):
        size = min(step, filled - start)
        for part, shift in enumerate(shifts):
            lanes = slice(part * WIDTH, (part + 1) * WIDTH)
            value = dot(rows[start : start + size, :], weight[:, lanes])
            qkv[start : start + size, lanes] = low(value if shift is None else value + shift)

    keep = key_valid((1, key_rows), 1, slot, group, length, slot_len, mem_rows)
    bias = jnp.where(keep, 0.0, -1e30)
    log_columns = jnp.zeros((OWN, LANES), F32)
    for pair in range(HEADS // 2):
        at = pair * LANES
        own = jnp.concatenate(
            [qkv[aligned(rank, ROWS), at : at + LANES], qkv[slot_len:filled, at : at + LANES]], 0
        )
        keys = qkv[:, WIDTH + at : WIDTH + at + LANES]
        values = qkv[:, 2 * WIDTH + at : 2 * WIDTH + at + LANES]
        scores = dot(both_heads(own, 0.125), keys, NT) + bias
        highest = jnp.max(scores, axis=1, keepdims=True)
        expos = jnp.exp(scores - highest)
        total = jnp.sum(expos, axis=1, keepdims=True)
        attn[:, at : at + LANES] = join_heads(dot(low(expos), values) / total)
        log_total = highest + jnp.log(total)
        lanes = lane_index((OWN, LANES))
        log_columns = jnp.where(lanes == 2 * pair, log_total[:OWN], log_columns)
        log_columns = jnp.where(lanes == 2 * pair + 1, log_total[OWN:], log_columns)
    lse_col[...] = log_columns


def feed_kernel(layout, mem_rows, *refs):
    lengths, tokens, arrived, memory, cots, cot_arrived, cot_memory = refs[:7]
    attn, lse_col, vectors, up_bias = refs[7:11]
    outs, ups, downs = refs[11:15], refs[15:19], refs[19:23]
    pack, grad_mem, lse_mem, delta_mem, delta_col, first_grad, out_own, out_send = refs[23:31]
    attn_low, branch_low, hidden_low, grad_linear, active, feed_low, vector_grads, up_grads = refs[
        31:39
    ]
    w_out, w_up, w_down, slope = refs[39:]
    group = layout.group
    place = lax.axis_index("seq")
    slot, rank = place // group, place % group
    block = layout.block()
    length = lengths[slot]
    place_blocks(w_out, outs, GATHER_QKV, block, 16, slice(3 * WIDTH, 4 * WIDTH))
    place_blocks(w_up, ups, GATHER_UP, block, 16, slice(0, FF))
    place_blocks(w_down, downs, GATHER_DOWN, block, 64, slice(0, WIDTH))

    vec = vectors[...]
    out_bias, gain_one, shift_one, down_bias, gain_two, shift_two = [
        vec[k : k + 1] for k in range(2, 8)
    ]
    rows = jnp.concatenate([high(tokens[slot]), high(arrived[...]), high(memory[slot])], 0)
    cot = jnp.concatenate([high(cots[slot]), high(cot_arrived[...]), high(cot_memory[slot])], 0)
    valid = jnp.where(own_valid((OWN, 1), slot, group, rank, length, mem_rows), 1.0, 0.0)
    share = 1.0 / group
    row = lax.broadcasted_iota(jnp.int32, (OWN, 1), 0)
    weight = jnp.where(row < ROWS, 1.0, share)
    weight_low = low(weight)

    def total(v):
        return jnp.sum(v * weight, axis=0, keepdims=True)

    heads_out = attn[...]
    attn_low[...] = low(heads_out)
    branch = dot(attn_low[...], w_out[...]) + out_bias
    normed_one, inverse_one = normalize(rows + branch)
    hidden_one = normed_one * gain_one + shift_one
    hidden_low[...] = low(hidden_one)
    feed = jnp.zeros((OWN, WIDTH), F32) + down_bias
    for at in range(0, FF, WIDTH):
        cols = slice(at, at + WIDTH)
        t = dot(hidden_low[...], w_up[:, cols]) + up_bias[0:1, cols]
        square = t * t
        bent = jnp.tanh(0.7978845608 * (t + 0.044715 * (square * t)))
        half = 0.5 * (1.0 + bent)
        slope[:, cols] = half + (0.5 * 0.7978845608) * t * (1.0 - bent * bent) * (
            1.0 + (3 * 0.044715) * square
        )
        act = low(t * half)
        active[:, cols] = act
        feed += dot(act, w_down[cols, :])
    normed_two, inverse_two = normalize(hidden_one + feed)
    output = (normed_two * gain_two + shift_two) * valid
    out_own[:HEAD_DIM, :] = low(output[:HEAD_DIM])
    out_own[HEAD_DIM:, :] = low(output[ROWS:])
    out_send[...] = low(output[HEAD_DIM:])
    token_valid = jnp.where(row < ROWS, valid, 0.0)
    squares = jnp.sum(feed * feed * token_valid, axis=0, keepdims=True)

    g = cot * valid
    grads = [None] * 8
    grads[6] = total(g * normed_two)
    grads[7] = total(g)
    second = norm_back(g * gain_two, normed_two, inverse_two)
    grad_feed = low(second)
    feed_low[...] = grad_feed * weight_low
    grads[5] = total(high(grad_feed))
    grad_hidden = second
    for at in range(0, FF, WIDTH):
        cols = slice(at, at + WIDTH)
        linear = low(dot(grad_feed, w_down[cols, :], NT) * slope[:, cols])
        grad_linear[:, cols] = linear * weight_low
        up_grads[:, cols] = jnp.broadcast_to(total(high(linear)), (8, WIDTH))
        grad_hidden += dot(linear, w_up[:, cols], NT)
    grads[3] = total(grad_hidden * normed_one)
    grads[4] = total(grad_hidden)
    first = norm_back(grad_hidden * gain_one, normed_one, inverse_one)
    first_grad[...] = first
    grad_branch = low(first)
    branch_low[...] = grad_branch * weight_low
    grads[2] = total(high(grad_branch))
    grads[0] = grads[1] = jnp.zeros((1, WIDTH), F32)
    vector_grads[...] = jnp.concatenate(grads, 0)

    grad_attn = low(dot(grad_branch, w_out[...], NT))
    product = high(grad_attn) * heads_out
    chosen = lax.broadcasted_iota(jnp.int32, (16, WIDTH), 0)
    head = lax.broadcasted_iota(jnp.int32, (16, WIDTH), 1) // HEAD_DIM
    pick = low(jnp.where(chosen == head, 1.0, 0.0))
    down = lax.broadcasted_iota(jnp.int32, (WIDTH, LANES), 0) // HEAD_DIM
    pick_col = low(jnp.where(down == lane_index((WIDTH, LANES)), 1.0, 0.0))
    identity = low(
        jnp.where(
            lax.broadcasted_iota(jnp.int32, (16, LANES), 0) == lane_index((16, LANES)), 1.0, 0.0
        )
    )
    terms = [low(v) for v in split_three(product)]
    delta_col[...] = sum(dot(v, pick_col) for v in terms)
    delta_row = sum(dot(pick, v, NT) for v in terms)[:8]
    log_row = sum(dot(identity, low(v), NT) for v in split_three(lse_col[...]))[:8]
    log_terms = split_three(log_row[:, :ROWS])
    delta_terms = split_three(delta_row[:, :ROWS])
    square_terms = split_three(squares)
    square_rows = jnp.concatenate(
        [v[:, k * LANES : (k + 1) * LANES] for v in square_terms[:2] for k in range(4)], 0
    )
    pack[0, :ROWS, :] = grad_attn[:ROWS]
    pack[0, ROWS:, :] = low(
        jnp.concatenate(
            [
                jnp.concatenate([*log_terms, delta_terms[0]], 1),
                jnp.concatenate(
                    [delta_terms[1], delta_terms[2], square_rows, jnp.zeros((8, LANES), F32)], 1
                ),
            ],
            0,
        )
    )
    grad_mem[...] = grad_attn[ROWS:]
    blank = jnp.zeros((8, LANES - MEM_PAD), F32)
    lse_mem[...] = jnp.concatenate([log_row[:, ROWS:], blank], 1)
    delta_mem[...] = jnp.concatenate([delta_row[:, ROWS:], blank], 1)


def weight_kernel(layout, *refs):
    attn_low, branch_low, hidden_low, grad_linear, active, feed_low = refs[:6]
    up_keep, up_send, down_keep, down_send = refs[6:10]
    up, down, out = refs[10:]
    block = layout.block()
    for at in range(0, FF, WIDTH):
        cols = slice(at, at + WIDTH)
        down[cols, :] = low(dot(active[:, cols], feed_low[...], TN))
    out[...] = low(dot(attn_low[...], branch_low[...], TN))
    every = slice(0, WIDTH)
    emit_blocks(down, down_keep, down_send, REDUCE_DOWN, block, 64, slice(0, 64), every)
    emit_blocks(out, down_keep, down_send, REDUCE_DOWN, block, 16, slice(64, 80), every)
    for at in range(0, FF, WIDTH):
        cols = slice(at, at + WIDTH)
        up[:, cols] = low(dot(hidden_low[...], grad_linear[:, cols], TN))
    emit_blocks(up, up_keep, up_send, REDUCE_UP, block, 16, slice(0, 16), slice(0, FF))


def backward_kernel(layout, mem_rows, slot_len, *refs):
    lengths, tokens, arrived, memory, qkv, near, far, grad_mem, lse_mem, delta_mem = refs[:10]
    lse_col, delta_col, first_grad, vector_grads, up_grads = refs[10:15]
    parts = refs[15:19]
    keep_out, send_out, own_out, give_out = refs[19:23]
    weight, grad_rows, log_row, delta_row, squares, packed, grad_weight, extra = refs[23:]
    group = layout.group
    place = lax.axis_index("seq")
    slot, rank = place // group, place % group
    block = layout.block()
    length = lengths[slot]
    filled = slot_len + MEM_PAD
    key_rows = slot_len + MEM_KEYS
    place_blocks(weight, parts, GATHER_QKV, block, 16, slice(0, 3 * WIDTH))
    for part, masks in zip((near, far), layout.group_masks()):
        for k, mask in enumerate(masks):
            at = rank ^ mask
            grad_rows[aligned(at, ROWS), :] = part[k, :ROWS, :]
            more = high(part[k, ROWS:, :])
            cell = [[more[8 * a : 8 * a + 8, LANES * b : LANES * (b + 1)] for b in range(4)] for a in range(2)]
            log_row[:, aligned(at, LANES)] = cell[0][0] + cell[0][1] + cell[0][2]
            delta_row[:, aligned(at, LANES)] = cell[0][3] + cell[1][0] + cell[1][1]
            squares[at] = cell[1][2]
    grad_rows[slot_len:filled, :] = grad_mem[...]
    grad_rows[filled:, :] = jnp.zeros((key_rows - filled, WIDTH), BF)
    log_row[:, slot_len:] = lse_mem[...]
    delta_row[:, slot_len:] = delta_mem[...]

    own_keep = jnp.where(own_valid((OWN, 1), slot, group, rank, length, mem_rows), 0.0, -1e30)
    own_bias = jnp.concatenate([own_keep, own_keep], 0)
    chunk = min(slot_len, 512)
    spans = [(s, chunk) for s in range(0, slot_len, chunk)]
    spans[-1] = (spans[-1][0], chunk + MEM_KEYS)

    def own_rows(ref, lanes):
        return jnp.concatenate([ref[aligned(rank, ROWS), lanes], ref[slot_len:filled, lanes]], 0)

    for pair in range(HEADS // 2):
        at = pair * LANES
        q_lanes = slice(at, at + LANES)
        k_lanes = slice(WIDTH + at, WIDTH + at + LANES)
        v_lanes = slice(2 * WIDTH + at, 2 * WIDTH + at + LANES)
        own_q = both_heads(own_rows(qkv, q_lanes), 0.125)
        own_k = both_heads(own_rows(qkv, k_lanes), 0.125)
        own_v = both_heads(own_rows(qkv, v_lanes))
        own_g = both_heads(own_rows(grad_rows, q_lanes))
        log_column = head_column(lse_col[...], pair)
        delta_column = head_column(delta_col[...], pair)
        d_query = jnp.zeros((2 * OWN, LANES), F32)
        d_key = jnp.zeros((2 * OWN, LANES), F32)
        d_value = jnp.zeros((2 * OWN, LANES), F32)
        for start, size in spans:
            span = slice(start, start + size)
            keep = (
                lax.broadcasted_iota(jnp.int32, (1, size), 1) + start
            )
            half = (keep >> 6) & 1
            position = ((half ^ slot) * group + (keep >> 7)) * HEAD_DIM + (keep & 63)
            good = jnp.logical_or(
                jnp.logical_and(keep < slot_len, position < length),
                jnp.logical_and(keep >= slot_len, keep < slot_len + mem_rows),
            )
            bias = jnp.where(good, 0.0, -1e30)
            keys, values = qkv[span, k_lanes], qkv[span, v_lanes]
            weights = jnp.exp(dot(own_q, keys, NT) + bias - log_column)
            slopes = dot(own_g, values, NT)
            scores = low(weights * (slopes - delta_column))
            d_query += dot(scores, keys)

            queries, grads = qkv[span, q_lanes], grad_rows[span, q_lanes]

            def row_pair(ref):
                return jnp.concatenate(
                    [
                        jnp.broadcast_to(ref[2 * pair + k : 2 * pair + k + 1, span], (OWN, size))
                        for k in range(2)
                    ],
                    0,
                )

            weights = jnp.exp(dot(own_k, queries, NT) + own_bias - row_pair(log_row))
            slopes = dot(own_v, grads, NT)
            scores = low(weights * (slopes - row_pair(delta_row)))
            d_value += dot(low(weights), grads)
            d_key += dot(scores, queries)
        packed[:, q_lanes] = low(join_heads(d_query) * 0.125)
        packed[:, k_lanes] = low(join_heads(d_key) * 0.125)
        packed[:, v_lanes] = low(join_heads(d_value))

    share = 1.0 / group
    row = lax.broadcasted_iota(jnp.int32, (OWN, 1), 0)
    row_weight = low(jnp.where(row < ROWS, 1.0, share))
    rows = jnp.concatenate([tokens[slot], arrived[...], memory[slot]], 0)
    scaled = packed[...] * row_weight
    for at in range(0, 3 * WIDTH, WIDTH):
        cols = slice(at, at + WIDTH)
        grad_weight[:, cols] = low(dot(rows, scaled[:, cols], TN))
    emit_blocks(
        grad_weight, keep_out, send_out, REDUCE_QKV, block, 16, slice(0, 16), slice(0, 3 * WIDTH)
    )
    query_bias = jnp.sum(high(scaled[:, :WIDTH]), axis=0, keepdims=True)
    value_bias = jnp.sum(high(scaled[:, 2 * WIDTH :]), axis=0, keepdims=True)
    vec = jnp.concatenate([query_bias, value_bias, vector_grads[2:8, :]], 0)
    ups = up_grads[...]
    lane8 = lane_index((8, LANES))
    for p in range(BLOCKS):
        g = p // 8
        top = roll_lanes(vec[:, g * LANES : (g + 1) * LANES], -16 * (p % 8))
        top = jnp.where(lane8 < 16, top, 0.0)
        g = p // 2
        bottom = roll_lanes(ups[:, g * LANES : (g + 1) * LANES], -64 * (p % 2))
        both = jnp.concatenate([top, bottom], 0)
        extra[p * 16 : (p + 1) * 16, :] = split_lanes(both)
    emit_blocks(
        extra,
        keep_out,
        send_out,
        REDUCE_QKV,
        block,
        16,
        slice(0, 16),
        slice(3 * WIDTH, 3 * WIDTH + LANES),
    )

    grad_in = first_grad[...] + dot(packed[...], weight[...], NT)
    square = squares[0]
    for k in range(1, group):
        square += squares[k]
    square = square[:4] + square[4:]
    square = jnp.concatenate([square[k : k + 1] for k in range(4)], 1)
    first, second, _ = split_three(square)
    tail = low(jnp.concatenate([first, second, jnp.zeros((14, WIDTH), F32)], 0))
    own_out[:64, :] = low(grad_in[:64])
    own_out[64:96, :] = low(grad_in[ROWS:])
    own_out[96:, :] = tail
    give_out[:96, :] = low(grad_in[64:])
    give_out[96:, :] = tail


def split_lanes(v):
    first = high(low(v))
    second = pltpu.roll(v - first, 64, v.ndim - 1)
    lanes = lax.broadcasted_iota(jnp.int32, v.shape, v.ndim - 1)
    return low(jnp.where(lanes < 64, first, second))


def fold_kernel(width, keep, other, keep_out, send_out):
    half = keep.shape[0] // 2
    for start, out in ((0, keep_out), (half, send_out)):
        span = slice(start, start + half)
        total = high(keep[span, :, :width]) + high(other[span, :, :width])
        out[:, :, :width] = low(total)
        for k in range(half):
            extra = high(keep[start + k, :, width:]) + high(other[start + k, :, width:])
            out[k, :, width:] = split_lanes(extra + pltpu.roll(extra, 64, 1))


def fold_with_extra(keep, other):
    shape = (keep.shape[0] // 2,) + keep.shape[1:]
    return pl.pallas_call(
        functools.partial(fold_kernel, 3 * WIDTH),
        out_shape=[jax.ShapeDtypeStruct(shape, BF)] * 2,
        name="fold",
    )(keep, other)


def fold_plain(keep, other):
    half = keep.shape[0] // 2
    return tuple(
        low(high(keep[part]) + high(other[part])) for part in (slice(0, half), slice(half, None))
    )


def emit_kernel(layout, mem_rows, *refs):
    lengths, out_own, out_got, grad_own, grad_got = refs[:5]
    out_tokens, out_memory, grad_tokens, grad_memory, rms = refs[5:]
    slot = lax.axis_index("seq") // layout.group
    for own, got, tokens, memory in (
        (out_own, out_got, out_tokens, out_memory),
        (grad_own, grad_got, grad_tokens, grad_memory),
    ):
        for source, at in ((own, slot), (got, 1 - slot)):
            tokens[at] = source[:64, :]
            memory[at] = low(high(source[64:96, :])[:mem_rows])
    result = []
    for source, at in ((grad_own, slot), (grad_got, 1 - slot)):
        tail = high(source[96:112, :])
        square = tail[0:1] + tail[1:2]
        result.append(jnp.sqrt(square / lengths[at].astype(F32)))
    row = lax.broadcasted_iota(jnp.int32, (2, WIDTH), 0)
    rms[...] = jnp.where(row == slot, result[0], result[1])


def call(kernel, name, outs, scratch, args, smem=1, limit=48, flops=0):
    vmem = pl.BlockSpec(memory_space=pltpu.VMEM)
    in_specs = [pl.BlockSpec(memory_space=pltpu.SMEM)] * smem + [vmem] * (len(args) - smem)
    size = sum(a.size * a.dtype.itemsize for a in args)
    return pl.pallas_call(
        kernel,
        out_shape=[jax.ShapeDtypeStruct(shape, kind) for shape, kind in outs],
        in_specs=in_specs,
        out_specs=[vmem] * len(outs),
        scratch_shapes=[pltpu.VMEM(shape, kind) for shape, kind in scratch],
        compiler_params=pltpu.CompilerParams(vmem_limit_bytes=limit * MIB),
        cost_estimate=pl.CostEstimate(flops=flops, bytes_accessed=size, transcendentals=0),
        name=name,
    )(*args)


def local(
    layout,
    tokens,
    memory,
    lengths,
    w_qkv,
    b_query,
    b_value,
    w_out,
    b_out,
    gain_one,
    shift_one,
    w_up,
    b_up,
    w_down,
    b_down,
    gain_two,
    shift_two,
    cot_tokens,
    cot_memory,
):
    mem_rows = memory.shape[1]
    tok_rows = tokens.shape[1]
    slot_len = tok_rows * layout.seq
    key_rows = slot_len + MEM_KEYS
    partner = layout.seq_bits - 1
    slot = lax.axis_index("seq") // layout.group

    def pick(x, at):
        return lax.dynamic_index_in_dim(x, at, 0, False)

    arrived = layout.swap(pick(tokens, 1 - slot), partner)
    near, far = layout.gather_group(jnp.concatenate([pick(tokens, slot), arrived], 0)[None])

    vectors = jnp.stack(
        [b_query, b_value, b_out, gain_one, shift_one, b_down, gain_two, shift_two]
    )
    vectors = layout.join_low(vectors, 1)
    extra = jnp.concatenate(
        [
            jnp.pad(vectors, ((0, 0), (0, LANES - 16))),
            jnp.pad(layout.join_low(b_up, 0)[None], ((0, 7), (0, LANES - 64))),
        ],
        0,
    )
    first = jnp.concatenate([layout.join_low(w_qkv, 0), layout.join_low(w_out, 0), extra], 1)
    qkv_parts = layout.gather(first[None], GATHER_QKV)
    up_parts = layout.gather(layout.join_low(w_up, 0)[None], GATHER_UP)
    down_parts = layout.gather(layout.join_low(w_down, 0)[None], GATHER_DOWN)
    cot_arrived = layout.swap(pick(cot_tokens, 1 - slot), partner)
    pad_rows = ((0, 0), (0, MEM_PAD - mem_rows), (0, 0))
    memory_full = jnp.pad(memory, pad_rows)
    cot_memory_full = jnp.pad(cot_memory, pad_rows)

    qkv, attn, lse_col, vector_rows, up_bias = call(
        functools.partial(forward_kernel, layout, mem_rows, slot_len),
        "attention_forward",
        [
            ((key_rows, 3 * WIDTH), BF),
            ((OWN, WIDTH), F32),
            ((OWN, LANES), F32),
            ((8, WIDTH), F32),
            ((8, FF), F32),
        ],
        [((slot_len + MEM_PAD, WIDTH), BF), ((WIDTH, 3 * WIDTH), BF), ((WIDTH, LANES), BF)],
        (lengths, near, far, memory_full, *qkv_parts),
    )
    (
        pack,
        grad_mem,
        lse_mem,
        delta_mem,
        delta_col,
        first_grad,
        out_own,
        out_send,
        attn_low,
        branch_low,
        hidden_low,
        grad_linear,
        active,
        feed_low,
        vector_grads,
        up_grads,
    ) = call(
        functools.partial(feed_kernel, layout, mem_rows),
        "feed_forward",
        [
            ((1, ROWS + 16, WIDTH), BF),
            ((MEM_PAD, WIDTH), BF),
            ((8, LANES), F32),
            ((8, LANES), F32),
            ((OWN, LANES), F32),
            ((OWN, WIDTH), F32),
            ((64 + MEM_PAD, WIDTH), BF),
            ((64 + MEM_PAD, WIDTH), BF),
            ((OWN, WIDTH), BF),
            ((OWN, WIDTH), BF),
            ((OWN, WIDTH), BF),
            ((OWN, FF), BF),
            ((OWN, FF), BF),
            ((OWN, WIDTH), BF),
            ((8, WIDTH), F32),
            ((8, FF), F32),
        ],
        [((WIDTH, WIDTH), BF), ((WIDTH, FF), BF), ((FF, WIDTH), BF), ((OWN, FF), F32)],
        (
            lengths,
            tokens,
            arrived,
            memory_full,
            cot_tokens,
            cot_arrived,
            cot_memory_full,
            attn,
            lse_col,
            vector_rows,
            up_bias,
            *qkv_parts,
            *up_parts,
            *down_parts,
        ),
    )
    grads_near, grads_far = layout.gather_group(pack)
    out_got = layout.swap(out_send, partner)
    half = BLOCKS // 2
    up_keep, up_send, down_keep, down_send = call(
        functools.partial(weight_kernel, layout),
        "weight_gradients",
        [
            ((half, 16, FF), BF),
            ((half, 16, FF), BF),
            ((half, 80, WIDTH), BF),
            ((half, 80, WIDTH), BF),
        ],
        [((WIDTH, FF), BF), ((FF, WIDTH), BF), ((WIDTH, WIDTH), BF)],
        (attn_low, branch_low, hidden_low, grad_linear, active, feed_low),
        smem=0,
    )
    up_total = layout.reduce(up_keep, up_send, REDUCE_UP, fold_plain)
    down_total = layout.reduce(down_keep, down_send, REDUCE_DOWN, fold_plain)
    qkv_keep, qkv_send, grad_own, grad_send = call(
        functools.partial(backward_kernel, layout, mem_rows, slot_len),
        "attention_backward",
        [
            ((half, 16, 3 * WIDTH + LANES), BF),
            ((half, 16, 3 * WIDTH + LANES), BF),
            ((112, WIDTH), BF),
            ((112, WIDTH), BF),
        ],
        [
            ((WIDTH, 3 * WIDTH), BF),
            ((key_rows, WIDTH), BF),
            ((8, key_rows), F32),
            ((8, key_rows), F32),
            ((layout.group, 8, LANES), F32),
            ((OWN, 3 * WIDTH), BF),
            ((WIDTH, 3 * WIDTH), BF),
            ((WIDTH, LANES), BF),
        ],
        (
            lengths,
            tokens,
            arrived,
            memory_full,
            qkv,
            grads_near,
            grads_far,
            grad_mem,
            lse_mem,
            delta_mem,
            lse_col,
            delta_col,
            first_grad,
            vector_grads,
            up_grads,
            *qkv_parts,
        ),
    )
    qkv_total = layout.reduce(qkv_keep, qkv_send, REDUCE_QKV, fold_with_extra)
    grad_got = layout.swap(grad_send, partner)

    def add(pair):
        return high(pair[0][0]) + high(pair[1][0])

    up_sum = layout.reduce_low(add(up_total), 0)
    down_sum = add(down_total)
    out_sum = layout.reduce_low(down_sum[64:], 0)
    down_sum = layout.reduce_low(down_sum[:64], 0)
    qkv_sum = add(qkv_total)
    extra_sum = qkv_sum[:, 3 * WIDTH :]
    qkv_sum = layout.reduce_low(qkv_sum[:, : 3 * WIDTH], 0)
    vec = layout.reduce_low(extra_sum[:8, :16] + extra_sum[:8, 64:80], 1)
    up_vec = layout.reduce_low(extra_sum[8, :64] + extra_sum[8, 64:], 0)

    out_tokens, out_memory, grad_tokens, grad_memory, rms = call(
        functools.partial(emit_kernel, layout, mem_rows),
        "emit",
        [
            (tokens.shape, BF),
            (memory.shape, BF),
            (tokens.shape, BF),
            (memory.shape, BF),
            ((2, WIDTH), F32),
        ],
        [],
        (lengths, out_own, out_got, grad_own, grad_got),
    )
    return (
        out_tokens,
        out_memory,
        grad_tokens,
        grad_memory,
        qkv_sum,
        vec[0],
        vec[1],
        out_sum,
        vec[2],
        vec[3],
        vec[4],
        up_sum,
        up_vec,
        down_sum,
        vec[5],
        vec[6],
        vec[7],
        rms,
    )


def solution(mesh):
    rows = P("dp", "seq", None)
    slots = P("dp", None, None)
    matrix = P(("dp", "seq"), None)
    vector = P(("dp", "seq"))
    weights = (
        matrix,
        vector,
        vector,
        matrix,
        vector,
        vector,
        vector,
        matrix,
        vector,
        matrix,
        vector,
        vector,
        vector,
    )
    return jax.shard_map(
        functools.partial(local, Layout(mesh)),
        mesh=mesh,
        in_specs=(rows, slots, P("dp"), *weights, rows, slots),
        out_specs=(rows, slots, rows, slots, *weights, P("dp", None)),
        check_vma=False,
    )
```

```python
import functools

import jax
import jax.numpy as jnp
from jax import lax
from jax.experimental import pallas as pl
from jax.experimental.pallas import tpu as pltpu
from jax.sharding import PartitionSpec as P

HEADS = 8
HEAD_DIM = 64
WIDTH = 512
FF = 2048
BLOCKS = 32
ROWS = 128
MEM_PAD = 32
OWN = ROWS + MEM_PAD
MEM_KEYS = 128
LANES = 128
MIB = 1 << 20

BF = jnp.bfloat16
F32 = jnp.float32
NN = (((1,), (0,)), ((), ()))
NT = (((1,), (1,)), ((), ()))
TN = (((0,), (0,)), ((), ()))

GATHER_QKV = (2, 1, 3, 4, 0)
GATHER_UP = (2, 3, 4, 1, 0)
GATHER_DOWN = (2, 4, 1, 3, 0)
REDUCE_UP = (0, 1, 4, 3, 2)
REDUCE_DOWN = (0, 3, 1, 4, 2)
REDUCE_QKV = (0, 4, 3, 1, 2)
PAIRS = BLOCKS // 2
PAIR_UP = (2, 3, 0, 1)
PAIR_DOWN = (3, 2, 0, 1)
PAIR_QKV = (2, 3, 1, 0)
GIVEN = FF + 2 * WIDTH + WIDTH // 2 + FF // 2 + WIDTH // 2


def dot(a, b, dims=NN):
    return lax.dot_general(a, b, dims, preferred_element_type=F32)


def low(v):
    return v.astype(BF)


def high(v):
    return v.astype(F32)


def split_three(v):
    first = high(low(v))
    second = high(low(v - first))
    return first, second, high(low(v - first - second))


def aligned(index, size):
    return pl.ds(pl.multiple_of(index * size, size), size)


class Layout:
    def __init__(self, mesh):
        self.dp = mesh.shape["dp"]
        self.seq = mesh.shape["seq"]
        self.devices = self.dp * self.seq
        self.low_bits = (self.devices // BLOCKS).bit_length() - 1
        self.group = self.seq // 2
        self.seq_bits = self.seq.bit_length() - 1

    def dim(self, bit):
        if bit < self.seq_bits:
            return "seq", 1 << bit
        return "dp", 1 << (bit - self.seq_bits)

    def swap(self, x, bit):
        axis, mask = self.dim(bit)
        size = self.seq if axis == "seq" else self.dp
        return lax.ppermute(x, axis, [(i, i ^ mask) for i in range(size)])

    def block_swap(self, x, bit):
        return self.swap(x, bit + self.low_bits)

    def pair_swap(self, x, bit):
        return self.swap(x, bit + 1)

    def device(self):
        return lax.axis_index("dp") * self.seq + lax.axis_index("seq")

    def block(self):
        return self.device() >> self.low_bits

    def join_low(self, x, axis):
        for bit in range(self.low_bits):
            other = self.swap(x, bit)
            first = (self.device() >> bit) % 2 == 0
            x = jnp.where(
                first, jnp.concatenate([x, other], axis), jnp.concatenate([other, x], axis)
            )
        return x

    def reduce_low(self, x, axis):
        for bit in reversed(range(self.low_bits)):
            first = (self.device() >> bit) % 2 == 0
            lower, upper = jnp.split(x, 2, axis)
            other = self.swap(jnp.where(first, upper, lower), bit)
            x = jnp.where(first, lower, upper) + other
        return x

    def gather(self, x, order):
        held = x
        for bit in order[:3]:
            held = jnp.concatenate([held, self.block_swap(held, bit)], 0)
        last = self.block_swap(held, order[3])
        return held, last, self.block_swap(held, order[4]), self.block_swap(last, order[4])

    def reduce(self, keep, send, order, fold, swap=None):
        swap = swap or self.block_swap
        other = swap(send, order[0])
        for bit in order[1:]:
            keep, send = fold(keep, other)
            other = swap(send, bit)
        return keep, other

    def gather_group(self, x):
        near = x
        mask = self.group // 2
        while mask > 1:
            near = jnp.concatenate([near, self.swap(near, mask.bit_length() - 1)], 0)
            mask //= 2
        return near, self.swap(near, 0)

    def group_masks(self):
        near = [0]
        mask = self.group // 2
        while mask > 1:
            near += [m ^ mask for m in near]
            mask //= 2
        return near, [m ^ 1 for m in near]


def gather_masks(order):
    held = [0]
    for bit in order[:3]:
        held = held + [m ^ (1 << bit) for m in held]
    last = [m ^ (1 << order[3]) for m in held]
    swapped = [[m ^ (1 << order[4]) for m in part] for part in (held, last)]
    return held, last, swapped[0], swapped[1]


def reduce_masks(order):
    bits = len(order)
    return [
        sum(((place >> (bits - 1 - k)) & 1) << bit for k, bit in enumerate(order))
        for place in range(1 << bits)
    ]


def place_blocks(target, parts, order, block, unit, lanes):
    for part, masks in zip(parts, gather_masks(order)):
        for place, mask in enumerate(masks):
            target[aligned(block ^ mask, unit), :] = part[place, :, lanes]


def emit_blocks(source, keep, send, order, block, unit, at, lanes):
    masks = reduce_masks(order)
    half = len(masks) // 2
    for place, mask in enumerate(masks):
        target = keep if place < half else send
        target[place % half, at, lanes] = source[aligned(block ^ mask, unit), :]


def roll_lanes(v, shift):
    return pltpu.roll(v, shift % LANES, 1) if shift % LANES else v


def lane_index(shape):
    return lax.broadcasted_iota(jnp.int32, shape, 1)


def normalize(hidden):
    center = hidden - jnp.mean(hidden, axis=-1, keepdims=True)
    inverse = lax.rsqrt(jnp.mean(center * center, axis=-1, keepdims=True) + 1e-05)
    return center * inverse, inverse


def norm_back(grad_normed, normed, inverse):
    mean_grad = jnp.mean(grad_normed, axis=-1, keepdims=True)
    mean_cross = jnp.mean(grad_normed * normed, axis=-1, keepdims=True)
    return inverse * (grad_normed - mean_grad - normed * mean_cross)


def half_masks():
    first = lane_index((1, LANES)) < HEAD_DIM
    return low(jnp.where(first, 1.0, 0.0)), low(jnp.where(first, 0.0, 1.0))


def both_heads(pair, scale=1.0):
    first, second = half_masks()
    return jnp.concatenate([pair * (first * scale), pair * (second * scale)], 0)


def join_heads(pair):
    half = pair.shape[0] // 2
    return jnp.where(lane_index((half, LANES)) < HEAD_DIM, pair[:half], pair[half:])


def head_column(columns, pair):
    lanes = lane_index(columns.shape)
    picked = [
        jnp.sum(jnp.where(lanes == 2 * pair + k, columns, 0.0), axis=1, keepdims=True)
        for k in range(2)
    ]
    return jnp.concatenate(picked, 0)


def key_valid(shape, axis, slot, group, length, slot_len, mem_rows):
    place = lax.broadcasted_iota(jnp.int32, shape, axis)
    half = (place >> 6) & 1
    position = ((half ^ slot) * group + (place >> 7)) * HEAD_DIM + (place & 63)
    token = jnp.logical_and(place < slot_len, position < length)
    mem = jnp.logical_and(place >= slot_len, place < slot_len + mem_rows)
    return jnp.logical_or(token, mem)


def own_valid(shape, slot, group, rank, length, mem_rows):
    place = lax.broadcasted_iota(jnp.int32, shape, 0)
    half = (place >> 6) & 1
    position = ((half ^ slot) * group + rank) * HEAD_DIM + (place & 63)
    token = jnp.logical_and(place < ROWS, position < length)
    mem = jnp.logical_and(place >= ROWS, place < ROWS + mem_rows)
    return jnp.logical_or(token, mem)


def forward_kernel(layout, mem_rows, slot_len, *refs):
    lengths, near, far, memory, w0, w1, w2, w3 = refs[:8]
    qkv, attn, lse_col, vectors, up_bias = refs[8:13]
    rows, weight, extra = refs[13:]
    group = layout.group
    place = lax.axis_index("seq")
    slot, rank = place // group, place % group
    block = layout.block()
    length = lengths[slot]
    parts = (w0, w1, w2, w3)
    place_blocks(weight, parts, GATHER_QKV, block, 16, slice(0, 3 * WIDTH))
    place_blocks(extra, parts, GATHER_QKV, block, 16, slice(4 * WIDTH, 4 * WIDTH + LANES))
    for part, masks in zip((near, far), layout.group_masks()):
        for k, mask in enumerate(masks):
            rows[aligned(rank ^ mask, ROWS), :] = part[k]
    rows[slot_len : slot_len + MEM_PAD, :] = memory[slot]

    pieces, ups = [], []
    for g in range(4):
        total = jnp.zeros((8, LANES), F32)
        for p in range(8):
            total += roll_lanes(high(extra[(8 * g + p) * 16 : (8 * g + p + 1) * 16, :])[:8], 16 * p)
        pieces.append(total)
    for g in range(16):
        total = jnp.zeros((8, LANES), F32)
        for p in range(2):
            at = (2 * g + p) * 16
            total += roll_lanes(high(extra[at : at + 16, :])[8:], 64 * p)
        ups.append(total)
    vector_rows = jnp.concatenate(pieces, 1)
    vectors[...] = vector_rows
    up_bias[...] = jnp.concatenate(ups, 1)

    key_rows = slot_len + MEM_KEYS
    filled = slot_len + MEM_PAD
    qkv[filled:key_rows, :] = jnp.zeros((key_rows - filled, 3 * WIDTH), BF)
    shifts = (vector_rows[0:1], None, vector_rows[1:2])
    step = 544 if filled == 544 else 512
    for start in range(0, filled, step):
        size = min(step, filled - start)
        for part, shift in enumerate(shifts):
            lanes = slice(part * WIDTH, (part + 1) * WIDTH)
            value = dot(rows[start : start + size, :], weight[:, lanes])
            qkv[start : start + size, lanes] = low(value if shift is None else value + shift)

    keep = key_valid((1, key_rows), 1, slot, group, length, slot_len, mem_rows)
    bias = jnp.where(keep, 0.0, -1e30)
    log_columns = jnp.zeros((OWN, LANES), F32)
    for pair in range(HEADS // 2):
        at = pair * LANES
        own = jnp.concatenate(
            [qkv[aligned(rank, ROWS), at : at + LANES], qkv[slot_len:filled, at : at + LANES]], 0
        )
        keys = qkv[:, WIDTH + at : WIDTH + at + LANES]
        values = qkv[:, 2 * WIDTH + at : 2 * WIDTH + at + LANES]
        scores = dot(both_heads(own, 0.125), keys, NT) + bias
        highest = jnp.max(scores, axis=1, keepdims=True)
        expos = jnp.exp(scores - highest)
        total = jnp.sum(expos, axis=1, keepdims=True)
        attn[:, at : at + LANES] = join_heads(dot(low(expos), values) / total)
        log_total = highest + jnp.log(total)
        lanes = lane_index((OWN, LANES))
        log_columns = jnp.where(lanes == 2 * pair, log_total[:OWN], log_columns)
        log_columns = jnp.where(lanes == 2 * pair + 1, log_total[OWN:], log_columns)
    lse_col[...] = log_columns


def feed_kernel(layout, mem_rows, *refs):
    lengths, tokens, arrived, memory, cots, cot_arrived, cot_memory = refs[:7]
    attn, lse_col, vectors, up_bias = refs[7:11]
    outs, ups, downs = refs[11:15], refs[15:19], refs[19:23]
    pack, grad_mem, lse_mem, delta_mem, delta_col, first_grad, out_own, out_send = refs[23:31]
    attn_low, branch_low, hidden_low, grad_linear, active, feed_low, vector_grads, up_grads = refs[
        31:39
    ]
    w_out, w_up, w_down, slope = refs[39:]
    group = layout.group
    place = lax.axis_index("seq")
    slot, rank = place // group, place % group
    block = layout.block()
    length = lengths[slot]
    place_blocks(w_out, outs, GATHER_QKV, block, 16, slice(3 * WIDTH, 4 * WIDTH))
    place_blocks(w_up, ups, GATHER_UP, block, 16, slice(0, FF))
    place_blocks(w_down, downs, GATHER_DOWN, block, 64, slice(0, WIDTH))

    vec = vectors[...]
    out_bias, gain_one, shift_one, down_bias, gain_two, shift_two = [
        vec[k : k + 1] for k in range(2, 8)
    ]
    rows = jnp.concatenate([high(tokens[slot]), high(arrived[...]), high(memory[slot])], 0)
    cot = jnp.concatenate([high(cots[slot]), high(cot_arrived[...]), high(cot_memory[slot])], 0)
    valid = jnp.where(own_valid((OWN, 1), slot, group, rank, length, mem_rows), 1.0, 0.0)
    share = 1.0 / group
    row = lax.broadcasted_iota(jnp.int32, (OWN, 1), 0)
    weight = jnp.where(row < ROWS, 1.0, share)
    weight_low = low(weight)

    def total(v):
        return jnp.sum(v * weight, axis=0, keepdims=True)

    heads_out = attn[...]
    attn_low[...] = low(heads_out)
    branch = dot(attn_low[...], w_out[...]) + out_bias
    normed_one, inverse_one = normalize(rows + branch)
    hidden_one = normed_one * gain_one + shift_one
    hidden_low[...] = low(hidden_one)
    feed = jnp.zeros((OWN, WIDTH), F32) + down_bias
    for at in range(0, FF, WIDTH):
        cols = slice(at, at + WIDTH)
        t = dot(hidden_low[...], w_up[:, cols]) + up_bias[0:1, cols]
        square = t * t
        bent = jnp.tanh(0.7978845608 * (t + 0.044715 * (square * t)))
        half = 0.5 * (1.0 + bent)
        slope[:, cols] = half + (0.5 * 0.7978845608) * t * (1.0 - bent * bent) * (
            1.0 + (3 * 0.044715) * square
        )
        act = low(t * half)
        active[:, cols] = act
        feed += dot(act, w_down[cols, :])
    normed_two, inverse_two = normalize(hidden_one + feed)
    output = (normed_two * gain_two + shift_two) * valid
    out_own[:HEAD_DIM, :] = low(output[:HEAD_DIM])
    out_own[HEAD_DIM:, :] = low(output[ROWS:])
    out_send[...] = low(output[HEAD_DIM:])
    token_valid = jnp.where(row < ROWS, valid, 0.0)
    squares = jnp.sum(feed * feed * token_valid, axis=0, keepdims=True)

    g = cot * valid
    grads = [None] * 8
    grads[6] = total(g * normed_two)
    grads[7] = total(g)
    second = norm_back(g * gain_two, normed_two, inverse_two)
    grad_feed = low(second)
    feed_low[...] = grad_feed * weight_low
    grads[5] = total(high(grad_feed))
    grad_hidden = second
    for at in range(0, FF, WIDTH):
        cols = slice(at, at + WIDTH)
        linear = low(dot(grad_feed, w_down[cols, :], NT) * slope[:, cols])
        grad_linear[:, cols] = linear * weight_low
        up_grads[:, cols] = jnp.broadcast_to(total(high(linear)), (8, WIDTH))
        grad_hidden += dot(linear, w_up[:, cols], NT)
    grads[3] = total(grad_hidden * normed_one)
    grads[4] = total(grad_hidden)
    first = norm_back(grad_hidden * gain_one, normed_one, inverse_one)
    first_grad[...] = first
    grad_branch = low(first)
    branch_low[...] = grad_branch * weight_low
    grads[2] = total(high(grad_branch))
    grads[0] = grads[1] = jnp.zeros((1, WIDTH), F32)
    vector_grads[...] = jnp.concatenate(grads, 0)

    grad_attn = low(dot(grad_branch, w_out[...], NT))
    product = high(grad_attn) * heads_out
    chosen = lax.broadcasted_iota(jnp.int32, (16, WIDTH), 0)
    head = lax.broadcasted_iota(jnp.int32, (16, WIDTH), 1) // HEAD_DIM
    pick = low(jnp.where(chosen == head, 1.0, 0.0))
    down = lax.broadcasted_iota(jnp.int32, (WIDTH, LANES), 0) // HEAD_DIM
    pick_col = low(jnp.where(down == lane_index((WIDTH, LANES)), 1.0, 0.0))
    identity = low(
        jnp.where(
            lax.broadcasted_iota(jnp.int32, (16, LANES), 0) == lane_index((16, LANES)), 1.0, 0.0
        )
    )
    terms = [low(v) for v in split_three(product)]
    delta_col[...] = sum(dot(v, pick_col) for v in terms)
    delta_row = sum(dot(pick, v, NT) for v in terms)[:8]
    log_row = sum(dot(identity, low(v), NT) for v in split_three(lse_col[...]))[:8]
    log_terms = split_three(log_row[:, :ROWS])
    delta_terms = split_three(delta_row[:, :ROWS])
    square_terms = split_three(squares)
    square_rows = jnp.concatenate(
        [v[:, k * LANES : (k + 1) * LANES] for v in square_terms[:2] for k in range(4)], 0
    )
    pack[0, :ROWS, :] = grad_attn[:ROWS]
    pack[0, ROWS:, :] = low(
        jnp.concatenate(
            [
                jnp.concatenate([*log_terms, delta_terms[0]], 1),
                jnp.concatenate(
                    [delta_terms[1], delta_terms[2], square_rows, jnp.zeros((8, LANES), F32)], 1
                ),
            ],
            0,
        )
    )
    grad_mem[...] = grad_attn[ROWS:]
    blank = jnp.zeros((8, LANES - MEM_PAD), F32)
    lse_mem[...] = jnp.concatenate([log_row[:, ROWS:], blank], 1)
    delta_mem[...] = jnp.concatenate([delta_row[:, ROWS:], blank], 1)


def weight_kernel(layout, *refs):
    attn_low, branch_low, hidden_low, grad_linear, active, feed_low = refs[:6]
    up_keep, up_send, down_keep, down_send = refs[6:10]
    up, down, out = refs[10:]
    block = layout.block()
    for at in range(0, FF, WIDTH):
        cols = slice(at, at + WIDTH)
        down[cols, :] = low(dot(active[:, cols], feed_low[...], TN))
    out[...] = low(dot(attn_low[...], branch_low[...], TN))
    every = slice(0, WIDTH)
    emit_blocks(down, down_keep, down_send, REDUCE_DOWN, block, 64, slice(0, 64), every)
    emit_blocks(out, down_keep, down_send, REDUCE_DOWN, block, 16, slice(64, 80), every)
    for at in range(0, FF, WIDTH):
        cols = slice(at, at + WIDTH)
        up[:, cols] = low(dot(hidden_low[...], grad_linear[:, cols], TN))
    emit_blocks(up, up_keep, up_send, REDUCE_UP, block, 16, slice(0, 16), slice(0, FF))


def backward_kernel(layout, mem_rows, slot_len, *refs):
    lengths, tokens, arrived, memory, qkv, near, far, grad_mem, lse_mem, delta_mem = refs[:10]
    lse_col, delta_col, first_grad, vector_grads, up_grads = refs[10:15]
    parts = refs[15:19]
    keep_out, send_out, own_out, give_out = refs[19:23]
    weight, grad_rows, log_row, delta_row, squares, packed, grad_weight, extra = refs[23:]
    group = layout.group
    place = lax.axis_index("seq")
    slot, rank = place // group, place % group
    block = layout.block()
    length = lengths[slot]
    filled = slot_len + MEM_PAD
    key_rows = slot_len + MEM_KEYS
    place_blocks(weight, parts, GATHER_QKV, block, 16, slice(0, 3 * WIDTH))
    for part, masks in zip((near, far), layout.group_masks()):
        for k, mask in enumerate(masks):
            at = rank ^ mask
            grad_rows[aligned(at, ROWS), :] = part[k, :ROWS, :]
            more = high(part[k, ROWS:, :])
            cell = [[more[8 * a : 8 * a + 8, LANES * b : LANES * (b + 1)] for b in range(4)] for a in range(2)]
            log_row[:, aligned(at, LANES)] = cell[0][0] + cell[0][1] + cell[0][2]
            delta_row[:, aligned(at, LANES)] = cell[0][3] + cell[1][0] + cell[1][1]
            squares[at] = cell[1][2]
    grad_rows[slot_len:filled, :] = grad_mem[...]
    grad_rows[filled:, :] = jnp.zeros((key_rows - filled, WIDTH), BF)
    log_row[:, slot_len:] = lse_mem[...]
    delta_row[:, slot_len:] = delta_mem[...]

    own_keep = jnp.where(own_valid((OWN, 1), slot, group, rank, length, mem_rows), 0.0, -1e30)
    own_bias = jnp.concatenate([own_keep, own_keep], 0)
    chunk = min(slot_len, 512)
    spans = [(s, chunk) for s in range(0, slot_len, chunk)]
    spans[-1] = (spans[-1][0], chunk + MEM_KEYS)

    def own_rows(ref, lanes):
        return jnp.concatenate([ref[aligned(rank, ROWS), lanes], ref[slot_len:filled, lanes]], 0)

    for pair in range(HEADS // 2):
        at = pair * LANES
        q_lanes = slice(at, at + LANES)
        k_lanes = slice(WIDTH + at, WIDTH + at + LANES)
        v_lanes = slice(2 * WIDTH + at, 2 * WIDTH + at + LANES)
        own_q = both_heads(own_rows(qkv, q_lanes), 0.125)
        own_k = both_heads(own_rows(qkv, k_lanes), 0.125)
        own_v = both_heads(own_rows(qkv, v_lanes))
        own_g = both_heads(own_rows(grad_rows, q_lanes))
        log_column = head_column(lse_col[...], pair)
        delta_column = head_column(delta_col[...], pair)
        d_query = jnp.zeros((2 * OWN, LANES), F32)
        d_key = jnp.zeros((2 * OWN, LANES), F32)
        d_value = jnp.zeros((2 * OWN, LANES), F32)
        for start, size in spans:
            span = slice(start, start + size)
            keep = (
                lax.broadcasted_iota(jnp.int32, (1, size), 1) + start
            )
            half = (keep >> 6) & 1
            position = ((half ^ slot) * group + (keep >> 7)) * HEAD_DIM + (keep & 63)
            good = jnp.logical_or(
                jnp.logical_and(keep < slot_len, position < length),
                jnp.logical_and(keep >= slot_len, keep < slot_len + mem_rows),
            )
            bias = jnp.where(good, 0.0, -1e30)
            keys, values = qkv[span, k_lanes], qkv[span, v_lanes]
            weights = jnp.exp(dot(own_q, keys, NT) + bias - log_column)
            slopes = dot(own_g, values, NT)
            scores = low(weights * (slopes - delta_column))
            d_query += dot(scores, keys)

            queries, grads = qkv[span, q_lanes], grad_rows[span, q_lanes]

            def row_pair(ref):
                return jnp.concatenate(
                    [
                        jnp.broadcast_to(ref[2 * pair + k : 2 * pair + k + 1, span], (OWN, size))
                        for k in range(2)
                    ],
                    0,
                )

            weights = jnp.exp(dot(own_k, queries, NT) + own_bias - row_pair(log_row))
            slopes = dot(own_v, grads, NT)
            scores = low(weights * (slopes - row_pair(delta_row)))
            d_value += dot(low(weights), grads)
            d_key += dot(scores, queries)
        packed[:, q_lanes] = low(join_heads(d_query) * 0.125)
        packed[:, k_lanes] = low(join_heads(d_key) * 0.125)
        packed[:, v_lanes] = low(join_heads(d_value))

    share = 1.0 / group
    row = lax.broadcasted_iota(jnp.int32, (OWN, 1), 0)
    row_weight = low(jnp.where(row < ROWS, 1.0, share))
    rows = jnp.concatenate([tokens[slot], arrived[...], memory[slot]], 0)
    scaled = packed[...] * row_weight
    for at in range(0, 3 * WIDTH, WIDTH):
        cols = slice(at, at + WIDTH)
        grad_weight[:, cols] = low(dot(rows, scaled[:, cols], TN))
    emit_blocks(
        grad_weight, keep_out, send_out, REDUCE_QKV, block, 16, slice(0, 16), slice(0, 3 * WIDTH)
    )
    query_bias = jnp.sum(high(scaled[:, :WIDTH]), axis=0, keepdims=True)
    value_bias = jnp.sum(high(scaled[:, 2 * WIDTH :]), axis=0, keepdims=True)
    vec = jnp.concatenate([query_bias, value_bias, vector_grads[2:8, :]], 0)
    ups = up_grads[...]
    lane8 = lane_index((8, LANES))
    for p in range(BLOCKS):
        g = p // 8
        top = roll_lanes(vec[:, g * LANES : (g + 1) * LANES], -16 * (p % 8))
        top = jnp.where(lane8 < 16, top, 0.0)
        g = p // 2
        bottom = roll_lanes(ups[:, g * LANES : (g + 1) * LANES], -64 * (p % 2))
        both = jnp.concatenate([top, bottom], 0)
        extra[p * 16 : (p + 1) * 16, :] = split_lanes(both)
    emit_blocks(
        extra,
        keep_out,
        send_out,
        REDUCE_QKV,
        block,
        16,
        slice(0, 16),
        slice(3 * WIDTH, 3 * WIDTH + LANES),
    )

    grad_in = first_grad[...] + dot(packed[...], weight[...], NT)
    square = squares[0]
    for k in range(1, group):
        square += squares[k]
    square = square[:4] + square[4:]
    square = jnp.concatenate([square[k : k + 1] for k in range(4)], 1)
    first, second, _ = split_three(square)
    tail = low(jnp.concatenate([first, second, jnp.zeros((14, WIDTH), F32)], 0))
    own_out[:64, :] = low(grad_in[:64])
    own_out[64:96, :] = low(grad_in[ROWS:])
    own_out[96:, :] = tail
    give_out[:96, :] = low(grad_in[64:])
    give_out[96:, :] = tail


def split_lanes(v):
    first = high(low(v))
    second = pltpu.roll(v - first, 64, v.ndim - 1)
    lanes = lax.broadcasted_iota(jnp.int32, v.shape, v.ndim - 1)
    return low(jnp.where(lanes < 64, first, second))


def fold_kernel(width, keep, other, keep_out, send_out):
    half = keep.shape[0] // 2
    for start, out in ((0, keep_out), (half, send_out)):
        span = slice(start, start + half)
        total = high(keep[span, :, :width]) + high(other[span, :, :width])
        out[:, :, :width] = low(total)
        for k in range(half):
            extra = high(keep[start + k, :, width:]) + high(other[start + k, :, width:])
            out[k, :, width:] = split_lanes(extra + pltpu.roll(extra, 64, 1))


def fold_with_extra(keep, other):
    shape = (keep.shape[0] // 2,) + keep.shape[1:]
    return pl.pallas_call(
        functools.partial(fold_kernel, 3 * WIDTH),
        out_shape=[jax.ShapeDtypeStruct(shape, BF)] * 2,
        name="fold",
    )(keep, other)


def fold_plain(keep, other):
    half = keep.shape[0] // 2
    return tuple(
        low(high(keep[part]) + high(other[part])) for part in (slice(0, half), slice(half, None))
    )


def emit_kernel(layout, mem_rows, *refs):
    lengths, out_own, out_got, grad_own, grad_got = refs[:5]
    out_tokens, out_memory, grad_tokens, grad_memory, rms = refs[5:]
    slot = lax.axis_index("seq") // layout.group
    for own, got, tokens, memory in (
        (out_own, out_got, out_tokens, out_memory),
        (grad_own, grad_got, grad_tokens, grad_memory),
    ):
        for source, at in ((own, slot), (got, 1 - slot)):
            tokens[at] = source[:64, :]
            memory[at] = low(high(source[64:96, :])[:mem_rows])
    result = []
    for source, at in ((grad_own, slot), (grad_got, 1 - slot)):
        tail = high(source[96:112, :])
        square = tail[0:1] + tail[1:2]
        result.append(jnp.sqrt(square / lengths[at].astype(F32)))
    row = lax.broadcasted_iota(jnp.int32, (2, WIDTH), 0)
    rms[...] = jnp.where(row == slot, result[0], result[1])


def call(kernel, name, outs, scratch, args, smem=1, limit=32, flops=0):
    vmem = pl.BlockSpec(memory_space=pltpu.VMEM)
    in_specs = [pl.BlockSpec(memory_space=pltpu.SMEM)] * smem + [vmem] * (len(args) - smem)
    size = sum(a.size * a.dtype.itemsize for a in args)
    return pl.pallas_call(
        kernel,
        out_shape=[jax.ShapeDtypeStruct(shape, kind) for shape, kind in outs],
        in_specs=in_specs,
        out_specs=[vmem] * len(outs),
        scratch_shapes=[pltpu.VMEM(shape, kind) for shape, kind in scratch],
        compiler_params=pltpu.CompilerParams(vmem_limit_bytes=limit * MIB),
        cost_estimate=pl.CostEstimate(flops=flops, bytes_accessed=size, transcendentals=0),
        name=name,
    )(*args)


def local_wide(
    layout,
    tokens,
    memory,
    lengths,
    w_qkv,
    b_query,
    b_value,
    w_out,
    b_out,
    gain_one,
    shift_one,
    w_up,
    b_up,
    w_down,
    b_down,
    gain_two,
    shift_two,
    cot_tokens,
    cot_memory,
):
    mem_rows = memory.shape[1]
    tok_rows = tokens.shape[1]
    slot_len = tok_rows * layout.seq
    key_rows = slot_len + MEM_KEYS
    partner = layout.seq_bits - 1
    slot = lax.axis_index("seq") // layout.group

    def pick(x, at):
        return lax.dynamic_index_in_dim(x, at, 0, False)

    arrived = layout.swap(pick(tokens, 1 - slot), partner)
    near, far = layout.gather_group(jnp.concatenate([pick(tokens, slot), arrived], 0)[None])

    vectors = jnp.stack(
        [b_query, b_value, b_out, gain_one, shift_one, b_down, gain_two, shift_two]
    )
    vectors = layout.join_low(vectors, 1)
    extra = jnp.concatenate(
        [
            jnp.pad(vectors, ((0, 0), (0, LANES - 16))),
            jnp.pad(layout.join_low(b_up, 0)[None], ((0, 7), (0, LANES - 64))),
        ],
        0,
    )
    first = jnp.concatenate([layout.join_low(w_qkv, 0), layout.join_low(w_out, 0), extra], 1)
    qkv_parts = layout.gather(first[None], GATHER_QKV)
    up_parts = layout.gather(layout.join_low(w_up, 0)[None], GATHER_UP)
    down_parts = layout.gather(layout.join_low(w_down, 0)[None], GATHER_DOWN)
    cot_arrived = layout.swap(pick(cot_tokens, 1 - slot), partner)
    pad_rows = ((0, 0), (0, MEM_PAD - mem_rows), (0, 0))
    memory_full = jnp.pad(memory, pad_rows)
    cot_memory_full = jnp.pad(cot_memory, pad_rows)

    qkv, attn, lse_col, vector_rows, up_bias = call(
        functools.partial(forward_kernel, layout, mem_rows, slot_len),
        "attention_forward",
        [
            ((key_rows, 3 * WIDTH), BF),
            ((OWN, WIDTH), F32),
            ((OWN, LANES), F32),
            ((8, WIDTH), F32),
            ((8, FF), F32),
        ],
        [((slot_len + MEM_PAD, WIDTH), BF), ((WIDTH, 3 * WIDTH), BF), ((WIDTH, LANES), BF)],
        (lengths, near, far, memory_full, *qkv_parts),
    )
    (
        pack,
        grad_mem,
        lse_mem,
        delta_mem,
        delta_col,
        first_grad,
        out_own,
        out_send,
        attn_low,
        branch_low,
        hidden_low,
        grad_linear,
        active,
        feed_low,
        vector_grads,
        up_grads,
    ) = call(
        functools.partial(feed_kernel, layout, mem_rows),
        "feed_forward",
        [
            ((1, ROWS + 16, WIDTH), BF),
            ((MEM_PAD, WIDTH), BF),
            ((8, LANES), F32),
            ((8, LANES), F32),
            ((OWN, LANES), F32),
            ((OWN, WIDTH), F32),
            ((64 + MEM_PAD, WIDTH), BF),
            ((64 + MEM_PAD, WIDTH), BF),
            ((OWN, WIDTH), BF),
            ((OWN, WIDTH), BF),
            ((OWN, WIDTH), BF),
            ((OWN, FF), BF),
            ((OWN, FF), BF),
            ((OWN, WIDTH), BF),
            ((8, WIDTH), F32),
            ((8, FF), F32),
        ],
        [((WIDTH, WIDTH), BF), ((WIDTH, FF), BF), ((FF, WIDTH), BF), ((OWN, FF), F32)],
        (
            lengths,
            tokens,
            arrived,
            memory_full,
            cot_tokens,
            cot_arrived,
            cot_memory_full,
            attn,
            lse_col,
            vector_rows,
            up_bias,
            *qkv_parts,
            *up_parts,
            *down_parts,
        ),
    )
    grads_near, grads_far = layout.gather_group(pack)
    out_got = layout.swap(out_send, partner)
    half = BLOCKS // 2
    up_keep, up_send, down_keep, down_send = call(
        functools.partial(weight_kernel, layout),
        "weight_gradients",
        [
            ((half, 16, FF), BF),
            ((half, 16, FF), BF),
            ((half, 80, WIDTH), BF),
            ((half, 80, WIDTH), BF),
        ],
        [((WIDTH, FF), BF), ((FF, WIDTH), BF), ((WIDTH, WIDTH), BF)],
        (attn_low, branch_low, hidden_low, grad_linear, active, feed_low),
        smem=0,
    )
    up_total = layout.reduce(up_keep, up_send, REDUCE_UP, fold_plain)
    down_total = layout.reduce(down_keep, down_send, REDUCE_DOWN, fold_plain)
    qkv_keep, qkv_send, grad_own, grad_send = call(
        functools.partial(backward_kernel, layout, mem_rows, slot_len),
        "attention_backward",
        [
            ((half, 16, 3 * WIDTH + LANES), BF),
            ((half, 16, 3 * WIDTH + LANES), BF),
            ((112, WIDTH), BF),
            ((112, WIDTH), BF),
        ],
        [
            ((WIDTH, 3 * WIDTH), BF),
            ((key_rows, WIDTH), BF),
            ((8, key_rows), F32),
            ((8, key_rows), F32),
            ((layout.group, 8, LANES), F32),
            ((OWN, 3 * WIDTH), BF),
            ((WIDTH, 3 * WIDTH), BF),
            ((WIDTH, LANES), BF),
        ],
        (
            lengths,
            tokens,
            arrived,
            memory_full,
            qkv,
            grads_near,
            grads_far,
            grad_mem,
            lse_mem,
            delta_mem,
            lse_col,
            delta_col,
            first_grad,
            vector_grads,
            up_grads,
            *qkv_parts,
        ),
    )
    qkv_total = layout.reduce(qkv_keep, qkv_send, REDUCE_QKV, fold_with_extra)
    grad_got = layout.swap(grad_send, partner)

    def add(pair):
        return high(pair[0][0]) + high(pair[1][0])

    up_sum = layout.reduce_low(add(up_total), 0)
    down_sum = add(down_total)
    out_sum = layout.reduce_low(down_sum[64:], 0)
    down_sum = layout.reduce_low(down_sum[:64], 0)
    qkv_sum = add(qkv_total)
    extra_sum = qkv_sum[:, 3 * WIDTH :]
    qkv_sum = layout.reduce_low(qkv_sum[:, : 3 * WIDTH], 0)
    vec = layout.reduce_low(extra_sum[:8, :16] + extra_sum[:8, 64:80], 1)
    up_vec = layout.reduce_low(extra_sum[8, :64] + extra_sum[8, 64:], 0)

    out_tokens, out_memory, grad_tokens, grad_memory, rms = call(
        functools.partial(emit_kernel, layout, mem_rows),
        "emit",
        [
            (tokens.shape, BF),
            (memory.shape, BF),
            (tokens.shape, BF),
            (memory.shape, BF),
            ((2, WIDTH), F32),
        ],
        [],
        (lengths, out_own, out_got, grad_own, grad_got),
    )
    return (
        out_tokens,
        out_memory,
        grad_tokens,
        grad_memory,
        qkv_sum,
        vec[0],
        vec[1],
        out_sum,
        vec[2],
        vec[3],
        vec[4],
        up_sum,
        up_vec,
        down_sum,
        vec[5],
        vec[6],
        vec[7],
        rms,
    )


def prepare_kernel(*refs):
    w_qkv, w_out = refs[:2]
    vectors, b_up = refs[2:10], refs[10]
    first, up_cell, sems = refs[11:14]
    cells = refs[14:]
    moves = [
        (w_qkv, first.at[:, : 3 * WIDTH]),
        (w_out, first.at[:, 3 * WIDTH : 4 * WIDTH]),
        (b_up, up_cell),
    ]
    moves += [(v, cells[k]) for k, v in enumerate(vectors)]
    copies = [
        pltpu.make_async_copy(source, target, sems.at[k])
        for k, (source, target) in enumerate(moves)
    ]
    for copy in copies:
        copy.start()
    for copy in copies:
        copy.wait()
    blank = jnp.zeros((1, LANES - 16), F32)
    rows = [jnp.concatenate([high(v[...]).reshape(1, 16), blank], 1) for v in cells]
    rows.append(jnp.concatenate([high(up_cell[...]).reshape(1, 64), blank[:, :64]], 1))
    rows.append(jnp.zeros((7, LANES), F32))
    first[:, 4 * WIDTH :] = low(jnp.concatenate(rows, 0))


def gather_vectors(extra):
    pieces, ups = [], []
    for g in range(4):
        total = jnp.zeros((8, LANES), F32)
        for p in range(8):
            at = (8 * g + p) * 16
            total += roll_lanes(high(extra[at : at + 16, :])[:8], 16 * p)
        pieces.append(total)
    for g in range(16):
        total = jnp.zeros((8, LANES), F32)
        for p in range(2):
            at = (2 * g + p) * 16
            total += roll_lanes(high(extra[at : at + 16, :])[8:], 64 * p)
        ups.append(total)
    return jnp.concatenate(pieces, 1), jnp.concatenate(ups, 1)


def quad_forward_kernel(layout, mem_rows, slot_len, *refs):
    lengths, near, far, memory, w0, w1, w2, w3 = refs[:8]
    attn, qkv_own, rows, w_own, vectors, up_bias = refs[8:14]
    qkv, weight, extra = refs[14:]
    group = layout.group
    place = lax.axis_index("seq")
    slot, rank = place // group, place % group
    block = layout.block()
    length = lengths[slot]
    parts = (w0, w1, w2, w3)
    place_blocks(weight, parts, GATHER_QKV, block, 16, slice(0, 3 * WIDTH))
    place_blocks(extra, parts, GATHER_QKV, block, 16, slice(4 * WIDTH, 4 * WIDTH + LANES))
    for part, masks in zip((near, far), layout.group_masks()):
        for k, mask in enumerate(masks):
            rows[aligned(rank ^ mask, ROWS), :] = part[k]
    rows[slot_len : slot_len + MEM_PAD, :] = memory[...]
    vector_rows, up_rows = gather_vectors(extra)
    vectors[...] = vector_rows
    up_bias[...] = up_rows

    key_rows = slot_len + MEM_KEYS
    filled = slot_len + MEM_PAD
    qkv[filled:key_rows, :] = jnp.zeros((key_rows - filled, 3 * WIDTH), BF)
    for part, shift in enumerate((vector_rows[0:1], None, vector_rows[1:2])):
        lanes = slice(part * WIDTH, (part + 1) * WIDTH)
        value = dot(rows[...], weight[:, lanes])
        qkv[:filled, lanes] = low(value if shift is None else value + shift)
    for part in range(3):
        own = pl.ds(pl.multiple_of(part * WIDTH + rank * LANES, LANES), LANES)
        qkv_own[:, part * LANES : (part + 1) * LANES] = qkv[:, own]
        w_own[:, part * LANES : (part + 1) * LANES] = weight[:, own]

    keep = key_valid((1, key_rows), 1, slot, group, length, slot_len, mem_rows)
    bias = jnp.where(keep, 0.0, -1e30)
    for pair in range(HEADS // 2):
        at = pair * LANES
        own = jnp.concatenate(
            [qkv[aligned(rank, ROWS), at : at + LANES], qkv[slot_len:filled, at : at + LANES]], 0
        )
        keys = qkv[:, WIDTH + at : WIDTH + at + LANES]
        values = qkv[:, 2 * WIDTH + at : 2 * WIDTH + at + LANES]
        scores = dot(both_heads(own, 0.125), keys, NT) + bias
        highest = jnp.max(scores, axis=1, keepdims=True)
        expos = jnp.exp(scores - highest)
        total = jnp.sum(expos, axis=1, keepdims=True)
        attn[:, at : at + LANES] = join_heads(dot(low(expos), values) / total)


def quad_feed_kernel(layout, mem_rows, *refs):
    lengths, tokens, arrived, memory, cots, cot_arrived, cot_memory = refs[:7]
    attn, vectors, up_bias = refs[7:10]
    outs, ups, downs = refs[10:14], refs[14:18], refs[18:22]
    pack, grad_mem, first_grad, out_own, out_send = refs[22:27]
    own, give, vector_grads, up_grads, w_heads = refs[27:32]
    w_out, w_up, w_down, slope, grad_linear = refs[32:]
    group = layout.group
    place = lax.axis_index("seq")
    slot, rank = place // group, place % group
    core = place % 2
    block = layout.block()
    length = lengths[slot]
    place_blocks(w_up, ups, GATHER_UP, block, 16, slice(0, FF))
    place_blocks(w_out, outs, GATHER_QKV, block, 16, slice(3 * WIDTH, 4 * WIDTH))
    place_blocks(w_down, downs, GATHER_DOWN, block, 64, slice(0, WIDTH))
    w_heads[...] = w_out[aligned(rank, LANES), :]

    vec = vectors[...]
    out_bias, gain_one, shift_one, down_bias, gain_two, shift_two = [
        vec[k : k + 1] for k in range(2, 8)
    ]
    rows = jnp.concatenate([high(tokens[slot]), high(arrived[...]), high(memory[...])], 0)
    cot = jnp.concatenate([high(cots[slot]), high(cot_arrived[...]), high(cot_memory[...])], 0)
    valid = jnp.where(own_valid((OWN, 1), slot, group, rank, length, mem_rows), 1.0, 0.0)
    row = lax.broadcasted_iota(jnp.int32, (OWN, 1), 0)
    weight = jnp.where(row < ROWS, 1.0, 1.0 / group)
    weight_low = low(weight)

    def total(v):
        return jnp.sum(v * weight, axis=0, keepdims=True)

    def hand_out(value, start):
        half = value.shape[1] // 2
        first, second = value[:, :half], value[:, half:]
        mine = core == 0
        own[:, start : start + half] = jnp.where(mine, first, second)
        give[:, start : start + half] = jnp.where(mine, second, first)

    heads_out = low(attn[...])
    branch = dot(heads_out, w_out[...]) + out_bias
    normed_one, inverse_one = normalize(rows + branch)
    hidden_one = normed_one * gain_one + shift_one
    hidden_low = low(hidden_one)
    for target in (own, give):
        target[:, FF : FF + WIDTH] = hidden_low
        target[:, FF + WIDTH : FF + 2 * WIDTH] = heads_out
    feed = jnp.zeros((OWN, WIDTH), F32) + down_bias
    for at in range(0, FF, WIDTH):
        cols = slice(at, at + WIDTH)
        t = dot(hidden_low, w_up[:, cols]) + up_bias[0:1, cols]
        square = t * t
        bent = jnp.tanh(0.7978845608 * (t + 0.044715 * (square * t)))
        half = 0.5 * (1.0 + bent)
        slope[:, cols] = half + (0.5 * 0.7978845608) * t * (1.0 - bent * bent) * (
            1.0 + (3 * 0.044715) * square
        )
        act = low(t * half)
        own[:, cols] = act
        give[:, cols] = act
        feed += dot(act, w_down[cols, :])
    normed_two, inverse_two = normalize(hidden_one + feed)
    output = (normed_two * gain_two + shift_two) * valid
    out_own[:HEAD_DIM, :] = low(output[:HEAD_DIM])
    out_own[HEAD_DIM:, :] = low(output[ROWS:])
    out_send[...] = low(output[HEAD_DIM:])
    token_valid = jnp.where(row < ROWS, valid, 0.0)
    squares = jnp.sum(feed * feed * token_valid, axis=0, keepdims=True)

    g = cot * valid
    grads = [None] * 8
    grads[6] = total(g * normed_two)
    grads[7] = total(g)
    second = norm_back(g * gain_two, normed_two, inverse_two)
    grad_feed = low(second)
    hand_out(grad_feed * weight_low, FF + 2 * WIDTH)
    grads[5] = total(high(grad_feed))
    grad_hidden = second
    for at in range(0, FF, WIDTH):
        cols = slice(at, at + WIDTH)
        linear = low(dot(grad_feed, w_down[cols, :], NT) * slope[:, cols])
        grad_linear[:, cols] = linear * weight_low
        up_grads[:, cols] = jnp.broadcast_to(total(high(linear)), (8, WIDTH))
        grad_hidden += dot(linear, w_up[:, cols], NT)
    at = FF + 2 * WIDTH + WIDTH // 2
    own[:, at : at + FF // 2] = grad_linear[:, aligned(core, FF // 2)]
    give[:, at : at + FF // 2] = grad_linear[:, aligned(1 - core, FF // 2)]
    grads[3] = total(grad_hidden * normed_one)
    grads[4] = total(grad_hidden)
    first = norm_back(grad_hidden * gain_one, normed_one, inverse_one)
    first_grad[...] = first
    grad_branch = low(first)
    hand_out(grad_branch * weight_low, FF + 2 * WIDTH + WIDTH // 2 + FF // 2)
    grads[2] = total(high(grad_branch))
    grads[0] = grads[1] = jnp.zeros((1, WIDTH), F32)
    vector_grads[...] = jnp.concatenate(grads, 0)
    pack[0, :ROWS, :] = grad_branch[:ROWS]
    pack[0, ROWS:, :] = low(
        jnp.concatenate([*split_three(squares), jnp.zeros((13, WIDTH), F32)], 0)
    )
    grad_mem[...] = grad_branch[ROWS:]


def quad_weight_kernel(layout, *refs):
    own, got, up_keep, up_send, down_keep, down_send, up, down, out = refs

    def both(start, size):
        cols = slice(start, start + size)
        return jnp.concatenate([own[:, cols], got[:, cols]], 0)

    pair = layout.block() >> 1
    half = WIDTH // 2
    at = FF + 2 * WIDTH
    grad_feed = both(at, half)
    linear = at + half
    grad_branch = both(linear + FF // 2, half)
    for start in range(0, FF, WIDTH):
        down[start : start + WIDTH, :] = low(dot(both(start, WIDTH), grad_feed, TN))
    value = low(dot(both(FF + WIDTH, WIDTH), grad_branch, TN))
    for p in range(BLOCKS):
        out[p % 2, p // 2 * 16 : p // 2 * 16 + 16, :] = value[16 * p : 16 * p + 16]
    every = slice(0, half)
    emit_blocks(down, down_keep, down_send, PAIR_DOWN, pair, 128, slice(0, 128), every)
    for k, (keep, send, order) in enumerate(
        ((up_keep, up_send, PAIR_UP), (down_keep, down_send, PAIR_DOWN))
    ):
        emit_blocks(out.at[k], keep, send, order, pair, 16, slice(128, 144), every)
    hidden = both(FF, WIDTH)
    for start in range(0, FF // 2, WIDTH):
        up[:, start : start + WIDTH] = low(dot(hidden, both(linear + start, WIDTH), TN))
    for k in range(4):
        emit_blocks(
            up.at[:, half * k : half * (k + 1)],
            up_keep,
            up_send,
            PAIR_UP,
            pair,
            32,
            slice(32 * k, 32 * k + 32),
            every,
        )


def quad_backward_kernel(layout, mem_rows, slot_len, *refs):
    lengths, qkv, rows, w_own, w_heads, near, far, grad_mem, vector_grads, up_grads = refs[:10]
    keep_out, send_out, in_keep, in_send, tail = refs[10:15]
    grad_rows, squares, packed, grad_weight, grad_in, vec, extra = refs[15:]
    group = layout.group
    place = lax.axis_index("seq")
    slot, rank = place // group, place % group
    pair = layout.block() >> 1
    length = lengths[slot]
    filled = slot_len + MEM_PAD
    key_rows = slot_len + MEM_KEYS
    for part, masks in zip((near, far), layout.group_masks()):
        for k, mask in enumerate(masks):
            at = rank ^ mask
            grad_rows[aligned(at, ROWS), :] = part[k, :ROWS, :]
            squares[at] = high(part[k, ROWS:, :])
    grad_rows[slot_len:filled, :] = grad_mem[...]

    keep = key_valid((1, key_rows), 1, slot, group, length, slot_len, mem_rows)
    bias = jnp.where(keep, 0.0, -1e30)
    grad_attn = low(dot(grad_rows[...], w_heads[...], NT))
    queries = qkv[:filled, :LANES]
    keys = qkv[:, LANES : 2 * LANES]
    values = qkv[:, 2 * LANES :]
    d_query = jnp.zeros((filled, LANES), F32)
    d_key = jnp.zeros((key_rows, LANES), F32)
    d_value = jnp.zeros((key_rows, LANES), F32)
    for mask in half_masks():
        query = queries * (mask * 0.125)
        grads = grad_attn * mask
        scores = dot(query, keys, NT) + bias
        expos = jnp.exp(scores - jnp.max(scores, axis=1, keepdims=True))
        weights = expos * (1.0 / jnp.sum(expos, axis=1, keepdims=True))
        weights_low = low(weights)
        heads_out = dot(weights_low, values)
        delta = jnp.sum(high(grads) * heads_out, axis=1, keepdims=True)
        slopes = low(weights * (dot(grads, values, NT) - delta))
        d_query += dot(slopes, keys) * (high(mask) * 0.125)
        d_key += dot(slopes, query, TN)
        d_value += dot(weights_low, grads, TN)
    packed[:, :LANES] = low(d_query)
    packed[:, LANES : 2 * LANES] = low(d_key[:filled])
    packed[:, 2 * LANES :] = low(d_value[:filled])

    grad_weight[...] = low(dot(rows[...], packed[...], TN))
    for part in range(3):
        emit_blocks(
            grad_weight.at[:, part * LANES : (part + 1) * LANES],
            keep_out,
            send_out,
            PAIR_QKV,
            pair,
            32,
            slice(32 * part, 32 * part + 32),
            slice(0, LANES),
        )
    grad_in[...] = low(dot(packed[...], w_own[...], NT))
    for k, (target, mask) in enumerate(((in_keep, 0), (in_keep, 1), (in_send, 2), (in_send, 3))):
        start = (k % 2) * ROWS
        target[start : start + ROWS, :] = grad_in[aligned(rank ^ mask, ROWS), :]
    for target in (in_keep, in_send):
        target[2 * ROWS :, :] = grad_in[slot_len:filled, :]

    vec[...] = vector_grads[...]
    own = aligned(rank, LANES)
    vec[0:1, own] = jnp.sum(high(packed[:, :LANES]), axis=0, keepdims=True)
    vec[1:2, own] = jnp.sum(high(packed[:, 2 * LANES :]), axis=0, keepdims=True)
    lanes = lane_index((8, LANES))
    sublane = lax.broadcasted_iota(jnp.int32, (8, LANES), 0)
    for p in range(0, BLOCKS, 2):
        both = []
        for q in (p, p + 1):
            g = q // 8
            cell = roll_lanes(vec[:, g * LANES : (g + 1) * LANES], -16 * (q % 8))
            g = q // 2
            ups = up_grads[:, g * LANES : (g + 1) * LANES]
            up = jnp.zeros((8, LANES), F32)
            for k in range(4):
                up = jnp.where(sublane == k, roll_lanes(ups, 16 - 64 * (q % 2) - 16 * k), up)
            both.append(jnp.where(lanes < 16, cell, jnp.where(lanes < 32, up, 0.0)))
        extra[p * 8 : p * 8 + 16, :] = low(jnp.concatenate(both, 0))
    emit_blocks(extra, keep_out, send_out, PAIR_QKV, pair, 16, slice(96, 112), slice(0, LANES))

    square = squares[0]
    for k in range(1, group):
        square += squares[k]
    square = square[0:1] + square[1:2] + square[2:3]
    tail[...] = low(jnp.concatenate([*split_three(square), jnp.zeros((13, WIDTH), F32)], 0))


def feed_rows(core):
    at = [pl.ds(pl.multiple_of(32 * k + 16 * core, 16), 16) for k in range(4)]
    at.append(pl.ds(pl.multiple_of(144 + 64 * core, 16), 64))
    at.append(pl.ds(pl.multiple_of(128 + 144 * core, 16), 16))
    return at


def turn_feed_kernel(keep, other, send):
    start = 0
    for at in feed_rows(1 - lax.axis_index("seq") % 2):
        send[start : start + at.size, :] = low(high(keep[0, at, :]) + high(other[0, at, :]))
        start += at.size


def emit_feed_kernel(keep, other, got, w_up, w_down, w_out):
    core = lax.axis_index("seq") % 2
    half = WIDTH // 2
    own, theirs = aligned(core, half), aligned(1 - core, half)
    start = 0
    for k, at in enumerate(feed_rows(core)):
        total = high(keep[0, at, :]) + high(other[0, at, :])
        arrived = high(got[start : start + at.size, :])
        start += at.size
        if k < 4:
            w_up[:, pl.ds(pl.multiple_of(core * 1024 + half * k, half), half)] = total
            w_up[:, pl.ds(pl.multiple_of((1 - core) * 1024 + half * k, half), half)] = arrived
        else:
            target = w_down if k == 4 else w_out
            target[:, own] = total
            target[:, theirs] = arrived


def turn_qkv_kernel(keep, other, send):
    away = 1 - lax.axis_index("seq") % 2
    for k, source in enumerate((keep, other)):
        for part in range(3):
            at = pl.ds(pl.multiple_of(32 * part + 16 * away, 16), 16)
            start = 48 * k + 16 * part
            send[start : start + 16, :] = source[0, at, :]
    send[96:112, :] = low(high(keep[0, 96:112, :]) + high(other[0, 96:112, :]))


def emit_qkv_kernel(keep, other, got, w_qkv, *vectors):
    place = lax.axis_index("seq")
    core, rank = place % 2, place % 4
    for part in range(3):
        at = pl.ds(pl.multiple_of(32 * part + 16 * core, 16), 16)
        pieces = (
            (rank, keep[0, at, :]),
            (rank ^ 2, other[0, at, :]),
            (rank ^ 1, got[16 * part : 16 * part + 16, :]),
            (rank ^ 3, got[48 + 16 * part : 64 + 16 * part, :]),
        )
        for whose, piece in pieces:
            lanes = pl.ds(pl.multiple_of(part * WIDTH + whose * LANES, LANES), LANES)
            w_qkv[:, lanes] = high(piece)
    total = high(keep[0, 96:112, :]) + high(other[0, 96:112, :]) + high(got[96:112, :])
    total = jnp.where(core == 0, total[:8], total[8:])
    for k in range(8):
        vectors[k][...] = total[k, :16]
    lanes = lane_index((1, LANES))
    ups = jnp.zeros((1, LANES), F32)
    for k in range(4):
        rolled = roll_lanes(total[k : k + 1], 16 * k - 16)
        ups = jnp.where(jnp.logical_and(lanes >= 16 * k, lanes < 16 * k + 16), rolled, ups)
    vectors[8][...] = ups[0, :64]


def emit_tokens_kernel(layout, mem_rows, *refs):
    lengths, out_own, grad_own, grad_got, tail = refs[:5]
    out_tokens, out_memory, grad_tokens, grad_memory, rms = refs[5:]
    slot = lax.axis_index("seq") // layout.group
    pieces = (
        (out_own, 0, 64, slot, out_tokens, out_memory),
        (grad_got, 112, 176, 1 - slot, out_tokens, out_memory),
        (grad_own, 0, 128, slot, grad_tokens, grad_memory),
        (grad_got, 0, 64, 1 - slot, grad_tokens, grad_memory),
    )
    for source, start, mem, at, tokens, memory in pieces:
        tokens[at] = source[start : start + 64, :]
        memory[at] = low(high(source[mem : mem + 32, :])[:mem_rows])
    result = []
    for cell, at in ((tail[...], slot), (grad_got[96:112, :], 1 - slot)):
        cell = high(cell)
        square = cell[0:1] + cell[1:2] + cell[2:3]
        result.append(jnp.sqrt(square / lengths[at].astype(F32)))
    row = lax.broadcasted_iota(jnp.int32, (2, WIDTH), 0)
    rms[...] = jnp.where(row == slot, result[0], result[1])


def local_quad(
    layout,
    tokens,
    memory,
    lengths,
    w_qkv,
    b_query,
    b_value,
    w_out,
    b_out,
    gain_one,
    shift_one,
    w_up,
    b_up,
    w_down,
    b_down,
    gain_two,
    shift_two,
    cot_tokens,
    cot_memory,
):
    mem_rows = memory.shape[1]
    slot_len = tokens.shape[1] * layout.seq
    key_rows = slot_len + MEM_KEYS
    filled = slot_len + MEM_PAD
    partner = layout.seq_bits - 1
    slot = lax.axis_index("seq") // layout.group

    def pick(x, at):
        return lax.dynamic_index_in_dim(x, at, 0, False)

    small = (b_query, b_value, b_out, gain_one, shift_one, b_down, gain_two, shift_two)
    first = pl.pallas_call(
        prepare_kernel,
        out_shape=jax.ShapeDtypeStruct((16, 4 * WIDTH + LANES), BF),
        in_specs=[pl.BlockSpec(memory_space=pl.ANY)] * 11,
        out_specs=pl.BlockSpec(memory_space=pltpu.VMEM),
        scratch_shapes=[pltpu.VMEM((64,), BF), pltpu.SemaphoreType.DMA((11,))]
        + [pltpu.VMEM((16,), BF)] * 8,
        name="prepare",
    )(w_qkv, w_out, *small, b_up)

    def after(x, *others):
        return lax.optimization_barrier((x, *others))[0]

    def gather(held, order, *ready):
        held = jnp.concatenate([held, layout.block_swap(held, order[1])], 0)
        held = jnp.concatenate([held, layout.block_swap(held, order[2])], 0)
        held = after(held, *ready)
        last = layout.block_swap(held, order[3])
        return held, last, layout.block_swap(held, 0), layout.block_swap(last, 0)

    def begin(x, order):
        x = x[None]
        return jnp.concatenate([x, layout.block_swap(x, order[0])], 0)

    second = begin(w_up, GATHER_UP)
    third = begin(w_down, GATHER_DOWN)
    first = begin(first, GATHER_QKV)
    arrived = layout.swap(pick(after(tokens, first), 1 - slot), partner)
    near = jnp.concatenate([pick(tokens, slot), arrived], 0)[None]
    near = jnp.concatenate([near, layout.swap(near, 1)], 0)
    cot_arrived = layout.swap(pick(after(cot_tokens, third), 1 - slot), partner)
    pad_rows = ((0, MEM_PAD - mem_rows), (0, 0))
    own_memory = jnp.pad(pick(after(memory, third), slot), pad_rows)
    own_cot_memory = jnp.pad(pick(after(cot_memory, third), slot), pad_rows)
    far = layout.swap(near, 0)
    up_parts = gather(second, GATHER_UP, near, own_memory, own_cot_memory)
    down_parts = gather(third, GATHER_DOWN)
    qkv_parts = gather(first, GATHER_QKV)

    attn, qkv_own, rows, w_own, vector_rows, up_bias = call(
        functools.partial(quad_forward_kernel, layout, mem_rows, slot_len),
        "attention_forward",
        [
            ((OWN, WIDTH), F32),
            ((key_rows, 3 * LANES), BF),
            ((filled, WIDTH), BF),
            ((WIDTH, 3 * LANES), BF),
            ((8, WIDTH), F32),
            ((8, FF), F32),
        ],
        [((key_rows, 3 * WIDTH), BF), ((WIDTH, 3 * WIDTH), BF), ((WIDTH, LANES), BF)],
        (lengths, near, far, own_memory, *qkv_parts),
        flops=4 * 10**9,
    )
    (
        pack,
        grad_mem,
        first_grad,
        out_own,
        out_send,
        own,
        give,
        vector_grads,
        up_grads,
        w_heads,
    ) = call(
        functools.partial(quad_feed_kernel, layout, mem_rows),
        "feed_forward",
        [
            ((1, ROWS + 16, WIDTH), BF),
            ((MEM_PAD, WIDTH), BF),
            ((OWN, WIDTH), F32),
            ((64 + MEM_PAD, WIDTH), BF),
            ((64 + MEM_PAD, WIDTH), BF),
            ((OWN, GIVEN), BF),
            ((OWN, GIVEN), BF),
            ((8, WIDTH), F32),
            ((8, FF), F32),
            ((LANES, WIDTH), BF),
        ],
        [
            ((WIDTH, WIDTH), BF),
            ((WIDTH, FF), BF),
            ((FF, WIDTH), BF),
            ((OWN, FF), F32),
            ((OWN, FF), BF),
        ],
        (
            lengths,
            tokens,
            arrived,
            own_memory,
            cot_tokens,
            cot_arrived,
            own_cot_memory,
            attn,
            vector_rows,
            up_bias,
            *qkv_parts,
            *up_parts,
            *down_parts,
        ),
        flops=6 * 10**9,
    )
    taken = layout.swap(give, 0)
    grads_next = layout.swap(pack, 1)
    half = PAIRS // 2
    up_keep, up_send, down_keep, down_send = call(
        functools.partial(quad_weight_kernel, layout),
        "weight_gradients",
        [
            ((half, 144, WIDTH // 2), BF),
            ((half, 144, WIDTH // 2), BF),
            ((half, 144, WIDTH // 2), BF),
            ((half, 144, WIDTH // 2), BF),
        ],
        [((WIDTH, FF // 2), BF), ((FF, WIDTH // 2), BF), ((2, WIDTH // 2, WIDTH // 2), BF)],
        (own, taken),
        smem=0,
        flops=3 * 10**9,
    )
    grads_next, _ = lax.optimization_barrier((grads_next, up_send))
    grads_near = jnp.concatenate([pack, grads_next], 0)
    grads_far = layout.swap(grads_near, 0)
    qkv_keep, qkv_send, in_keep, in_send, tail = call(
        functools.partial(quad_backward_kernel, layout, mem_rows, slot_len),
        "attention_backward",
        [
            ((half, 112, LANES), BF),
            ((half, 112, LANES), BF),
            ((2 * ROWS + MEM_PAD, WIDTH), BF),
            ((2 * ROWS + MEM_PAD, WIDTH), BF),
            ((16, WIDTH), BF),
        ],
        [
            ((filled, WIDTH), BF),
            ((layout.group, 16, WIDTH), F32),
            ((filled, 3 * LANES), BF),
            ((WIDTH, 3 * LANES), BF),
            ((filled, WIDTH), BF),
            ((8, WIDTH), F32),
            ((8 * BLOCKS, LANES), BF),
        ],
        (
            lengths,
            qkv_own,
            rows,
            w_own,
            w_heads,
            grads_near,
            grads_far,
            grad_mem,
            vector_grads,
            up_grads,
        ),
        flops=6 * 10**9,
    )
    swap = layout.pair_swap
    up_other, down_other = swap(up_send, PAIR_UP[0]), swap(down_send, PAIR_DOWN[0])
    up_keep, up_send = fold_plain(up_keep, up_other)
    down_keep, down_send = fold_plain(down_keep, down_other)
    qkv_send = after(qkv_send, up_send)
    up_ready, down_ready = up_send, down_send
    up_other, down_other = swap(up_send, PAIR_UP[1]), swap(down_send, PAIR_DOWN[1])
    up_keep, up_send = fold_plain(up_keep, up_other)
    down_keep, down_send = fold_plain(down_keep, down_other)
    feed_keep = jnp.concatenate([up_keep, down_keep], 1)
    feed_send = jnp.concatenate([up_send, down_send], 1)
    feed_other = swap(feed_send, PAIR_UP[2])
    feed_keep, feed_send = fold_plain(feed_keep, feed_other)
    in_sum = high(in_keep) + high(after(layout.swap(in_send, 1), up_ready, down_ready))
    in_send = low(in_sum[ROWS:])
    in_got = layout.swap(in_send, 0)
    grad_own = low(
        jnp.concatenate([in_sum[:ROWS], high(in_send[ROWS:])], 0) + high(in_got) + first_grad
    )
    grad_got = layout.swap(jnp.concatenate([grad_own[64:], tail, out_send], 0), partner)

    feed_total = feed_keep, swap(after(feed_send, grad_got), PAIR_UP[3])
    qkv_total = layout.reduce(qkv_keep, qkv_send, PAIR_QKV, fold_plain, swap)

    (feed_send,) = call(
        turn_feed_kernel, "turn_feed", [((144, WIDTH // 2), BF)], [], feed_total, smem=0
    )
    out_tokens, out_memory, grad_tokens, grad_memory, rms = call(
        functools.partial(emit_tokens_kernel, layout, mem_rows),
        "emit_tokens",
        [
            (tokens.shape, BF),
            (memory.shape, BF),
            (tokens.shape, BF),
            (memory.shape, BF),
            ((2, WIDTH), F32),
        ],
        [],
        (lengths, out_own, grad_own, grad_got, tail),
    )
    (qkv_send,) = call(turn_qkv_kernel, "turn_qkv", [((112, LANES), BF)], [], qkv_total, smem=0)
    qkv_sum, *vec = call(
        emit_qkv_kernel,
        "emit_qkv",
        [(w_qkv.shape, F32)] + [((16,), F32)] * 8 + [((64,), F32)],
        [],
        (*qkv_total, layout.swap(qkv_send, 0)),
        smem=0,
    )
    up_sum, down_sum, out_sum = call(
        emit_feed_kernel,
        "emit_feed",
        [(w_up.shape, F32), (w_down.shape, F32), (w_out.shape, F32)],
        [],
        (*feed_total, after(layout.swap(feed_send, 0), rms, qkv_sum)),
        smem=0,
    )
    return (
        out_tokens,
        out_memory,
        grad_tokens,
        grad_memory,
        qkv_sum,
        vec[0],
        vec[1],
        out_sum,
        vec[2],
        vec[3],
        vec[4],
        up_sum,
        vec[8],
        down_sum,
        vec[5],
        vec[6],
        vec[7],
        rms,
    )


def solution(mesh):
    rows = P("dp", "seq", None)
    slots = P("dp", None, None)
    matrix = P(("dp", "seq"), None)
    vector = P(("dp", "seq"))
    weights = (
        matrix,
        vector,
        vector,
        matrix,
        vector,
        vector,
        vector,
        matrix,
        vector,
        matrix,
        vector,
        vector,
        vector,
    )
    layout = Layout(mesh)
    quad = layout.group == 4 and layout.devices == BLOCKS
    return jax.shard_map(
        functools.partial(local_quad if quad else local_wide, layout),
        mesh=mesh,
        in_specs=(rows, slots, P("dp"), *weights, rows, slots),
        out_specs=(rows, slots, rows, slots, *weights, P("dp", None)),
        check_vma=False,
    )
```

```python
import functools

import jax
import jax.numpy as jnp
from jax import lax
from jax.experimental import pallas as pl
from jax.experimental.pallas import tpu as pltpu
from jax.sharding import PartitionSpec as P

HEADS = 8
HEAD_DIM = 64
WIDTH = 512
FF = 2048
BLOCKS = 32
ROWS = 128
MEM_PAD = 32
OWN = ROWS + MEM_PAD
MEM_KEYS = 128
LANES = 128
MIB = 1 << 20

BF = jnp.bfloat16
F32 = jnp.float32
NN = (((1,), (0,)), ((), ()))
NT = (((1,), (1,)), ((), ()))
TN = (((0,), (0,)), ((), ()))

GATHER_QKV = (2, 1, 4, 3, 0)
GATHER_UP = (2, 3, 1, 4, 0)
GATHER_DOWN = (2, 4, 3, 1, 0)
REDUCE_UP = (0, 1, 4, 3, 2)
REDUCE_DOWN = (0, 3, 1, 4, 2)
REDUCE_QKV = (0, 4, 3, 1, 2)
PAIRS = BLOCKS // 2
PAIR_MAIN = ((2, 3, 0, 1), (3, 2, 0, 1))
PAIR_REST = ((0, 3, 2, 1), (0, 2, 3, 1))
PAIR_QKV = ((3, 2, 1), (2, 3, 1))


def dot(a, b, dims=NN):
    return lax.dot_general(a, b, dims, preferred_element_type=F32)


def low(v):
    return v.astype(BF)


def high(v):
    return v.astype(F32)


def split_three(v):
    first = high(low(v))
    second = high(low(v - first))
    return first, second, high(low(v - first - second))


def aligned(index, size):
    return pl.ds(pl.multiple_of(index * size, size), size)


class Layout:
    def __init__(self, mesh):
        self.dp = mesh.shape["dp"]
        self.seq = mesh.shape["seq"]
        self.devices = self.dp * self.seq
        self.low_bits = (self.devices // BLOCKS).bit_length() - 1
        self.group = self.seq // 2
        self.seq_bits = self.seq.bit_length() - 1

    def dim(self, bit):
        if bit < self.seq_bits:
            return "seq", 1 << bit
        return "dp", 1 << (bit - self.seq_bits)

    def swap(self, x, bit):
        axis, mask = self.dim(bit)
        size = self.seq if axis == "seq" else self.dp
        return lax.ppermute(x, axis, [(i, i ^ mask) for i in range(size)])

    def block_swap(self, x, bit):
        return self.swap(x, bit + self.low_bits)

    def pair_swap(self, x, bit):
        return self.swap(x, bit + 1)

    def pair_swap_by_core(self, x, bits):
        pairs = [(i, i ^ (2 << bits[i % 2])) for i in range(self.devices)]
        return lax.ppermute(x, ("dp", "seq"), pairs)

    def device(self):
        return lax.axis_index("dp") * self.seq + lax.axis_index("seq")

    def block(self):
        return self.device() >> self.low_bits

    def join_low(self, x, axis):
        for bit in range(self.low_bits):
            other = self.swap(x, bit)
            first = (self.device() >> bit) % 2 == 0
            x = jnp.where(
                first, jnp.concatenate([x, other], axis), jnp.concatenate([other, x], axis)
            )
        return x

    def reduce_low(self, x, axis):
        for bit in reversed(range(self.low_bits)):
            first = (self.device() >> bit) % 2 == 0
            lower, upper = jnp.split(x, 2, axis)
            other = self.swap(jnp.where(first, upper, lower), bit)
            x = jnp.where(first, lower, upper) + other
        return x

    def gather(self, x, order):
        held = x
        for bit in order[:3]:
            held = jnp.concatenate([held, self.block_swap(held, bit)], 0)
        last = self.block_swap(held, order[3])
        return held, last, self.block_swap(held, order[4]), self.block_swap(last, order[4])

    def reduce(self, keep, send, order, fold, swap=None):
        swap = swap or self.block_swap
        other = swap(send, order[0])
        for bit in order[1:]:
            keep, send = fold(keep, other)
            other = swap(send, bit)
        return keep, other

    def gather_group(self, x):
        near = x
        mask = self.group // 2
        while mask > 1:
            near = jnp.concatenate([near, self.swap(near, mask.bit_length() - 1)], 0)
            mask //= 2
        return near, self.swap(near, 0)

    def group_masks(self):
        near = [0]
        mask = self.group // 2
        while mask > 1:
            near += [m ^ mask for m in near]
            mask //= 2
        return near, [m ^ 1 for m in near]


def gather_masks(order):
    held = [0]
    for bit in order[:3]:
        held = held + [m ^ (1 << bit) for m in held]
    last = [m ^ (1 << order[3]) for m in held]
    swapped = [[m ^ (1 << order[4]) for m in part] for part in (held, last)]
    return held, last, swapped[0], swapped[1]


def reduce_masks(order):
    bits = len(order)
    return [
        sum(((place >> (bits - 1 - k)) & 1) << bit for k, bit in enumerate(order))
        for place in range(1 << bits)
    ]


def place_blocks(target, parts, order, block, unit, lanes):
    for part, masks in zip(parts, gather_masks(order)):
        for place, mask in enumerate(masks):
            target[aligned(block ^ mask, unit), :] = part[place, :, lanes]


def emit_blocks(source, keep, send, order, block, unit, at, lanes):
    masks = reduce_masks(order)
    half = len(masks) // 2
    for place, mask in enumerate(masks):
        target = keep if place < half else send
        target[place % half, at, lanes] = source[aligned(block ^ mask, unit), :]


def emit_pairs(source, keep, send, orders, pair, core, unit, at):
    masks = [reduce_masks(order) for order in orders]
    count = len(masks[0]) // 2
    for spot, (first, second) in enumerate(zip(*masks)):
        target = keep if spot < count else send
        whose = pair ^ jnp.where(core == 0, first, second)
        target[spot % count, at, :] = source[aligned(whose, unit), :]


def roll_lanes(v, shift):
    return pltpu.roll(v, shift % LANES, 1) if shift % LANES else v


def lane_index(shape):
    return lax.broadcasted_iota(jnp.int32, shape, 1)


def normalize(hidden):
    center = hidden - jnp.mean(hidden, axis=-1, keepdims=True)
    inverse = lax.rsqrt(jnp.mean(center * center, axis=-1, keepdims=True) + 1e-05)
    return center * inverse, inverse


def norm_back(grad_normed, normed, inverse):
    mean_grad = jnp.mean(grad_normed, axis=-1, keepdims=True)
    mean_cross = jnp.mean(grad_normed * normed, axis=-1, keepdims=True)
    return inverse * (grad_normed - mean_grad - normed * mean_cross)


def half_masks():
    first = lane_index((1, LANES)) < HEAD_DIM
    return low(jnp.where(first, 1.0, 0.0)), low(jnp.where(first, 0.0, 1.0))


def both_heads(pair, scale=1.0):
    first, second = half_masks()
    return jnp.concatenate([pair * (first * scale), pair * (second * scale)], 0)


def join_heads(pair):
    half = pair.shape[0] // 2
    return jnp.where(lane_index((half, LANES)) < HEAD_DIM, pair[:half], pair[half:])


def head_column(columns, pair):
    lanes = lane_index(columns.shape)
    picked = [
        jnp.sum(jnp.where(lanes == 2 * pair + k, columns, 0.0), axis=1, keepdims=True)
        for k in range(2)
    ]
    return jnp.concatenate(picked, 0)


def key_valid(shape, axis, slot, group, length, slot_len, mem_rows):
    place = lax.broadcasted_iota(jnp.int32, shape, axis)
    half = (place >> 6) & 1
    position = ((half ^ slot) * group + (place >> 7)) * HEAD_DIM + (place & 63)
    token = jnp.logical_and(place < slot_len, position < length)
    mem = jnp.logical_and(place >= slot_len, place < slot_len + mem_rows)
    return jnp.logical_or(token, mem)


def own_valid(shape, slot, group, rank, length, mem_rows):
    place = lax.broadcasted_iota(jnp.int32, shape, 0)
    half = (place >> 6) & 1
    position = ((half ^ slot) * group + rank) * HEAD_DIM + (place & 63)
    token = jnp.logical_and(place < ROWS, position < length)
    mem = jnp.logical_and(place >= ROWS, place < ROWS + mem_rows)
    return jnp.logical_or(token, mem)


def forward_kernel(layout, mem_rows, slot_len, *refs):
    lengths, near, far, memory, w0, w1, w2, w3 = refs[:8]
    qkv, attn, lse_col, vectors, up_bias = refs[8:13]
    rows, weight, extra = refs[13:]
    group = layout.group
    place = lax.axis_index("seq")
    slot, rank = place // group, place % group
    block = layout.block()
    length = lengths[slot]
    parts = (w0, w1, w2, w3)
    place_blocks(weight, parts, GATHER_QKV, block, 16, slice(0, 3 * WIDTH))
    place_blocks(extra, parts, GATHER_QKV, block, 16, slice(4 * WIDTH, FIRST))
    for part, masks in zip((near, far), layout.group_masks()):
        for k, mask in enumerate(masks):
            rows[aligned(rank ^ mask, ROWS), :] = part[k]
    rows[slot_len : slot_len + MEM_PAD, :] = memory[slot]

    pieces, ups = [], []
    for g in range(4):
        total = jnp.zeros((8, LANES), F32)
        for p in range(8):
            total += roll_lanes(high(extra[(8 * g + p) * 16 : (8 * g + p + 1) * 16, :])[:8], 16 * p)
        pieces.append(total)
    for g in range(16):
        total = jnp.zeros((8, LANES), F32)
        for p in range(2):
            at = (2 * g + p) * 16
            total += roll_lanes(high(extra[at : at + 16, :])[8:], 64 * p)
        ups.append(total)
    vector_rows = jnp.concatenate(pieces, 1)
    vectors[...] = vector_rows
    up_bias[...] = jnp.concatenate(ups, 1)

    key_rows = slot_len + MEM_KEYS
    filled = slot_len + MEM_PAD
    qkv[filled:key_rows, :] = jnp.zeros((key_rows - filled, 3 * WIDTH), BF)
    shifts = (vector_rows[0:1], None, vector_rows[1:2])
    step = 544 if filled == 544 else 512
    for start in range(0, filled, step):
        size = min(step, filled - start)
        for part, shift in enumerate(shifts):
            lanes = slice(part * WIDTH, (part + 1) * WIDTH)
            value = dot(rows[start : start + size, :], weight[:, lanes])
            qkv[start : start + size, lanes] = low(value if shift is None else value + shift)

    keep = key_valid((1, key_rows), 1, slot, group, length, slot_len, mem_rows)
    bias = jnp.where(keep, 0.0, -1e30)
    log_columns = jnp.zeros((OWN, LANES), F32)
    for pair in range(HEADS // 2):
        at = pair * LANES
        own = jnp.concatenate(
            [qkv[aligned(rank, ROWS), at : at + LANES], qkv[slot_len:filled, at : at + LANES]], 0
        )
        keys = qkv[:, WIDTH + at : WIDTH + at + LANES]
        values = qkv[:, 2 * WIDTH + at : 2 * WIDTH + at + LANES]
        scores = dot(both_heads(own, 0.125), keys, NT) + bias
        highest = jnp.max(scores, axis=1, keepdims=True)
        expos = jnp.exp(scores - highest)
        total = jnp.sum(expos, axis=1, keepdims=True)
        attn[:, at : at + LANES] = join_heads(dot(low(expos), values) / total)
        log_total = highest + jnp.log(total)
        lanes = lane_index((OWN, LANES))
        log_columns = jnp.where(lanes == 2 * pair, log_total[:OWN], log_columns)
        log_columns = jnp.where(lanes == 2 * pair + 1, log_total[OWN:], log_columns)
    lse_col[...] = log_columns


def feed_kernel(layout, mem_rows, *refs):
    lengths, tokens, arrived, memory, cots, cot_arrived, cot_memory = refs[:7]
    attn, lse_col, vectors, up_bias = refs[7:11]
    outs, ups, downs = refs[11:15], refs[15:19], refs[19:23]
    pack, grad_mem, lse_mem, delta_mem, delta_col, first_grad, out_own, out_send = refs[23:31]
    attn_low, branch_low, hidden_low, grad_linear, active, feed_low, vector_grads, up_grads = refs[
        31:39
    ]
    w_out, w_up, w_down, slope = refs[39:]
    group = layout.group
    place = lax.axis_index("seq")
    slot, rank = place // group, place % group
    block = layout.block()
    length = lengths[slot]
    place_blocks(w_out, outs, GATHER_QKV, block, 16, slice(3 * WIDTH, 4 * WIDTH))
    place_blocks(w_up, ups, GATHER_UP, block, 16, slice(0, FF))
    place_blocks(w_down, downs, GATHER_DOWN, block, 64, slice(0, WIDTH))

    vec = vectors[...]
    out_bias, gain_one, shift_one, down_bias, gain_two, shift_two = [
        vec[k : k + 1] for k in range(2, 8)
    ]
    rows = jnp.concatenate([high(tokens[slot]), high(arrived[...]), high(memory[slot])], 0)
    cot = jnp.concatenate([high(cots[slot]), high(cot_arrived[...]), high(cot_memory[slot])], 0)
    valid = jnp.where(own_valid((OWN, 1), slot, group, rank, length, mem_rows), 1.0, 0.0)
    share = 1.0 / group
    row = lax.broadcasted_iota(jnp.int32, (OWN, 1), 0)
    weight = jnp.where(row < ROWS, 1.0, share)
    weight_low = low(weight)

    def total(v):
        return jnp.sum(v * weight, axis=0, keepdims=True)

    heads_out = attn[...]
    attn_low[...] = low(heads_out)
    branch = dot(attn_low[...], w_out[...]) + out_bias
    normed_one, inverse_one = normalize(rows + branch)
    hidden_one = normed_one * gain_one + shift_one
    hidden_low[...] = low(hidden_one)
    feed = jnp.zeros((OWN, WIDTH), F32) + down_bias
    for at in range(0, FF, WIDTH):
        cols = slice(at, at + WIDTH)
        t = dot(hidden_low[...], w_up[:, cols]) + up_bias[0:1, cols]
        square = t * t
        bent = jnp.tanh(0.7978845608 * (t + 0.044715 * (square * t)))
        half = 0.5 * (1.0 + bent)
        slope[:, cols] = half + (0.5 * 0.7978845608) * t * (1.0 - bent * bent) * (
            1.0 + (3 * 0.044715) * square
        )
        act = low(t * half)
        active[:, cols] = act
        feed += dot(act, w_down[cols, :])
    normed_two, inverse_two = normalize(hidden_one + feed)
    output = (normed_two * gain_two + shift_two) * valid
    out_own[:HEAD_DIM, :] = low(output[:HEAD_DIM])
    out_own[HEAD_DIM:, :] = low(output[ROWS:])
    out_send[...] = low(output[HEAD_DIM:])
    token_valid = jnp.where(row < ROWS, valid, 0.0)
    squares = jnp.sum(feed * feed * token_valid, axis=0, keepdims=True)

    g = cot * valid
    grads = [None] * 8
    grads[6] = total(g * normed_two)
    grads[7] = total(g)
    second = norm_back(g * gain_two, normed_two, inverse_two)
    grad_feed = low(second)
    feed_low[...] = grad_feed * weight_low
    grads[5] = total(high(grad_feed))
    grad_hidden = second
    for at in range(0, FF, WIDTH):
        cols = slice(at, at + WIDTH)
        linear = low(dot(grad_feed, w_down[cols, :], NT) * slope[:, cols])
        grad_linear[:, cols] = linear * weight_low
        up_grads[:, cols] = jnp.broadcast_to(total(high(linear)), (8, WIDTH))
        grad_hidden += dot(linear, w_up[:, cols], NT)
    grads[3] = total(grad_hidden * normed_one)
    grads[4] = total(grad_hidden)
    first = norm_back(grad_hidden * gain_one, normed_one, inverse_one)
    first_grad[...] = first
    grad_branch = low(first)
    branch_low[...] = grad_branch * weight_low
    grads[2] = total(high(grad_branch))
    grads[0] = grads[1] = jnp.zeros((1, WIDTH), F32)
    vector_grads[...] = jnp.concatenate(grads, 0)

    grad_attn = low(dot(grad_branch, w_out[...], NT))
    product = high(grad_attn) * heads_out
    chosen = lax.broadcasted_iota(jnp.int32, (16, WIDTH), 0)
    head = lax.broadcasted_iota(jnp.int32, (16, WIDTH), 1) // HEAD_DIM
    pick = low(jnp.where(chosen == head, 1.0, 0.0))
    down = lax.broadcasted_iota(jnp.int32, (WIDTH, LANES), 0) // HEAD_DIM
    pick_col = low(jnp.where(down == lane_index((WIDTH, LANES)), 1.0, 0.0))
    identity = low(
        jnp.where(
            lax.broadcasted_iota(jnp.int32, (16, LANES), 0) == lane_index((16, LANES)), 1.0, 0.0
        )
    )
    terms = [low(v) for v in split_three(product)]
    delta_col[...] = sum(dot(v, pick_col) for v in terms)
    delta_row = sum(dot(pick, v, NT) for v in terms)[:8]
    log_row = sum(dot(identity, low(v), NT) for v in split_three(lse_col[...]))[:8]
    log_terms = split_three(log_row[:, :ROWS])
    delta_terms = split_three(delta_row[:, :ROWS])
    square_terms = split_three(squares)
    square_rows = jnp.concatenate(
        [v[:, k * LANES : (k + 1) * LANES] for v in square_terms[:2] for k in range(4)], 0
    )
    pack[0, :ROWS, :] = grad_attn[:ROWS]
    pack[0, ROWS:, :] = low(
        jnp.concatenate(
            [
                jnp.concatenate([*log_terms, delta_terms[0]], 1),
                jnp.concatenate(
                    [delta_terms[1], delta_terms[2], square_rows, jnp.zeros((8, LANES), F32)], 1
                ),
            ],
            0,
        )
    )
    grad_mem[...] = grad_attn[ROWS:]
    blank = jnp.zeros((8, LANES - MEM_PAD), F32)
    lse_mem[...] = jnp.concatenate([log_row[:, ROWS:], blank], 1)
    delta_mem[...] = jnp.concatenate([delta_row[:, ROWS:], blank], 1)


def weight_kernel(layout, *refs):
    attn_low, branch_low, hidden_low, grad_linear, active, feed_low = refs[:6]
    up_keep, up_send, down_keep, down_send = refs[6:10]
    up, down, out = refs[10:]
    block = layout.block()
    for at in range(0, FF, WIDTH):
        cols = slice(at, at + WIDTH)
        down[cols, :] = low(dot(active[:, cols], feed_low[...], TN))
    out[...] = low(dot(attn_low[...], branch_low[...], TN))
    every = slice(0, WIDTH)
    emit_blocks(down, down_keep, down_send, REDUCE_DOWN, block, 64, slice(0, 64), every)
    emit_blocks(out, down_keep, down_send, REDUCE_DOWN, block, 16, slice(64, 80), every)
    for at in range(0, FF, WIDTH):
        cols = slice(at, at + WIDTH)
        up[:, cols] = low(dot(hidden_low[...], grad_linear[:, cols], TN))
    emit_blocks(up, up_keep, up_send, REDUCE_UP, block, 16, slice(0, 16), slice(0, FF))


def backward_kernel(layout, mem_rows, slot_len, *refs):
    lengths, tokens, arrived, memory, qkv, near, far, grad_mem, lse_mem, delta_mem = refs[:10]
    lse_col, delta_col, first_grad, vector_grads, up_grads = refs[10:15]
    parts = refs[15:19]
    keep_out, send_out, own_out, give_out = refs[19:23]
    weight, grad_rows, log_row, delta_row, squares, packed, grad_weight, extra = refs[23:]
    group = layout.group
    place = lax.axis_index("seq")
    slot, rank = place // group, place % group
    block = layout.block()
    length = lengths[slot]
    filled = slot_len + MEM_PAD
    key_rows = slot_len + MEM_KEYS
    place_blocks(weight, parts, GATHER_QKV, block, 16, slice(0, 3 * WIDTH))
    for part, masks in zip((near, far), layout.group_masks()):
        for k, mask in enumerate(masks):
            at = rank ^ mask
            grad_rows[aligned(at, ROWS), :] = part[k, :ROWS, :]
            more = high(part[k, ROWS:, :])
            cell = [[more[8 * a : 8 * a + 8, LANES * b : LANES * (b + 1)] for b in range(4)] for a in range(2)]
            log_row[:, aligned(at, LANES)] = cell[0][0] + cell[0][1] + cell[0][2]
            delta_row[:, aligned(at, LANES)] = cell[0][3] + cell[1][0] + cell[1][1]
            squares[at] = cell[1][2]
    grad_rows[slot_len:filled, :] = grad_mem[...]
    grad_rows[filled:, :] = jnp.zeros((key_rows - filled, WIDTH), BF)
    log_row[:, slot_len:] = lse_mem[...]
    delta_row[:, slot_len:] = delta_mem[...]

    own_keep = jnp.where(own_valid((OWN, 1), slot, group, rank, length, mem_rows), 0.0, -1e30)
    own_bias = jnp.concatenate([own_keep, own_keep], 0)
    chunk = min(slot_len, 512)
    spans = [(s, chunk) for s in range(0, slot_len, chunk)]
    spans[-1] = (spans[-1][0], chunk + MEM_KEYS)

    def own_rows(ref, lanes):
        return jnp.concatenate([ref[aligned(rank, ROWS), lanes], ref[slot_len:filled, lanes]], 0)

    for pair in range(HEADS // 2):
        at = pair * LANES
        q_lanes = slice(at, at + LANES)
        k_lanes = slice(WIDTH + at, WIDTH + at + LANES)
        v_lanes = slice(2 * WIDTH + at, 2 * WIDTH + at + LANES)
        own_q = both_heads(own_rows(qkv, q_lanes), 0.125)
        own_k = both_heads(own_rows(qkv, k_lanes), 0.125)
        own_v = both_heads(own_rows(qkv, v_lanes))
        own_g = both_heads(own_rows(grad_rows, q_lanes))
        log_column = head_column(lse_col[...], pair)
        delta_column = head_column(delta_col[...], pair)
        d_query = jnp.zeros((2 * OWN, LANES), F32)
        d_key = jnp.zeros((2 * OWN, LANES), F32)
        d_value = jnp.zeros((2 * OWN, LANES), F32)
        for start, size in spans:
            span = slice(start, start + size)
            keep = (
                lax.broadcasted_iota(jnp.int32, (1, size), 1) + start
            )
            half = (keep >> 6) & 1
            position = ((half ^ slot) * group + (keep >> 7)) * HEAD_DIM + (keep & 63)
            good = jnp.logical_or(
                jnp.logical_and(keep < slot_len, position < length),
                jnp.logical_and(keep >= slot_len, keep < slot_len + mem_rows),
            )
            bias = jnp.where(good, 0.0, -1e30)
            keys, values = qkv[span, k_lanes], qkv[span, v_lanes]
            weights = jnp.exp(dot(own_q, keys, NT) + bias - log_column)
            slopes = dot(own_g, values, NT)
            scores = low(weights * (slopes - delta_column))
            d_query += dot(scores, keys)

            queries, grads = qkv[span, q_lanes], grad_rows[span, q_lanes]

            def row_pair(ref):
                return jnp.concatenate(
                    [
                        jnp.broadcast_to(ref[2 * pair + k : 2 * pair + k + 1, span], (OWN, size))
                        for k in range(2)
                    ],
                    0,
                )

            weights = jnp.exp(dot(own_k, queries, NT) + own_bias - row_pair(log_row))
            slopes = dot(own_v, grads, NT)
            scores = low(weights * (slopes - row_pair(delta_row)))
            d_value += dot(low(weights), grads)
            d_key += dot(scores, queries)
        packed[:, q_lanes] = low(join_heads(d_query) * 0.125)
        packed[:, k_lanes] = low(join_heads(d_key) * 0.125)
        packed[:, v_lanes] = low(join_heads(d_value))

    share = 1.0 / group
    row = lax.broadcasted_iota(jnp.int32, (OWN, 1), 0)
    row_weight = low(jnp.where(row < ROWS, 1.0, share))
    rows = jnp.concatenate([tokens[slot], arrived[...], memory[slot]], 0)
    scaled = packed[...] * row_weight
    for at in range(0, 3 * WIDTH, WIDTH):
        cols = slice(at, at + WIDTH)
        grad_weight[:, cols] = low(dot(rows, scaled[:, cols], TN))
    emit_blocks(
        grad_weight, keep_out, send_out, REDUCE_QKV, block, 16, slice(0, 16), slice(0, 3 * WIDTH)
    )
    query_bias = jnp.sum(high(scaled[:, :WIDTH]), axis=0, keepdims=True)
    value_bias = jnp.sum(high(scaled[:, 2 * WIDTH :]), axis=0, keepdims=True)
    vec = jnp.concatenate([query_bias, value_bias, vector_grads[2:8, :]], 0)
    ups = up_grads[...]
    lane8 = lane_index((8, LANES))
    for p in range(BLOCKS):
        g = p // 8
        top = roll_lanes(vec[:, g * LANES : (g + 1) * LANES], -16 * (p % 8))
        top = jnp.where(lane8 < 16, top, 0.0)
        g = p // 2
        bottom = roll_lanes(ups[:, g * LANES : (g + 1) * LANES], -64 * (p % 2))
        both = jnp.concatenate([top, bottom], 0)
        extra[p * 16 : (p + 1) * 16, :] = split_lanes(both)
    emit_blocks(
        extra,
        keep_out,
        send_out,
        REDUCE_QKV,
        block,
        16,
        slice(0, 16),
        slice(3 * WIDTH, 3 * WIDTH + LANES),
    )

    grad_in = first_grad[...] + dot(packed[...], weight[...], NT)
    square = squares[0]
    for k in range(1, group):
        square += squares[k]
    square = square[:4] + square[4:]
    square = jnp.concatenate([square[k : k + 1] for k in range(4)], 1)
    first, second, _ = split_three(square)
    tail = low(jnp.concatenate([first, second, jnp.zeros((14, WIDTH), F32)], 0))
    own_out[:64, :] = low(grad_in[:64])
    own_out[64:96, :] = low(grad_in[ROWS:])
    own_out[96:, :] = tail
    give_out[:96, :] = low(grad_in[64:])
    give_out[96:, :] = tail


def split_lanes(v):
    first = high(low(v))
    second = pltpu.roll(v - first, 64, v.ndim - 1)
    lanes = lax.broadcasted_iota(jnp.int32, v.shape, v.ndim - 1)
    return low(jnp.where(lanes < 64, first, second))


def fold_kernel(width, keep, other, keep_out, send_out):
    half = keep.shape[0] // 2
    for start, out in ((0, keep_out), (half, send_out)):
        span = slice(start, start + half)
        total = high(keep[span, :, :width]) + high(other[span, :, :width])
        out[:, :, :width] = low(total)
        for k in range(half):
            extra = high(keep[start + k, :, width:]) + high(other[start + k, :, width:])
            out[k, :, width:] = split_lanes(extra + pltpu.roll(extra, 64, 1))


def fold_with_extra(keep, other):
    shape = (keep.shape[0] // 2,) + keep.shape[1:]
    return pl.pallas_call(
        functools.partial(fold_kernel, 3 * WIDTH),
        out_shape=[jax.ShapeDtypeStruct(shape, BF)] * 2,
        name="fold",
    )(keep, other)


def fold_plain(keep, other):
    half = keep.shape[0] // 2
    return tuple(
        low(high(keep[part]) + high(other[part])) for part in (slice(0, half), slice(half, None))
    )


def emit_kernel(layout, mem_rows, *refs):
    lengths, out_own, out_got, grad_own, grad_got = refs[:5]
    out_tokens, out_memory, grad_tokens, grad_memory, rms = refs[5:]
    slot = lax.axis_index("seq") // layout.group
    for own, got, tokens, memory in (
        (out_own, out_got, out_tokens, out_memory),
        (grad_own, grad_got, grad_tokens, grad_memory),
    ):
        for source, at in ((own, slot), (got, 1 - slot)):
            tokens[at] = source[:64, :]
            memory[at] = low(high(source[64:96, :])[:mem_rows])
    result = []
    for source, at in ((grad_own, slot), (grad_got, 1 - slot)):
        tail = high(source[96:112, :])
        square = tail[0:1] + tail[1:2]
        result.append(jnp.sqrt(square / lengths[at].astype(F32)))
    row = lax.broadcasted_iota(jnp.int32, (2, WIDTH), 0)
    rms[...] = jnp.where(row == slot, result[0], result[1])


def call(kernel, name, outs, scratch, args, smem=1, limit=32, flops=0):
    vmem = pl.BlockSpec(memory_space=pltpu.VMEM)
    in_specs = [pl.BlockSpec(memory_space=pltpu.SMEM)] * smem + [vmem] * (len(args) - smem)
    size = sum(a.size * a.dtype.itemsize for a in args)
    return pl.pallas_call(
        kernel,
        out_shape=[jax.ShapeDtypeStruct(shape, kind) for shape, kind in outs],
        in_specs=in_specs,
        out_specs=[vmem] * len(outs),
        scratch_shapes=[pltpu.VMEM(shape, kind) for shape, kind in scratch],
        compiler_params=pltpu.CompilerParams(vmem_limit_bytes=limit * MIB),
        cost_estimate=pl.CostEstimate(flops=flops, bytes_accessed=size, transcendentals=0),
        name=name,
    )(*args)


def local_wide(
    layout,
    tokens,
    memory,
    lengths,
    w_qkv,
    b_query,
    b_value,
    w_out,
    b_out,
    gain_one,
    shift_one,
    w_up,
    b_up,
    w_down,
    b_down,
    gain_two,
    shift_two,
    cot_tokens,
    cot_memory,
):
    mem_rows = memory.shape[1]
    tok_rows = tokens.shape[1]
    slot_len = tok_rows * layout.seq
    key_rows = slot_len + MEM_KEYS
    partner = layout.seq_bits - 1
    slot = lax.axis_index("seq") // layout.group

    def pick(x, at):
        return lax.dynamic_index_in_dim(x, at, 0, False)

    arrived = layout.swap(pick(tokens, 1 - slot), partner)
    near, far = layout.gather_group(jnp.concatenate([pick(tokens, slot), arrived], 0)[None])

    vectors = jnp.stack(
        [b_query, b_value, b_out, gain_one, shift_one, b_down, gain_two, shift_two]
    )
    vectors = layout.join_low(vectors, 1)
    extra = jnp.concatenate(
        [
            jnp.pad(vectors, ((0, 0), (0, LANES - 16))),
            jnp.pad(layout.join_low(b_up, 0)[None], ((0, 7), (0, LANES - 64))),
        ],
        0,
    )
    first = jnp.concatenate([layout.join_low(w_qkv, 0), layout.join_low(w_out, 0), extra], 1)
    qkv_parts = layout.gather(first[None], GATHER_QKV)
    up_parts = layout.gather(layout.join_low(w_up, 0)[None], GATHER_UP)
    down_parts = layout.gather(layout.join_low(w_down, 0)[None], GATHER_DOWN)
    cot_arrived = layout.swap(pick(cot_tokens, 1 - slot), partner)
    pad_rows = ((0, 0), (0, MEM_PAD - mem_rows), (0, 0))
    memory_full = jnp.pad(memory, pad_rows)
    cot_memory_full = jnp.pad(cot_memory, pad_rows)

    qkv, attn, lse_col, vector_rows, up_bias = call(
        functools.partial(forward_kernel, layout, mem_rows, slot_len),
        "attention_forward",
        [
            ((key_rows, 3 * WIDTH), BF),
            ((OWN, WIDTH), F32),
            ((OWN, LANES), F32),
            ((8, WIDTH), F32),
            ((8, FF), F32),
        ],
        [((slot_len + MEM_PAD, WIDTH), BF), ((WIDTH, 3 * WIDTH), BF), ((WIDTH, LANES), BF)],
        (lengths, near, far, memory_full, *qkv_parts),
    )
    (
        pack,
        grad_mem,
        lse_mem,
        delta_mem,
        delta_col,
        first_grad,
        out_own,
        out_send,
        attn_low,
        branch_low,
        hidden_low,
        grad_linear,
        active,
        feed_low,
        vector_grads,
        up_grads,
    ) = call(
        functools.partial(feed_kernel, layout, mem_rows),
        "feed_forward",
        [
            ((1, ROWS + 16, WIDTH), BF),
            ((MEM_PAD, WIDTH), BF),
            ((8, LANES), F32),
            ((8, LANES), F32),
            ((OWN, LANES), F32),
            ((OWN, WIDTH), F32),
            ((64 + MEM_PAD, WIDTH), BF),
            ((64 + MEM_PAD, WIDTH), BF),
            ((OWN, WIDTH), BF),
            ((OWN, WIDTH), BF),
            ((OWN, WIDTH), BF),
            ((OWN, FF), BF),
            ((OWN, FF), BF),
            ((OWN, WIDTH), BF),
            ((8, WIDTH), F32),
            ((8, FF), F32),
        ],
        [((WIDTH, WIDTH), BF), ((WIDTH, FF), BF), ((FF, WIDTH), BF), ((OWN, FF), F32)],
        (
            lengths,
            tokens,
            arrived,
            memory_full,
            cot_tokens,
            cot_arrived,
            cot_memory_full,
            attn,
            lse_col,
            vector_rows,
            up_bias,
            *qkv_parts,
            *up_parts,
            *down_parts,
        ),
    )
    grads_near, grads_far = layout.gather_group(pack)
    out_got = layout.swap(out_send, partner)
    half = BLOCKS // 2
    up_keep, up_send, down_keep, down_send = call(
        functools.partial(weight_kernel, layout),
        "weight_gradients",
        [
            ((half, 16, FF), BF),
            ((half, 16, FF), BF),
            ((half, 80, WIDTH), BF),
            ((half, 80, WIDTH), BF),
        ],
        [((WIDTH, FF), BF), ((FF, WIDTH), BF), ((WIDTH, WIDTH), BF)],
        (attn_low, branch_low, hidden_low, grad_linear, active, feed_low),
        smem=0,
    )
    up_total = layout.reduce(up_keep, up_send, REDUCE_UP, fold_plain)
    down_total = layout.reduce(down_keep, down_send, REDUCE_DOWN, fold_plain)
    qkv_keep, qkv_send, grad_own, grad_send = call(
        functools.partial(backward_kernel, layout, mem_rows, slot_len),
        "attention_backward",
        [
            ((half, 16, 3 * WIDTH + LANES), BF),
            ((half, 16, 3 * WIDTH + LANES), BF),
            ((112, WIDTH), BF),
            ((112, WIDTH), BF),
        ],
        [
            ((WIDTH, 3 * WIDTH), BF),
            ((key_rows, WIDTH), BF),
            ((8, key_rows), F32),
            ((8, key_rows), F32),
            ((layout.group, 8, LANES), F32),
            ((OWN, 3 * WIDTH), BF),
            ((WIDTH, 3 * WIDTH), BF),
            ((WIDTH, LANES), BF),
        ],
        (
            lengths,
            tokens,
            arrived,
            memory_full,
            qkv,
            grads_near,
            grads_far,
            grad_mem,
            lse_mem,
            delta_mem,
            lse_col,
            delta_col,
            first_grad,
            vector_grads,
            up_grads,
            *qkv_parts,
        ),
    )
    qkv_total = layout.reduce(qkv_keep, qkv_send, REDUCE_QKV, fold_with_extra)
    grad_got = layout.swap(grad_send, partner)

    def add(pair):
        return high(pair[0][0]) + high(pair[1][0])

    up_sum = layout.reduce_low(add(up_total), 0)
    down_sum = add(down_total)
    out_sum = layout.reduce_low(down_sum[64:], 0)
    down_sum = layout.reduce_low(down_sum[:64], 0)
    qkv_sum = add(qkv_total)
    extra_sum = qkv_sum[:, 3 * WIDTH :]
    qkv_sum = layout.reduce_low(qkv_sum[:, : 3 * WIDTH], 0)
    vec = layout.reduce_low(extra_sum[:8, :16] + extra_sum[:8, 64:80], 1)
    up_vec = layout.reduce_low(extra_sum[8, :64] + extra_sum[8, 64:], 0)

    out_tokens, out_memory, grad_tokens, grad_memory, rms = call(
        functools.partial(emit_kernel, layout, mem_rows),
        "emit",
        [
            (tokens.shape, BF),
            (memory.shape, BF),
            (tokens.shape, BF),
            (memory.shape, BF),
            ((2, WIDTH), F32),
        ],
        [],
        (lengths, out_own, out_got, grad_own, grad_got),
    )
    return (
        out_tokens,
        out_memory,
        grad_tokens,
        grad_memory,
        qkv_sum,
        vec[0],
        vec[1],
        out_sum,
        vec[2],
        vec[3],
        vec[4],
        up_sum,
        up_vec,
        down_sum,
        vec[5],
        vec[6],
        vec[7],
        rms,
    )


FIRST = 4 * WIDTH + LANES


def prepare_kernel(layout, *refs):
    tokens, w_qkv, w_out = refs[:3]
    vectors, b_up = refs[3:11], refs[11]
    own, give = refs[12:14]
    up_cell, sems = refs[14:16]
    cells = refs[16:]
    slot = lax.axis_index("seq") // layout.group
    moves = [(b_up, up_cell)]
    for target in (own, give):
        moves.append((w_qkv, target.at[:, : 3 * WIDTH]))
        moves.append((w_out, target.at[:, 3 * WIDTH : 4 * WIDTH]))
    for k in range(4):
        rows = slice(16 * k, 16 * k + 16)
        lanes = slice(FIRST + k * WIDTH, FIRST + (k + 1) * WIDTH)
        moves.append((tokens.at[slot, rows], own.at[:, lanes]))
        moves.append((tokens.at[1 - slot, rows], give.at[:, lanes]))
    moves += [(v, cells[k]) for k, v in enumerate(vectors)]
    copies = [
        pltpu.make_async_copy(source, target, sems.at[k])
        for k, (source, target) in enumerate(moves)
    ]
    for copy in copies:
        copy.start()
    for copy in copies:
        copy.wait()
    blank = jnp.zeros((1, LANES - 16), F32)
    rows = [jnp.concatenate([high(v[...]).reshape(1, 16), blank], 1) for v in cells]
    rows.append(jnp.concatenate([high(up_cell[...]).reshape(1, 64), blank[:, :64]], 1))
    rows.append(jnp.zeros((7, LANES), F32))
    extra = low(jnp.concatenate(rows, 0))
    own[:, 4 * WIDTH : FIRST] = extra
    give[:, 4 * WIDTH : FIRST] = extra


def stacked_rows(value):
    return jnp.concatenate([value[:, k * WIDTH : (k + 1) * WIDTH] for k in range(4)], 0)


def gather_vectors(extra):
    pieces, ups = [], []
    for g in range(4):
        total = jnp.zeros((8, LANES), F32)
        for p in range(8):
            at = (8 * g + p) * 16
            total += roll_lanes(high(extra[at : at + 16, :])[:8], 16 * p)
        pieces.append(total)
    for g in range(16):
        total = jnp.zeros((8, LANES), F32)
        for p in range(2):
            at = (2 * g + p) * 16
            total += roll_lanes(high(extra[at : at + 16, :])[8:], 64 * p)
        ups.append(total)
    return jnp.concatenate(pieces, 1), jnp.concatenate(ups, 1)


def quad_forward_kernel(layout, mem_rows, slot_len, *refs):
    lengths, near, far, memory, w0, w1, w2, w3 = refs[:8]
    attn, qkv_own, rows, w_own, vectors, up_bias = refs[8:14]
    qkv, weight, extra = refs[14:]
    group = layout.group
    place = lax.axis_index("seq")
    slot, rank = place // group, place % group
    block = layout.block()
    length = lengths[slot]
    parts = (w0, w1, w2, w3)
    place_blocks(weight, parts, GATHER_QKV, block, 16, slice(0, 3 * WIDTH))
    place_blocks(extra, parts, GATHER_QKV, block, 16, slice(4 * WIDTH, FIRST))
    for part, start, masks in zip((near, far), (FIRST, 0), layout.group_masks()):
        for k, mask in enumerate(masks):
            for part_half in range(2):
                at = aligned((rank ^ mask) * 2 + part_half, 64)
                rows[at, :] = stacked_rows(part[2 * k + part_half, :, start:])
    rows[slot_len : slot_len + MEM_PAD, :] = memory[...]
    vector_rows, up_rows = gather_vectors(extra)
    vectors[...] = vector_rows
    up_bias[...] = up_rows

    key_rows = slot_len + MEM_KEYS
    filled = slot_len + MEM_PAD
    qkv[filled:key_rows, :] = jnp.zeros((key_rows - filled, 3 * WIDTH), BF)
    for part, shift in enumerate((vector_rows[0:1], None, vector_rows[1:2])):
        lanes = slice(part * WIDTH, (part + 1) * WIDTH)
        value = dot(rows[...], weight[:, lanes])
        qkv[:filled, lanes] = low(value if shift is None else value + shift)
    half = WIDTH // 2
    for part in range(3):
        own = aligned(2 * part + place % 2, half)
        qkv_own[:, part * half : (part + 1) * half] = qkv[:, own]
        w_own[:, part * half : (part + 1) * half] = weight[:, own]

    keep = key_valid((1, key_rows), 1, slot, group, length, slot_len, mem_rows)
    bias = jnp.where(keep, 0.0, -1e30)
    for pair in range(HEADS // 2):
        at = pair * LANES
        own = jnp.concatenate(
            [qkv[aligned(rank, ROWS), at : at + LANES], qkv[slot_len:filled, at : at + LANES]], 0
        )
        keys = qkv[:, WIDTH + at : WIDTH + at + LANES]
        values = qkv[:, 2 * WIDTH + at : 2 * WIDTH + at + LANES]
        scores = dot(both_heads(own, 0.125), keys, NT) + bias
        highest = jnp.max(scores, axis=1, keepdims=True)
        expos = jnp.exp(scores - highest)
        total = jnp.sum(expos, axis=1, keepdims=True)
        attn[:, at : at + LANES] = join_heads(dot(low(expos), values) / total)


PACK = 32

ACT_LANES = FF + 2 * WIDTH + WIDTH // 2
LINEAR_LANES = FF // 2 + WIDTH // 2


def hand_out(core, own, give, value, start):
    half = value.shape[1] // 2
    first, second = value[:, :half], value[:, half:]
    mine = core == 0
    own[:, start : start + half] = jnp.where(mine, first, second)
    give[:, start : start + half] = jnp.where(mine, second, first)


def row_weights(group):
    row = lax.broadcasted_iota(jnp.int32, (OWN, 1), 0)
    return jnp.where(row < ROWS, 1.0, 1.0 / group)


def quad_feed_kernel(layout, mem_rows, *refs):
    lengths, tokens, arrived, memory, cots, cot_arrived, cot_memory = refs[:7]
    attn, vectors, up_bias = refs[7:10]
    outs, ups, downs = refs[10:14], refs[14:18], refs[18:22]
    out_own, out_send, own, give, sums, squares_out, w_heads = refs[22:29]
    w_out, w_up, w_down, slope, second_out, normed_out, inverse_out = refs[29:]
    group = layout.group
    place = lax.axis_index("seq")
    slot, rank = place // group, place % group
    block = layout.block()
    length = lengths[slot]
    place_blocks(w_out, outs, GATHER_QKV, block, 16, slice(3 * WIDTH, 4 * WIDTH))
    place_blocks(w_up, ups, GATHER_UP, block, 16, slice(0, FF))
    place_blocks(w_down, downs, GATHER_DOWN, block, 64, slice(0, WIDTH))
    w_heads[...] = w_out[aligned(place % 2, WIDTH // 2), :]

    vec = vectors[...]
    out_bias, gain_one, shift_one, down_bias, gain_two, shift_two = [
        vec[k : k + 1] for k in range(2, 8)
    ]
    got = high(stacked_rows(arrived[...]))
    rows = jnp.concatenate([high(tokens[slot]), got, high(memory[...])], 0)
    cot = jnp.concatenate([high(cots[slot]), high(cot_arrived[...]), high(cot_memory[...])], 0)
    valid = jnp.where(own_valid((OWN, 1), slot, group, rank, length, mem_rows), 1.0, 0.0)
    weight = row_weights(group)

    def total(v):
        return jnp.sum(v * weight, axis=0, keepdims=True)

    heads_out = low(attn[...])
    branch = dot(heads_out, w_out[...]) + out_bias
    normed_one, inverse_one = normalize(rows + branch)
    normed_out[...] = normed_one
    inverse_out[...] = jnp.broadcast_to(inverse_one, (OWN, LANES))
    hidden_one = normed_one * gain_one + shift_one
    hidden_low = low(hidden_one)
    for target in (own, give):
        target[:, FF : FF + WIDTH] = hidden_low
        target[:, FF + WIDTH : FF + 2 * WIDTH] = heads_out
    feed = jnp.zeros((OWN, WIDTH), F32) + down_bias
    for at in range(0, FF, WIDTH):
        cols = slice(at, at + WIDTH)
        t = dot(hidden_low, w_up[:, cols]) + up_bias[0:1, cols]
        square = t * t
        bent = jnp.tanh(0.7978845608 * (t + 0.044715 * (square * t)))
        half = 0.5 * (1.0 + bent)
        slope[:, cols] = half + (0.5 * 0.7978845608) * t * (1.0 - bent * bent) * (
            1.0 + (3 * 0.044715) * square
        )
        act = low(t * half)
        own[:, cols] = act
        give[:, cols] = act
        feed += dot(act, w_down[cols, :])
    normed_two, inverse_two = normalize(hidden_one + feed)
    output = (normed_two * gain_two + shift_two) * valid
    out_own[:HEAD_DIM, :] = low(output[:HEAD_DIM])
    out_own[HEAD_DIM:, :] = low(output[ROWS:])
    out_send[...] = low(output[HEAD_DIM:])
    row = lax.broadcasted_iota(jnp.int32, (OWN, 1), 0)
    token_valid = jnp.where(row < ROWS, valid, 0.0)
    squares = jnp.sum(feed * feed * token_valid, axis=0, keepdims=True)
    squares_out[...] = low(
        jnp.concatenate([*split_three(squares), jnp.zeros((13, WIDTH), F32)], 0)
    )
    g = cot * valid
    second = norm_back(g * gain_two, normed_two, inverse_two)
    second_out[...] = second
    grad_feed = low(second)
    hand_out(place % 2, own, give, grad_feed * low(weight), FF + 2 * WIDTH)
    blank = jnp.zeros((5, WIDTH), F32)
    sums[...] = jnp.concatenate(
        [blank, total(high(grad_feed)), total(g * normed_two), total(g)], 0
    )


def quad_slope_kernel(layout, *refs):
    vectors, sums, squares, w_out, w_up, w_down, slope, second_in, normed_in, inverse_in = refs[:10]
    pack, grad_mem, first_grad, own, give, grad_linear = refs[10:]
    place = lax.axis_index("seq")
    core = place % 2
    weight = row_weights(layout.group)
    weight_low = low(weight)

    def total(v):
        return jnp.sum(v * weight, axis=0, keepdims=True)

    ups = []
    second = second_in[...]
    grad_feed = low(second)
    grad_hidden = second
    for at in range(0, FF, WIDTH):
        cols = slice(at, at + WIDTH)
        linear = low(dot(grad_feed, w_down[cols, :], NT) * slope[:, cols])
        grad_linear[:, cols] = linear * weight_low
        ups.append(total(high(linear)))
        grad_hidden += dot(linear, w_up[:, cols], NT)
    own[:, : FF // 2] = grad_linear[:, aligned(core, FF // 2)]
    give[:, : FF // 2] = grad_linear[:, aligned(1 - core, FF // 2)]
    normed_one = normed_in[...]
    gains = [total(grad_hidden * normed_one), total(grad_hidden)]
    first = norm_back(grad_hidden * vectors[3:4, :], normed_one, inverse_in[:, :1])
    first_grad[...] = first
    grad_branch = low(first)
    hand_out(core, own, give, grad_branch * weight_low, FF // 2)
    sizes = jnp.concatenate([total(high(grad_branch)), *gains, sums[5:8, :], *ups], 0)
    first, second, _ = split_three(sizes)
    blank = jnp.zeros((PACK - 23, WIDTH), F32)
    pack[0, :ROWS, :] = grad_branch[:ROWS]
    pack[0, ROWS:, :] = low(
        jnp.concatenate([high(squares[...])[:3], first, second, blank], 0)
    )
    grad_mem[...] = grad_branch[ROWS:]


MAIN_ROWS = 176
REST_ROWS = 112
FEED_ROWS = MAIN_ROWS + REST_ROWS


def quad_weight_kernel(layout, *refs):
    acts, got_acts, linear, got_linear = refs[:4]
    main, rest = refs[4:6], refs[6:8]
    up, down, out = refs[8:]
    core = lax.axis_index("seq") % 2
    pair = layout.block() >> 1
    half = WIDTH // 2

    def both(first, second, start, size):
        cols = slice(start, start + size)
        return jnp.concatenate([first[:, cols], second[:, cols]], 0)

    def emit(source, target, unit, start):
        orders = PAIR_MAIN if target is main else PAIR_REST
        at = slice(start, start + unit)
        emit_pairs(source, *target, orders, pair, core, unit, at)

    grad_feed = both(acts, got_acts, FF + 2 * WIDTH, half)
    for start in range(0, FF, WIDTH):
        act = both(acts, got_acts, start, WIDTH)
        down[start : start + WIDTH, :] = low(dot(act, grad_feed, TN))
    emit(down, main, 128, 0)
    hidden = both(acts, got_acts, FF, WIDTH)
    for start in range(0, FF // 2, WIDTH):
        up[:, start : start + WIDTH] = low(dot(hidden, both(linear, got_linear, start, WIDTH), TN))
    heads_out = both(acts, got_acts, FF + WIDTH, WIDTH)
    value = low(dot(heads_out, both(linear, got_linear, FF // 2, half), TN))
    for p in range(BLOCKS):
        out[p % 2, p // 2 * 16 : p // 2 * 16 + 16, :] = value[16 * p : 16 * p + 16]
    for k in range(4):
        target, start = (main, 128) if k == 0 else (rest, 32 * k - 32)
        emit(up.at[:, half * k : half * (k + 1)], target, 32, start)
    emit(out.at[0], main, 16, 160)
    emit(out.at[1], rest, 16, 96)


def quad_backward_kernel(layout, mem_rows, slot_len, *refs):
    lengths, qkv, rows, w_own, w_heads, near, far, grad_mem = refs[:8]
    keep_out, send_out, in_keep, in_send, tail = refs[8:13]
    grad_rows, sums, packed, grad_weight, extra = refs[13:]
    group = layout.group
    place = lax.axis_index("seq")
    slot, rank = place // group, place % group
    core = place % 2
    pair = layout.block() >> 1
    length = lengths[slot]
    filled = slot_len + MEM_PAD
    key_rows = slot_len + MEM_KEYS
    half = WIDTH // 2
    for part, masks in zip((near, far), layout.group_masks()):
        for k, mask in enumerate(masks):
            at = rank ^ mask
            grad_rows[aligned(at, ROWS), :] = part[k, :ROWS, :]
            sums[at] = high(part[k, ROWS:, :])
    grad_rows[slot_len:filled, :] = grad_mem[...]

    keep = key_valid((1, key_rows), 1, slot, group, length, slot_len, mem_rows)
    bias = jnp.where(keep, 0.0, -1e30)
    grad_attn = low(dot(grad_rows[...], w_heads[...], NT))
    for k in range(2):
        at = [slice(part * half + k * LANES, part * half + (k + 1) * LANES) for part in range(3)]
        queries, keys, values = qkv[:filled, at[0]], qkv[:, at[1]], qkv[:, at[2]]
        d_query = jnp.zeros((filled, LANES), F32)
        d_key = jnp.zeros((key_rows, LANES), F32)
        d_value = jnp.zeros((key_rows, LANES), F32)
        for mask in half_masks():
            query = queries * (mask * 0.125)
            grads = grad_attn[:, k * LANES : (k + 1) * LANES] * mask
            scores = dot(query, keys, NT) + bias
            expos = jnp.exp(scores - jnp.max(scores, axis=1, keepdims=True))
            weights = expos * (1.0 / jnp.sum(expos, axis=1, keepdims=True))
            weights_low = low(weights)
            slopes = dot(grads, values, NT)
            delta = jnp.sum(high(weights_low) * slopes, axis=1, keepdims=True)
            slopes = low(weights * (slopes - delta))
            d_query += dot(slopes, keys) * (high(mask) * 0.125)
            d_key += dot(slopes, query, TN)
            d_value += dot(weights_low, grads, TN)
        packed[:, at[0]] = low(d_query)
        packed[:, at[1]] = low(d_key[:filled])
        packed[:, at[2]] = low(d_value[:filled])

    def emit(source, unit, at):
        emit_pairs(source, keep_out, send_out, PAIR_QKV, pair, core, unit, at)

    for part in range(3):
        lanes = slice(part * half, (part + 1) * half)
        grad_weight[...] = low(dot(rows[...], packed[:, lanes], TN))
        emit(grad_weight, 32, slice(32 * part, 32 * part + 32))
    for target, at in ((in_keep, rank), (in_send, rank ^ 1)):
        target[:ROWS, :] = low(dot(packed[aligned(at, ROWS), :], w_own[...], NT))
    grad_in = low(dot(packed[slot_len:filled, :], w_own[...], NT))
    in_keep[ROWS:, :] = grad_in
    in_send[ROWS:, :] = grad_in

    total = sums[0]
    for k in range(1, group):
        total += sums[k]
    square = total[0:1] + total[1:2] + total[2:3]
    tail[...] = low(jnp.concatenate([*split_three(square), jnp.zeros((13, WIDTH), F32)], 0))
    sizes = total[3:13] + total[13:23]
    first_core = core == 0
    blank = jnp.zeros((1, half), F32)
    biases = []
    for part in (0, 2):
        value = packed[:, part * half : (part + 1) * half]
        value = jnp.sum(high(value), axis=0, keepdims=True)
        first, second = jnp.where(first_core, value, 0.0), jnp.where(first_core, 0.0, value)
        biases.append(jnp.concatenate([first, second], 1))
    vec = jnp.concatenate([*biases, sizes[:6]], 0)
    ups = jnp.concatenate([sizes[6:10], jnp.zeros((4, WIDTH), F32)], 0)
    lanes = lane_index((8, LANES))
    sublane = lax.broadcasted_iota(jnp.int32, (8, LANES), 0)
    for p in range(0, BLOCKS, 2):
        both = []
        for q in (p, p + 1):
            mine = core == q % 2
            g = q // 8
            columns = slice(g * LANES, (g + 1) * LANES)
            cell = roll_lanes(vec[:, columns], -16 * (q % 8))
            cell = jnp.where(sublane < 2, cell, jnp.where(mine, cell, 0.0))
            g = q % 8 // 2
            row = ups[q // 8 : q // 8 + 1, g * LANES : (g + 1) * LANES]
            row = jnp.broadcast_to(jnp.where(mine, row, 0.0), (8, LANES))
            up = jnp.zeros((8, LANES), F32)
            for k in range(4):
                up = jnp.where(sublane == k, roll_lanes(row, 16 - 64 * (q % 2) - 16 * k), up)
            both.append(jnp.where(lanes < 16, cell, jnp.where(lanes < 32, up, 0.0)))
        wide = jnp.concatenate(both, 1)
        extra[p * 8 : p * 8 + 16, :] = low(jnp.concatenate([wide, jnp.zeros_like(wide)], 0))
    emit(extra, 16, slice(96, 112))


def feed_rows(core):
    starts = [128, *(MAIN_ROWS + 32 * k for k in range(3))]
    at = [pl.ds(pl.multiple_of(start + 16 * core, 16), 16) for start in starts]
    at.append(pl.ds(pl.multiple_of(64 * core, 64), 64))
    at.append(pl.ds(pl.multiple_of(160 + 112 * core, 16), 16))
    return at


def qkv_rows(core):
    return [pl.ds(pl.multiple_of(FEED_ROWS + 32 * k + 16 * core, 16), 16) for k in range(3)]


EXTRA_ROWS = pl.ds(FEED_ROWS + 96, 16)


def turn_kernel(keep, other, send):
    start = 0
    core = 1 - lax.axis_index("seq") % 2
    for at in [*feed_rows(core), *qkv_rows(core), EXTRA_ROWS]:
        send[start : start + at.size, :] = low(high(keep[0, at, :]) + high(other[0, at, :]))
        start += at.size


def emit_kernel_quad(keep, other, got, w_up, w_down, w_out, w_qkv, *vectors):
    core = lax.axis_index("seq") % 2
    half = WIDTH // 2
    start = 0
    places = [*feed_rows(core), *qkv_rows(core), EXTRA_ROWS]
    for k, at in enumerate(places):
        total = high(keep[0, at, :]) + high(other[0, at, :])
        arrived = high(got[start : start + at.size, :])
        start += at.size
        if k < 4:
            target, own, theirs = w_up, 4 * core + k, 4 - 4 * core + k
        elif k < 6:
            target, own, theirs = (w_down, w_out)[k - 4], core, 1 - core
        elif k < 9:
            target, own, theirs = w_qkv, 2 * k - 12 + core, 2 * k - 11 - core
        else:
            total += arrived
            continue
        target[:, aligned(own, half)] = total
        target[:, aligned(theirs, half)] = arrived
    total = jnp.where(core == 0, total[:8, :LANES], total[:8, LANES:])
    for k in range(8):
        vectors[k][...] = total[k, :16]
    lanes = lane_index((1, LANES))
    ups = jnp.zeros((1, LANES), F32)
    for k in range(4):
        rolled = roll_lanes(total[k : k + 1], 16 * k - 16)
        ups = jnp.where(jnp.logical_and(lanes >= 16 * k, lanes < 16 * k + 16), rolled, ups)
    vectors[8][...] = ups[0, :64]


def emit_tokens_kernel(layout, *refs):
    lengths, out_own, grad_own, grad_got, tail = refs[:5]
    out_tokens, out_memory, grad_tokens, grad_memory, rms = refs[5:]
    slot = lax.axis_index("seq") // layout.group
    pieces = (
        (out_own, 0, 64, slot, out_tokens, out_memory),
        (grad_got, 112, 176, 1 - slot, out_tokens, out_memory),
        (grad_own, 0, 128, slot, grad_tokens, grad_memory),
        (grad_got, 0, 64, 1 - slot, grad_tokens, grad_memory),
    )
    cells = [[None, None], [None, None]]
    for k, (source, start, mem, at, tokens, _) in enumerate(pieces):
        tokens[at] = source[start : start + 64, :]
        cells[k // 2][k % 2] = high(source[mem : mem + 32, :])
    for (own, got), memory in zip(cells, (out_memory, grad_memory)):
        first = jnp.where(slot == 0, own, got)
        second = jnp.where(slot == 0, got, own)
        rows = memory.shape[0]
        memory[...] = low(jnp.stack([first[:rows], second[:rows]], 1))
    result = []
    for cell, at in ((tail[...], slot), (grad_got[96:112, :], 1 - slot)):
        cell = high(cell)
        square = cell[0:1] + cell[1:2] + cell[2:3]
        result.append(jnp.sqrt(square / lengths[at].astype(F32)))
    row = lax.broadcasted_iota(jnp.int32, (2, WIDTH), 0)
    rms[...] = jnp.where(row == slot, result[0], result[1])


def local_quad(
    layout,
    tokens,
    memory,
    lengths,
    w_qkv,
    b_query,
    b_value,
    w_out,
    b_out,
    gain_one,
    shift_one,
    w_up,
    b_up,
    w_down,
    b_down,
    gain_two,
    shift_two,
    cot_tokens,
    cot_memory,
):
    mem_rows = memory.shape[1]
    slot_len = tokens.shape[1] * layout.seq
    key_rows = slot_len + MEM_KEYS
    filled = slot_len + MEM_PAD
    partner = layout.seq_bits - 1
    slot = lax.axis_index("seq") // layout.group

    def pick(x, at):
        return lax.dynamic_index_in_dim(x, at, 0, False)

    small = (b_query, b_value, b_out, gain_one, shift_one, b_down, gain_two, shift_two)
    own, give = pl.pallas_call(
        functools.partial(prepare_kernel, layout),
        out_shape=[jax.ShapeDtypeStruct((16, FIRST + FF), BF)] * 2,
        in_specs=[pl.BlockSpec(memory_space=pl.ANY)] * 12,
        out_specs=[pl.BlockSpec(memory_space=pltpu.VMEM)] * 2,
        scratch_shapes=[pltpu.VMEM((64,), BF), pltpu.SemaphoreType.DMA((21,))]
        + [pltpu.VMEM((16,), BF)] * 8,
        name="prepare",
    )(tokens, w_qkv, w_out, *small, b_up)

    def after(x, *others):
        return lax.optimization_barrier((x, *others))[0]

    def doubled(held, bit):
        return jnp.concatenate([held, layout.block_swap(held, bit)], 0)

    def finish(held, order, *ready):
        last = after(layout.block_swap(held, order[3]), *ready)
        return held, last, layout.block_swap(held, 0), layout.block_swap(last, 0)

    second = doubled(w_up[None], GATHER_UP[0])
    third = doubled(w_down[None], GATHER_DOWN[0])
    got = layout.swap(give, partner)[None]
    arrived = got[0, :, FIRST:]
    near = doubled(jnp.concatenate([own[None], got], 0), GATHER_QKV[1])
    far = layout.swap(near[:, :, FIRST:], 0)
    first = doubled(near[:, :, :FIRST], GATHER_QKV[2])
    second = doubled(doubled(second, GATHER_UP[1]), GATHER_UP[2])
    third = doubled(doubled(third, GATHER_DOWN[1]), GATHER_DOWN[2])
    cot_arrived = layout.swap(pick(after(cot_tokens, first), 1 - slot), partner)
    pad_rows = ((0, MEM_PAD - mem_rows), (0, 0))
    own_memory = jnp.pad(pick(memory, slot), pad_rows)
    own_cot_memory = jnp.pad(pick(cot_memory, slot), pad_rows)
    qkv_parts = finish(first, GATHER_QKV, cot_arrived)
    up_parts = finish(second, GATHER_UP)
    down_parts = finish(third, GATHER_DOWN)

    attn, qkv_own, rows, w_own, vector_rows, up_bias = call(
        functools.partial(quad_forward_kernel, layout, mem_rows, slot_len),
        "attention_forward",
        [
            ((OWN, WIDTH), F32),
            ((key_rows, 3 * WIDTH // 2), BF),
            ((filled, WIDTH), BF),
            ((WIDTH, 3 * WIDTH // 2), BF),
            ((8, WIDTH), F32),
            ((8, FF), F32),
        ],
        [((key_rows, 3 * WIDTH), BF), ((WIDTH, 3 * WIDTH), BF), ((WIDTH, LANES), BF)],
        (lengths, near, far, own_memory, *qkv_parts),
        flops=4 * 10**9,
    )
    (
        out_own,
        out_send,
        acts,
        acts_give,
        sums,
        squares,
        w_heads,
        w_out_all,
        w_up_all,
        w_down_all,
        slope,
        second_grad,
        normed_one,
        inverse_one,
    ) = call(
        functools.partial(quad_feed_kernel, layout, mem_rows),
        "feed_forward",
        [
            ((64 + MEM_PAD, WIDTH), BF),
            ((64 + MEM_PAD, WIDTH), BF),
            ((OWN, ACT_LANES), BF),
            ((OWN, ACT_LANES), BF),
            ((8, WIDTH), F32),
            ((16, WIDTH), BF),
            ((WIDTH // 2, WIDTH), BF),
            ((WIDTH, WIDTH), BF),
            ((WIDTH, FF), BF),
            ((FF, WIDTH), BF),
            ((OWN, FF), F32),
            ((OWN, WIDTH), F32),
            ((OWN, WIDTH), F32),
            ((OWN, LANES), F32),
        ],
        [],
        (
            lengths,
            tokens,
            arrived,
            own_memory,
            cot_tokens,
            cot_arrived,
            own_cot_memory,
            attn,
            vector_rows,
            up_bias,
            *qkv_parts,
            *up_parts,
            *down_parts,
        ),
        flops=3 * 10**9,
    )
    acts_got = layout.swap(acts_give, 0)
    pack, grad_mem, first_grad, linear, linear_give = call(
        functools.partial(quad_slope_kernel, layout),
        "feed_backward",
        [
            ((1, ROWS + PACK, WIDTH), BF),
            ((MEM_PAD, WIDTH), BF),
            ((OWN, WIDTH), F32),
            ((OWN, LINEAR_LANES), BF),
            ((OWN, LINEAR_LANES), BF),
        ],
        [((OWN, FF), BF)],
        (
            vector_rows,
            sums,
            squares,
            w_out_all,
            w_up_all,
            w_down_all,
            slope,
            second_grad,
            normed_one,
            inverse_one,
        ),
        smem=0,
        flops=3 * 10**9,
    )
    linear_got = layout.swap(linear_give, 0)
    grads_next = layout.swap(pack, 1)
    half = PAIRS // 2
    main_keep, main_send, rest_keep, rest_send = call(
        functools.partial(quad_weight_kernel, layout),
        "weight_gradients",
        [((half, MAIN_ROWS, WIDTH // 2), BF)] * 2 + [((half, REST_ROWS, WIDTH // 2), BF)] * 2,
        [((WIDTH, FF // 2), BF), ((FF, WIDTH // 2), BF), ((2, WIDTH // 2, WIDTH // 2), BF)],
        (acts, after(acts_got, pack), linear, linear_got),
        smem=0,
        flops=10**9,
    )
    grads_next = after(grads_next, main_send)
    grads_near = jnp.concatenate([pack, grads_next], 0)
    grads_far = layout.swap(grads_near, 0)
    qkv_keep, qkv_send, in_keep, in_send, tail = call(
        functools.partial(quad_backward_kernel, layout, mem_rows, slot_len),
        "attention_backward",
        [
            ((half // 2, 112, WIDTH // 2), BF),
            ((half // 2, 112, WIDTH // 2), BF),
            ((OWN, WIDTH), BF),
            ((OWN, WIDTH), BF),
            ((16, WIDTH), BF),
        ],
        [
            ((filled, WIDTH), BF),
            ((layout.group, PACK, WIDTH), F32),
            ((filled, 3 * WIDTH // 2), BF),
            ((WIDTH, WIDTH // 2), BF),
            ((8 * BLOCKS, WIDTH // 2), BF),
        ],
        (lengths, qkv_own, rows, w_own, w_heads, grads_near, grads_far, grad_mem),
        flops=0,
    )
    swap = layout.pair_swap_by_core

    def bits(orders, step):
        return tuple(order[step] for order in orders)

    main_other = swap(main_send, bits(PAIR_MAIN, 0))
    rest_other = swap(rest_send, bits(PAIR_REST, 0))
    main_keep, main_send = fold_plain(main_keep, main_other)
    rest_keep, rest_send = fold_plain(rest_keep, rest_other)
    qkv_send = after(qkv_send, main_send, rest_send)
    both_send = jnp.concatenate([main_send, rest_send, qkv_send], 1)
    both_other = swap(both_send, bits(PAIR_QKV, 0))
    main_keep, main_send = fold_plain(main_keep, both_other[:, :MAIN_ROWS])
    both_keep = jnp.concatenate([rest_keep, qkv_keep], 1)
    both_keep, both_send = fold_plain(both_keep, both_other[:, MAIN_ROWS:])
    second_ready = both_send
    main_other = swap(main_send, bits(PAIR_MAIN, 2))
    both_other = swap(both_send, bits(PAIR_QKV, 1))
    main_keep, main_send = fold_plain(main_keep, main_other)
    both_keep, both_send = fold_plain(both_keep, both_other)
    all_keep = jnp.concatenate([main_keep, both_keep], 1)
    all_send = jnp.concatenate([main_send, both_send], 1)

    in_got = layout.swap(in_send, 0)
    grad_own = low(high(in_keep) + high(in_got) + first_grad)
    grad_got = layout.swap(jnp.concatenate([grad_own[64:], tail, out_send], 0), partner)
    grad_got = after(grad_got, all_send)

    out_tokens, out_memory, grad_tokens, grad_memory, rms = call(
        functools.partial(emit_tokens_kernel, layout),
        "emit_tokens",
        [
            (tokens.shape, BF),
            ((mem_rows, 2, WIDTH), BF),
            (tokens.shape, BF),
            ((mem_rows, 2, WIDTH), BF),
            ((2, WIDTH), F32),
        ],
        [],
        (lengths, out_own, grad_own, grad_got, tail),
    )
    all_other = swap(all_send, bits(PAIR_MAIN, 3))
    order = (1, 0, 2)
    all_other, out_memory, grad_memory, rms = lax.optimization_barrier(
        (all_other, out_memory, grad_memory, rms)
    )
    out_memory, grad_memory = jnp.transpose(out_memory, order), jnp.transpose(grad_memory, order)
    (turned,) = call(
        turn_kernel, "turn", [((208, WIDTH // 2), BF)], [], (all_keep, all_other), smem=0
    )
    turned = layout.swap(turned, 0)
    up_sum, down_sum, out_sum, qkv_sum, *vec = call(
        emit_kernel_quad,
        "emit_weights",
        [(w_up.shape, F32), (w_down.shape, F32), (w_out.shape, F32), (w_qkv.shape, F32)]
        + [((16,), F32)] * 8
        + [((64,), F32)],
        [],
        (all_keep, all_other, turned),
        smem=0,
    )
    return (
        out_tokens,
        out_memory,
        grad_tokens,
        grad_memory,
        qkv_sum,
        vec[0],
        vec[1],
        out_sum,
        vec[2],
        vec[3],
        vec[4],
        up_sum,
        vec[8],
        down_sum,
        vec[5],
        vec[6],
        vec[7],
        rms,
    )


def solution(mesh):
    rows = P("dp", "seq", None)
    slots = P("dp", None, None)
    matrix = P(("dp", "seq"), None)
    vector = P(("dp", "seq"))
    weights = (
        matrix,
        vector,
        vector,
        matrix,
        vector,
        vector,
        vector,
        matrix,
        vector,
        matrix,
        vector,
        vector,
        vector,
    )
    layout = Layout(mesh)
    quad = layout.group == 4 and layout.devices == BLOCKS
    return jax.shard_map(
        functools.partial(local_quad if quad else local_wide, layout),
        mesh=mesh,
        in_specs=(rows, slots, P("dp"), *weights, rows, slots),
        out_specs=(rows, slots, rows, slots, *weights, P("dp", None)),
        check_vma=False,
    )
```

```python
import functools

import jax
import jax.numpy as jnp
from jax import lax
from jax.experimental import pallas as pl
from jax.experimental.pallas import tpu as pltpu
from jax.sharding import PartitionSpec as P

HEADS = 8
HEAD_DIM = 64
WIDTH = 512
FF = 2048
BLOCKS = 32
ROWS = 128
MEM_PAD = 32
OWN = ROWS + MEM_PAD
MEM_KEYS = 128
LANES = 128
MIB = 1 << 20

BF = jnp.bfloat16
F32 = jnp.float32
NN = (((1,), (0,)), ((), ()))
NT = (((1,), (1,)), ((), ()))
TN = (((0,), (0,)), ((), ()))

GATHER_QKV = (2, 1, 4, 3, 0)
GATHER_UP = (2, 3, 1, 4, 0)
GATHER_DOWN = (2, 4, 3, 1, 0)
REDUCE_UP = (0, 1, 4, 3, 2)
REDUCE_DOWN = (0, 3, 1, 4, 2)
REDUCE_QKV = (0, 4, 3, 1, 2)
PAIRS = BLOCKS // 2
PAIR_MAIN = ((2, 3, 0, 1), (3, 2, 0, 1))
PAIR_REST = ((0, 3, 2, 1), (0, 2, 3, 1))
PAIR_QKV = ((3, 2, 1), (2, 3, 1))


def dot(a, b, dims=NN):
    return lax.dot_general(a, b, dims, preferred_element_type=F32)


def low(v):
    return v.astype(BF)


def high(v):
    return v.astype(F32)


def split_three(v):
    first = high(low(v))
    second = high(low(v - first))
    return first, second, high(low(v - first - second))


def aligned(index, size):
    return pl.ds(pl.multiple_of(index * size, size), size)


class Layout:
    def __init__(self, mesh):
        self.dp = mesh.shape["dp"]
        self.seq = mesh.shape["seq"]
        self.devices = self.dp * self.seq
        self.low_bits = (self.devices // BLOCKS).bit_length() - 1
        self.group = self.seq // 2
        self.seq_bits = self.seq.bit_length() - 1

    def dim(self, bit):
        if bit < self.seq_bits:
            return "seq", 1 << bit
        return "dp", 1 << (bit - self.seq_bits)

    def swap(self, x, bit):
        axis, mask = self.dim(bit)
        size = self.seq if axis == "seq" else self.dp
        return lax.ppermute(x, axis, [(i, i ^ mask) for i in range(size)])

    def block_swap(self, x, bit):
        return self.swap(x, bit + self.low_bits)

    def pair_swap(self, x, bit):
        return self.swap(x, bit + 1)

    def pair_swap_by_core(self, x, bits):
        pairs = [(i, i ^ (2 << bits[i % 2])) for i in range(self.devices)]
        return lax.ppermute(x, ("dp", "seq"), pairs)

    def device(self):
        return lax.axis_index("dp") * self.seq + lax.axis_index("seq")

    def block(self):
        return self.device() >> self.low_bits

    def join_low(self, x, axis):
        for bit in range(self.low_bits):
            other = self.swap(x, bit)
            first = (self.device() >> bit) % 2 == 0
            x = jnp.where(
                first, jnp.concatenate([x, other], axis), jnp.concatenate([other, x], axis)
            )
        return x

    def reduce_low(self, x, axis):
        for bit in reversed(range(self.low_bits)):
            first = (self.device() >> bit) % 2 == 0
            lower, upper = jnp.split(x, 2, axis)
            other = self.swap(jnp.where(first, upper, lower), bit)
            x = jnp.where(first, lower, upper) + other
        return x

    def gather(self, x, order):
        held = x
        for bit in order[:3]:
            held = jnp.concatenate([held, self.block_swap(held, bit)], 0)
        last = self.block_swap(held, order[3])
        return held, last, self.block_swap(held, order[4]), self.block_swap(last, order[4])

    def reduce(self, keep, send, order, fold, swap=None):
        swap = swap or self.block_swap
        other = swap(send, order[0])
        for bit in order[1:]:
            keep, send = fold(keep, other)
            other = swap(send, bit)
        return keep, other

    def gather_group(self, x):
        near = x
        mask = self.group // 2
        while mask > 1:
            near = jnp.concatenate([near, self.swap(near, mask.bit_length() - 1)], 0)
            mask //= 2
        return near, self.swap(near, 0)

    def group_masks(self):
        near = [0]
        mask = self.group // 2
        while mask > 1:
            near += [m ^ mask for m in near]
            mask //= 2
        return near, [m ^ 1 for m in near]


def gather_masks(order):
    held = [0]
    for bit in order[:3]:
        held = held + [m ^ (1 << bit) for m in held]
    last = [m ^ (1 << order[3]) for m in held]
    swapped = [[m ^ (1 << order[4]) for m in part] for part in (held, last)]
    return held, last, swapped[0], swapped[1]


def reduce_masks(order):
    bits = len(order)
    return [
        sum(((place >> (bits - 1 - k)) & 1) << bit for k, bit in enumerate(order))
        for place in range(1 << bits)
    ]


def place_blocks(target, parts, order, block, unit, lanes):
    for part, masks in zip(parts, gather_masks(order)):
        for place, mask in enumerate(masks):
            target[aligned(block ^ mask, unit), :] = part[place, :, lanes]


def emit_blocks(source, keep, send, order, block, unit, at, lanes):
    masks = reduce_masks(order)
    half = len(masks) // 2
    for place, mask in enumerate(masks):
        target = keep if place < half else send
        target[place % half, at, lanes] = source[aligned(block ^ mask, unit), :]


def emit_pairs(source, keep, send, orders, pair, core, unit, at):
    masks = [reduce_masks(order) for order in orders]
    count = len(masks[0]) // 2
    for spot, (first, second) in enumerate(zip(*masks)):
        target = keep if spot < count else send
        whose = pair ^ jnp.where(core == 0, first, second)
        target[spot % count, at, :] = source[aligned(whose, unit), :]


def roll_lanes(v, shift):
    return pltpu.roll(v, shift % LANES, 1) if shift % LANES else v


def lane_index(shape):
    return lax.broadcasted_iota(jnp.int32, shape, 1)


def normalize(hidden):
    center = hidden - jnp.mean(hidden, axis=-1, keepdims=True)
    inverse = lax.rsqrt(jnp.mean(center * center, axis=-1, keepdims=True) + 1e-05)
    return center * inverse, inverse


def norm_back(grad_normed, normed, inverse):
    mean_grad = jnp.mean(grad_normed, axis=-1, keepdims=True)
    mean_cross = jnp.mean(grad_normed * normed, axis=-1, keepdims=True)
    return inverse * (grad_normed - mean_grad - normed * mean_cross)


def half_masks():
    first = lane_index((1, LANES)) < HEAD_DIM
    return low(jnp.where(first, 1.0, 0.0)), low(jnp.where(first, 0.0, 1.0))


def both_heads(pair, scale=1.0):
    first, second = half_masks()
    return jnp.concatenate([pair * (first * scale), pair * (second * scale)], 0)


def join_heads(pair):
    half = pair.shape[0] // 2
    return jnp.where(lane_index((half, LANES)) < HEAD_DIM, pair[:half], pair[half:])


def head_column(columns, pair):
    lanes = lane_index(columns.shape)
    picked = [
        jnp.sum(jnp.where(lanes == 2 * pair + k, columns, 0.0), axis=1, keepdims=True)
        for k in range(2)
    ]
    return jnp.concatenate(picked, 0)


def key_valid(shape, axis, slot, group, length, slot_len, mem_rows):
    place = lax.broadcasted_iota(jnp.int32, shape, axis)
    half = (place >> 6) & 1
    position = ((half ^ slot) * group + (place >> 7)) * HEAD_DIM + (place & 63)
    token = jnp.logical_and(place < slot_len, position < length)
    mem = jnp.logical_and(place >= slot_len, place < slot_len + mem_rows)
    return jnp.logical_or(token, mem)


def own_valid(shape, slot, group, rank, length, mem_rows):
    place = lax.broadcasted_iota(jnp.int32, shape, 0)
    half = (place >> 6) & 1
    position = ((half ^ slot) * group + rank) * HEAD_DIM + (place & 63)
    token = jnp.logical_and(place < ROWS, position < length)
    mem = jnp.logical_and(place >= ROWS, place < ROWS + mem_rows)
    return jnp.logical_or(token, mem)


def forward_kernel(layout, mem_rows, slot_len, *refs):
    lengths, near, far, memory, w0, w1, w2, w3 = refs[:8]
    qkv, attn, lse_col, vectors, up_bias = refs[8:13]
    rows, weight, extra = refs[13:]
    group = layout.group
    place = lax.axis_index("seq")
    slot, rank = place // group, place % group
    block = layout.block()
    length = lengths[slot]
    parts = (w0, w1, w2, w3)
    place_blocks(weight, parts, GATHER_QKV, block, 16, slice(0, 3 * WIDTH))
    place_blocks(extra, parts, GATHER_QKV, block, 16, slice(4 * WIDTH, FIRST))
    for part, masks in zip((near, far), layout.group_masks()):
        for k, mask in enumerate(masks):
            rows[aligned(rank ^ mask, ROWS), :] = part[k]
    rows[slot_len : slot_len + MEM_PAD, :] = memory[slot]

    pieces, ups = [], []
    for g in range(4):
        total = jnp.zeros((8, LANES), F32)
        for p in range(8):
            total += roll_lanes(high(extra[(8 * g + p) * 16 : (8 * g + p + 1) * 16, :])[:8], 16 * p)
        pieces.append(total)
    for g in range(16):
        total = jnp.zeros((8, LANES), F32)
        for p in range(2):
            at = (2 * g + p) * 16
            total += roll_lanes(high(extra[at : at + 16, :])[8:], 64 * p)
        ups.append(total)
    vector_rows = jnp.concatenate(pieces, 1)
    vectors[...] = vector_rows
    up_bias[...] = jnp.concatenate(ups, 1)

    key_rows = slot_len + MEM_KEYS
    filled = slot_len + MEM_PAD
    qkv[filled:key_rows, :] = jnp.zeros((key_rows - filled, 3 * WIDTH), BF)
    shifts = (vector_rows[0:1], None, vector_rows[1:2])
    step = 544 if filled == 544 else 512
    for start in range(0, filled, step):
        size = min(step, filled - start)
        for part, shift in enumerate(shifts):
            lanes = slice(part * WIDTH, (part + 1) * WIDTH)
            value = dot(rows[start : start + size, :], weight[:, lanes])
            qkv[start : start + size, lanes] = low(value if shift is None else value + shift)

    keep = key_valid((1, key_rows), 1, slot, group, length, slot_len, mem_rows)
    bias = jnp.where(keep, 0.0, -1e30)
    log_columns = jnp.zeros((OWN, LANES), F32)
    for pair in range(HEADS // 2):
        at = pair * LANES
        own = jnp.concatenate(
            [qkv[aligned(rank, ROWS), at : at + LANES], qkv[slot_len:filled, at : at + LANES]], 0
        )
        keys = qkv[:, WIDTH + at : WIDTH + at + LANES]
        values = qkv[:, 2 * WIDTH + at : 2 * WIDTH + at + LANES]
        scores = dot(both_heads(own, 0.125), keys, NT) + bias
        highest = jnp.max(scores, axis=1, keepdims=True)
        expos = jnp.exp(scores - highest)
        total = jnp.sum(expos, axis=1, keepdims=True)
        attn[:, at : at + LANES] = join_heads(dot(low(expos), values) / total)
        log_total = highest + jnp.log(total)
        lanes = lane_index((OWN, LANES))
        log_columns = jnp.where(lanes == 2 * pair, log_total[:OWN], log_columns)
        log_columns = jnp.where(lanes == 2 * pair + 1, log_total[OWN:], log_columns)
    lse_col[...] = log_columns


def feed_kernel(layout, mem_rows, *refs):
    lengths, tokens, arrived, memory, cots, cot_arrived, cot_memory = refs[:7]
    attn, lse_col, vectors, up_bias = refs[7:11]
    outs, ups, downs = refs[11:15], refs[15:19], refs[19:23]
    pack, grad_mem, lse_mem, delta_mem, delta_col, first_grad, out_own, out_send = refs[23:31]
    attn_low, branch_low, hidden_low, grad_linear, active, feed_low, vector_grads, up_grads = refs[
        31:39
    ]
    w_out, w_up, w_down, slope = refs[39:]
    group = layout.group
    place = lax.axis_index("seq")
    slot, rank = place // group, place % group
    block = layout.block()
    length = lengths[slot]
    place_blocks(w_out, outs, GATHER_QKV, block, 16, slice(3 * WIDTH, 4 * WIDTH))
    place_blocks(w_up, ups, GATHER_UP, block, 16, slice(0, FF))
    place_blocks(w_down, downs, GATHER_DOWN, block, 64, slice(0, WIDTH))

    vec = vectors[...]
    out_bias, gain_one, shift_one, down_bias, gain_two, shift_two = [
        vec[k : k + 1] for k in range(2, 8)
    ]
    rows = jnp.concatenate([high(tokens[slot]), high(arrived[...]), high(memory[slot])], 0)
    cot = jnp.concatenate([high(cots[slot]), high(cot_arrived[...]), high(cot_memory[slot])], 0)
    valid = jnp.where(own_valid((OWN, 1), slot, group, rank, length, mem_rows), 1.0, 0.0)
    share = 1.0 / group
    row = lax.broadcasted_iota(jnp.int32, (OWN, 1), 0)
    weight = jnp.where(row < ROWS, 1.0, share)
    weight_low = low(weight)

    def total(v):
        return jnp.sum(v * weight, axis=0, keepdims=True)

    heads_out = attn[...]
    attn_low[...] = low(heads_out)
    branch = dot(attn_low[...], w_out[...]) + out_bias
    normed_one, inverse_one = normalize(rows + branch)
    hidden_one = normed_one * gain_one + shift_one
    hidden_low[...] = low(hidden_one)
    feed = jnp.zeros((OWN, WIDTH), F32) + down_bias
    for at in range(0, FF, WIDTH):
        cols = slice(at, at + WIDTH)
        t = dot(hidden_low[...], w_up[:, cols]) + up_bias[0:1, cols]
        square = t * t
        bent = jnp.tanh(0.7978845608 * (t + 0.044715 * (square * t)))
        half = 0.5 * (1.0 + bent)
        slope[:, cols] = half + (0.5 * 0.7978845608) * t * (1.0 - bent * bent) * (
            1.0 + (3 * 0.044715) * square
        )
        act = low(t * half)
        active[:, cols] = act
        feed += dot(act, w_down[cols, :])
    normed_two, inverse_two = normalize(hidden_one + feed)
    output = (normed_two * gain_two + shift_two) * valid
    out_own[:HEAD_DIM, :] = low(output[:HEAD_DIM])
    out_own[HEAD_DIM:, :] = low(output[ROWS:])
    out_send[...] = low(output[HEAD_DIM:])
    token_valid = jnp.where(row < ROWS, valid, 0.0)
    squares = jnp.sum(feed * feed * token_valid, axis=0, keepdims=True)

    g = cot * valid
    grads = [None] * 8
    grads[6] = total(g * normed_two)
    grads[7] = total(g)
    second = norm_back(g * gain_two, normed_two, inverse_two)
    grad_feed = low(second)
    feed_low[...] = grad_feed * weight_low
    grads[5] = total(high(grad_feed))
    grad_hidden = second
    for at in range(0, FF, WIDTH):
        cols = slice(at, at + WIDTH)
        linear = low(dot(grad_feed, w_down[cols, :], NT) * slope[:, cols])
        grad_linear[:, cols] = linear * weight_low
        up_grads[:, cols] = jnp.broadcast_to(total(high(linear)), (8, WIDTH))
        grad_hidden += dot(linear, w_up[:, cols], NT)
    grads[3] = total(grad_hidden * normed_one)
    grads[4] = total(grad_hidden)
    first = norm_back(grad_hidden * gain_one, normed_one, inverse_one)
    first_grad[...] = first
    grad_branch = low(first)
    branch_low[...] = grad_branch * weight_low
    grads[2] = total(high(grad_branch))
    grads[0] = grads[1] = jnp.zeros((1, WIDTH), F32)
    vector_grads[...] = jnp.concatenate(grads, 0)

    grad_attn = low(dot(grad_branch, w_out[...], NT))
    product = high(grad_attn) * heads_out
    chosen = lax.broadcasted_iota(jnp.int32, (16, WIDTH), 0)
    head = lax.broadcasted_iota(jnp.int32, (16, WIDTH), 1) // HEAD_DIM
    pick = low(jnp.where(chosen == head, 1.0, 0.0))
    down = lax.broadcasted_iota(jnp.int32, (WIDTH, LANES), 0) // HEAD_DIM
    pick_col = low(jnp.where(down == lane_index((WIDTH, LANES)), 1.0, 0.0))
    identity = low(
        jnp.where(
            lax.broadcasted_iota(jnp.int32, (16, LANES), 0) == lane_index((16, LANES)), 1.0, 0.0
        )
    )
    terms = [low(v) for v in split_three(product)]
    delta_col[...] = sum(dot(v, pick_col) for v in terms)
    delta_row = sum(dot(pick, v, NT) for v in terms)[:8]
    log_row = sum(dot(identity, low(v), NT) for v in split_three(lse_col[...]))[:8]
    log_terms = split_three(log_row[:, :ROWS])
    delta_terms = split_three(delta_row[:, :ROWS])
    square_terms = split_three(squares)
    square_rows = jnp.concatenate(
        [v[:, k * LANES : (k + 1) * LANES] for v in square_terms[:2] for k in range(4)], 0
    )
    pack[0, :ROWS, :] = grad_attn[:ROWS]
    pack[0, ROWS:, :] = low(
        jnp.concatenate(
            [
                jnp.concatenate([*log_terms, delta_terms[0]], 1),
                jnp.concatenate(
                    [delta_terms[1], delta_terms[2], square_rows, jnp.zeros((8, LANES), F32)], 1
                ),
            ],
            0,
        )
    )
    grad_mem[...] = grad_attn[ROWS:]
    blank = jnp.zeros((8, LANES - MEM_PAD), F32)
    lse_mem[...] = jnp.concatenate([log_row[:, ROWS:], blank], 1)
    delta_mem[...] = jnp.concatenate([delta_row[:, ROWS:], blank], 1)


def weight_kernel(layout, *refs):
    attn_low, branch_low, hidden_low, grad_linear, active, feed_low = refs[:6]
    up_keep, up_send, down_keep, down_send = refs[6:10]
    up, down, out = refs[10:]
    block = layout.block()
    for at in range(0, FF, WIDTH):
        cols = slice(at, at + WIDTH)
        down[cols, :] = low(dot(active[:, cols], feed_low[...], TN))
    out[...] = low(dot(attn_low[...], branch_low[...], TN))
    every = slice(0, WIDTH)
    emit_blocks(down, down_keep, down_send, REDUCE_DOWN, block, 64, slice(0, 64), every)
    emit_blocks(out, down_keep, down_send, REDUCE_DOWN, block, 16, slice(64, 80), every)
    for at in range(0, FF, WIDTH):
        cols = slice(at, at + WIDTH)
        up[:, cols] = low(dot(hidden_low[...], grad_linear[:, cols], TN))
    emit_blocks(up, up_keep, up_send, REDUCE_UP, block, 16, slice(0, 16), slice(0, FF))


def backward_kernel(layout, mem_rows, slot_len, *refs):
    lengths, tokens, arrived, memory, qkv, near, far, grad_mem, lse_mem, delta_mem = refs[:10]
    lse_col, delta_col, first_grad, vector_grads, up_grads = refs[10:15]
    parts = refs[15:19]
    keep_out, send_out, own_out, give_out = refs[19:23]
    weight, grad_rows, log_row, delta_row, squares, packed, grad_weight, extra = refs[23:]
    group = layout.group
    place = lax.axis_index("seq")
    slot, rank = place // group, place % group
    block = layout.block()
    length = lengths[slot]
    filled = slot_len + MEM_PAD
    key_rows = slot_len + MEM_KEYS
    place_blocks(weight, parts, GATHER_QKV, block, 16, slice(0, 3 * WIDTH))
    for part, masks in zip((near, far), layout.group_masks()):
        for k, mask in enumerate(masks):
            at = rank ^ mask
            grad_rows[aligned(at, ROWS), :] = part[k, :ROWS, :]
            more = high(part[k, ROWS:, :])
            cell = [[more[8 * a : 8 * a + 8, LANES * b : LANES * (b + 1)] for b in range(4)] for a in range(2)]
            log_row[:, aligned(at, LANES)] = cell[0][0] + cell[0][1] + cell[0][2]
            delta_row[:, aligned(at, LANES)] = cell[0][3] + cell[1][0] + cell[1][1]
            squares[at] = cell[1][2]
    grad_rows[slot_len:filled, :] = grad_mem[...]
    grad_rows[filled:, :] = jnp.zeros((key_rows - filled, WIDTH), BF)
    log_row[:, slot_len:] = lse_mem[...]
    delta_row[:, slot_len:] = delta_mem[...]

    own_keep = jnp.where(own_valid((OWN, 1), slot, group, rank, length, mem_rows), 0.0, -1e30)
    own_bias = jnp.concatenate([own_keep, own_keep], 0)
    chunk = min(slot_len, 512)
    spans = [(s, chunk) for s in range(0, slot_len, chunk)]
    spans[-1] = (spans[-1][0], chunk + MEM_KEYS)

    def own_rows(ref, lanes):
        return jnp.concatenate([ref[aligned(rank, ROWS), lanes], ref[slot_len:filled, lanes]], 0)

    for pair in range(HEADS // 2):
        at = pair * LANES
        q_lanes = slice(at, at + LANES)
        k_lanes = slice(WIDTH + at, WIDTH + at + LANES)
        v_lanes = slice(2 * WIDTH + at, 2 * WIDTH + at + LANES)
        own_q = both_heads(own_rows(qkv, q_lanes), 0.125)
        own_k = both_heads(own_rows(qkv, k_lanes), 0.125)
        own_v = both_heads(own_rows(qkv, v_lanes))
        own_g = both_heads(own_rows(grad_rows, q_lanes))
        log_column = head_column(lse_col[...], pair)
        delta_column = head_column(delta_col[...], pair)
        d_query = jnp.zeros((2 * OWN, LANES), F32)
        d_key = jnp.zeros((2 * OWN, LANES), F32)
        d_value = jnp.zeros((2 * OWN, LANES), F32)
        for start, size in spans:
            span = slice(start, start + size)
            keep = (
                lax.broadcasted_iota(jnp.int32, (1, size), 1) + start
            )
            half = (keep >> 6) & 1
            position = ((half ^ slot) * group + (keep >> 7)) * HEAD_DIM + (keep & 63)
            good = jnp.logical_or(
                jnp.logical_and(keep < slot_len, position < length),
                jnp.logical_and(keep >= slot_len, keep < slot_len + mem_rows),
            )
            bias = jnp.where(good, 0.0, -1e30)
            keys, values = qkv[span, k_lanes], qkv[span, v_lanes]
            weights = jnp.exp(dot(own_q, keys, NT) + bias - log_column)
            slopes = dot(own_g, values, NT)
            scores = low(weights * (slopes - delta_column))
            d_query += dot(scores, keys)

            queries, grads = qkv[span, q_lanes], grad_rows[span, q_lanes]

            def row_pair(ref):
                return jnp.concatenate(
                    [
                        jnp.broadcast_to(ref[2 * pair + k : 2 * pair + k + 1, span], (OWN, size))
                        for k in range(2)
                    ],
                    0,
                )

            weights = jnp.exp(dot(own_k, queries, NT) + own_bias - row_pair(log_row))
            slopes = dot(own_v, grads, NT)
            scores = low(weights * (slopes - row_pair(delta_row)))
            d_value += dot(low(weights), grads)
            d_key += dot(scores, queries)
        packed[:, q_lanes] = low(join_heads(d_query) * 0.125)
        packed[:, k_lanes] = low(join_heads(d_key) * 0.125)
        packed[:, v_lanes] = low(join_heads(d_value))

    share = 1.0 / group
    row = lax.broadcasted_iota(jnp.int32, (OWN, 1), 0)
    row_weight = low(jnp.where(row < ROWS, 1.0, share))
    rows = jnp.concatenate([tokens[slot], arrived[...], memory[slot]], 0)
    scaled = packed[...] * row_weight
    for at in range(0, 3 * WIDTH, WIDTH):
        cols = slice(at, at + WIDTH)
        grad_weight[:, cols] = low(dot(rows, scaled[:, cols], TN))
    emit_blocks(
        grad_weight, keep_out, send_out, REDUCE_QKV, block, 16, slice(0, 16), slice(0, 3 * WIDTH)
    )
    query_bias = jnp.sum(high(scaled[:, :WIDTH]), axis=0, keepdims=True)
    value_bias = jnp.sum(high(scaled[:, 2 * WIDTH :]), axis=0, keepdims=True)
    vec = jnp.concatenate([query_bias, value_bias, vector_grads[2:8, :]], 0)
    ups = up_grads[...]
    lane8 = lane_index((8, LANES))
    for p in range(BLOCKS):
        g = p // 8
        top = roll_lanes(vec[:, g * LANES : (g + 1) * LANES], -16 * (p % 8))
        top = jnp.where(lane8 < 16, top, 0.0)
        g = p // 2
        bottom = roll_lanes(ups[:, g * LANES : (g + 1) * LANES], -64 * (p % 2))
        both = jnp.concatenate([top, bottom], 0)
        extra[p * 16 : (p + 1) * 16, :] = split_lanes(both)
    emit_blocks(
        extra,
        keep_out,
        send_out,
        REDUCE_QKV,
        block,
        16,
        slice(0, 16),
        slice(3 * WIDTH, 3 * WIDTH + LANES),
    )

    grad_in = first_grad[...] + dot(packed[...], weight[...], NT)
    square = squares[0]
    for k in range(1, group):
        square += squares[k]
    square = square[:4] + square[4:]
    square = jnp.concatenate([square[k : k + 1] for k in range(4)], 1)
    first, second, _ = split_three(square)
    tail = low(jnp.concatenate([first, second, jnp.zeros((14, WIDTH), F32)], 0))
    own_out[:64, :] = low(grad_in[:64])
    own_out[64:96, :] = low(grad_in[ROWS:])
    own_out[96:, :] = tail
    give_out[:96, :] = low(grad_in[64:])
    give_out[96:, :] = tail


def split_lanes(v):
    first = high(low(v))
    second = pltpu.roll(v - first, 64, v.ndim - 1)
    lanes = lax.broadcasted_iota(jnp.int32, v.shape, v.ndim - 1)
    return low(jnp.where(lanes < 64, first, second))


def fold_kernel(width, keep, other, keep_out, send_out):
    half = keep.shape[0] // 2
    for start, out in ((0, keep_out), (half, send_out)):
        span = slice(start, start + half)
        total = high(keep[span, :, :width]) + high(other[span, :, :width])
        out[:, :, :width] = low(total)
        for k in range(half):
            extra = high(keep[start + k, :, width:]) + high(other[start + k, :, width:])
            out[k, :, width:] = split_lanes(extra + pltpu.roll(extra, 64, 1))


def fold_with_extra(keep, other):
    shape = (keep.shape[0] // 2,) + keep.shape[1:]
    return pl.pallas_call(
        functools.partial(fold_kernel, 3 * WIDTH),
        out_shape=[jax.ShapeDtypeStruct(shape, BF)] * 2,
        name="fold",
    )(keep, other)


def fold_plain(keep, other):
    half = keep.shape[0] // 2
    return tuple(
        low(high(keep[part]) + high(other[part])) for part in (slice(0, half), slice(half, None))
    )


def emit_kernel(layout, mem_rows, *refs):
    lengths, out_own, out_got, grad_own, grad_got = refs[:5]
    out_tokens, out_memory, grad_tokens, grad_memory, rms = refs[5:]
    slot = lax.axis_index("seq") // layout.group
    for own, got, tokens, memory in (
        (out_own, out_got, out_tokens, out_memory),
        (grad_own, grad_got, grad_tokens, grad_memory),
    ):
        for source, at in ((own, slot), (got, 1 - slot)):
            tokens[at] = source[:64, :]
            memory[at] = low(high(source[64:96, :])[:mem_rows])
    result = []
    for source, at in ((grad_own, slot), (grad_got, 1 - slot)):
        tail = high(source[96:112, :])
        square = tail[0:1] + tail[1:2]
        result.append(jnp.sqrt(square / lengths[at].astype(F32)))
    row = lax.broadcasted_iota(jnp.int32, (2, WIDTH), 0)
    rms[...] = jnp.where(row == slot, result[0], result[1])


def call(kernel, name, outs, scratch, args, smem=1, limit=32, flops=0):
    vmem = pl.BlockSpec(memory_space=pltpu.VMEM)
    in_specs = [pl.BlockSpec(memory_space=pltpu.SMEM)] * smem + [vmem] * (len(args) - smem)
    size = sum(a.size * a.dtype.itemsize for a in args)
    return pl.pallas_call(
        kernel,
        out_shape=[jax.ShapeDtypeStruct(shape, kind) for shape, kind in outs],
        in_specs=in_specs,
        out_specs=[vmem] * len(outs),
        scratch_shapes=[pltpu.VMEM(shape, kind) for shape, kind in scratch],
        compiler_params=pltpu.CompilerParams(vmem_limit_bytes=limit * MIB),
        cost_estimate=pl.CostEstimate(flops=flops, bytes_accessed=size, transcendentals=0),
        name=name,
    )(*args)


def local_wide(
    layout,
    tokens,
    memory,
    lengths,
    w_qkv,
    b_query,
    b_value,
    w_out,
    b_out,
    gain_one,
    shift_one,
    w_up,
    b_up,
    w_down,
    b_down,
    gain_two,
    shift_two,
    cot_tokens,
    cot_memory,
):
    mem_rows = memory.shape[1]
    tok_rows = tokens.shape[1]
    slot_len = tok_rows * layout.seq
    key_rows = slot_len + MEM_KEYS
    partner = layout.seq_bits - 1
    slot = lax.axis_index("seq") // layout.group

    def pick(x, at):
        return lax.dynamic_index_in_dim(x, at, 0, False)

    arrived = layout.swap(pick(tokens, 1 - slot), partner)
    near, far = layout.gather_group(jnp.concatenate([pick(tokens, slot), arrived], 0)[None])

    vectors = jnp.stack(
        [b_query, b_value, b_out, gain_one, shift_one, b_down, gain_two, shift_two]
    )
    vectors = layout.join_low(vectors, 1)
    extra = jnp.concatenate(
        [
            jnp.pad(vectors, ((0, 0), (0, LANES - 16))),
            jnp.pad(layout.join_low(b_up, 0)[None], ((0, 7), (0, LANES - 64))),
        ],
        0,
    )
    first = jnp.concatenate([layout.join_low(w_qkv, 0), layout.join_low(w_out, 0), extra], 1)
    qkv_parts = layout.gather(first[None], GATHER_QKV)
    up_parts = layout.gather(layout.join_low(w_up, 0)[None], GATHER_UP)
    down_parts = layout.gather(layout.join_low(w_down, 0)[None], GATHER_DOWN)
    cot_arrived = layout.swap(pick(cot_tokens, 1 - slot), partner)
    pad_rows = ((0, 0), (0, MEM_PAD - mem_rows), (0, 0))
    memory_full = jnp.pad(memory, pad_rows)
    cot_memory_full = jnp.pad(cot_memory, pad_rows)

    qkv, attn, lse_col, vector_rows, up_bias = call(
        functools.partial(forward_kernel, layout, mem_rows, slot_len),
        "attention_forward",
        [
            ((key_rows, 3 * WIDTH), BF),
            ((OWN, WIDTH), F32),
            ((OWN, LANES), F32),
            ((8, WIDTH), F32),
            ((8, FF), F32),
        ],
        [((slot_len + MEM_PAD, WIDTH), BF), ((WIDTH, 3 * WIDTH), BF), ((WIDTH, LANES), BF)],
        (lengths, near, far, memory_full, *qkv_parts),
    )
    (
        pack,
        grad_mem,
        lse_mem,
        delta_mem,
        delta_col,
        first_grad,
        out_own,
        out_send,
        attn_low,
        branch_low,
        hidden_low,
        grad_linear,
        active,
        feed_low,
        vector_grads,
        up_grads,
    ) = call(
        functools.partial(feed_kernel, layout, mem_rows),
        "feed_forward",
        [
            ((1, ROWS + 16, WIDTH), BF),
            ((MEM_PAD, WIDTH), BF),
            ((8, LANES), F32),
            ((8, LANES), F32),
            ((OWN, LANES), F32),
            ((OWN, WIDTH), F32),
            ((64 + MEM_PAD, WIDTH), BF),
            ((64 + MEM_PAD, WIDTH), BF),
            ((OWN, WIDTH), BF),
            ((OWN, WIDTH), BF),
            ((OWN, WIDTH), BF),
            ((OWN, FF), BF),
            ((OWN, FF), BF),
            ((OWN, WIDTH), BF),
            ((8, WIDTH), F32),
            ((8, FF), F32),
        ],
        [((WIDTH, WIDTH), BF), ((WIDTH, FF), BF), ((FF, WIDTH), BF), ((OWN, FF), F32)],
        (
            lengths,
            tokens,
            arrived,
            memory_full,
            cot_tokens,
            cot_arrived,
            cot_memory_full,
            attn,
            lse_col,
            vector_rows,
            up_bias,
            *qkv_parts,
            *up_parts,
            *down_parts,
        ),
    )
    grads_near, grads_far = layout.gather_group(pack)
    out_got = layout.swap(out_send, partner)
    half = BLOCKS // 2
    up_keep, up_send, down_keep, down_send = call(
        functools.partial(weight_kernel, layout),
        "weight_gradients",
        [
            ((half, 16, FF), BF),
            ((half, 16, FF), BF),
            ((half, 80, WIDTH), BF),
            ((half, 80, WIDTH), BF),
        ],
        [((WIDTH, FF), BF), ((FF, WIDTH), BF), ((WIDTH, WIDTH), BF)],
        (attn_low, branch_low, hidden_low, grad_linear, active, feed_low),
        smem=0,
    )
    up_total = layout.reduce(up_keep, up_send, REDUCE_UP, fold_plain)
    down_total = layout.reduce(down_keep, down_send, REDUCE_DOWN, fold_plain)
    qkv_keep, qkv_send, grad_own, grad_send = call(
        functools.partial(backward_kernel, layout, mem_rows, slot_len),
        "attention_backward",
        [
            ((half, 16, 3 * WIDTH + LANES), BF),
            ((half, 16, 3 * WIDTH + LANES), BF),
            ((112, WIDTH), BF),
            ((112, WIDTH), BF),
        ],
        [
            ((WIDTH, 3 * WIDTH), BF),
            ((key_rows, WIDTH), BF),
            ((8, key_rows), F32),
            ((8, key_rows), F32),
            ((layout.group, 8, LANES), F32),
            ((OWN, 3 * WIDTH), BF),
            ((WIDTH, 3 * WIDTH), BF),
            ((WIDTH, LANES), BF),
        ],
        (
            lengths,
            tokens,
            arrived,
            memory_full,
            qkv,
            grads_near,
            grads_far,
            grad_mem,
            lse_mem,
            delta_mem,
            lse_col,
            delta_col,
            first_grad,
            vector_grads,
            up_grads,
            *qkv_parts,
        ),
    )
    qkv_total = layout.reduce(qkv_keep, qkv_send, REDUCE_QKV, fold_with_extra)
    grad_got = layout.swap(grad_send, partner)

    def add(pair):
        return high(pair[0][0]) + high(pair[1][0])

    up_sum = layout.reduce_low(add(up_total), 0)
    down_sum = add(down_total)
    out_sum = layout.reduce_low(down_sum[64:], 0)
    down_sum = layout.reduce_low(down_sum[:64], 0)
    qkv_sum = add(qkv_total)
    extra_sum = qkv_sum[:, 3 * WIDTH :]
    qkv_sum = layout.reduce_low(qkv_sum[:, : 3 * WIDTH], 0)
    vec = layout.reduce_low(extra_sum[:8, :16] + extra_sum[:8, 64:80], 1)
    up_vec = layout.reduce_low(extra_sum[8, :64] + extra_sum[8, 64:], 0)

    out_tokens, out_memory, grad_tokens, grad_memory, rms = call(
        functools.partial(emit_kernel, layout, mem_rows),
        "emit",
        [
            (tokens.shape, BF),
            (memory.shape, BF),
            (tokens.shape, BF),
            (memory.shape, BF),
            ((2, WIDTH), F32),
        ],
        [],
        (lengths, out_own, out_got, grad_own, grad_got),
    )
    return (
        out_tokens,
        out_memory,
        grad_tokens,
        grad_memory,
        qkv_sum,
        vec[0],
        vec[1],
        out_sum,
        vec[2],
        vec[3],
        vec[4],
        up_sum,
        up_vec,
        down_sum,
        vec[5],
        vec[6],
        vec[7],
        rms,
    )


FIRST = 4 * WIDTH + LANES


def prepare_kernel(layout, *refs):
    tokens, w_qkv, w_out = refs[:3]
    vectors, b_up = refs[3:11], refs[11]
    own, give = refs[12:14]
    up_cell, sems = refs[14:16]
    cells = refs[16:]
    slot = lax.axis_index("seq") // layout.group
    moves = [(b_up, up_cell)]
    for target in (own, give):
        moves.append((w_qkv, target.at[:, : 3 * WIDTH]))
        moves.append((w_out, target.at[:, 3 * WIDTH : 4 * WIDTH]))
    for k in range(4):
        rows = slice(16 * k, 16 * k + 16)
        lanes = slice(FIRST + k * WIDTH, FIRST + (k + 1) * WIDTH)
        moves.append((tokens.at[slot, rows], own.at[:, lanes]))
        moves.append((tokens.at[1 - slot, rows], give.at[:, lanes]))
    moves += [(v, cells[k]) for k, v in enumerate(vectors)]
    copies = [
        pltpu.make_async_copy(source, target, sems.at[k])
        for k, (source, target) in enumerate(moves)
    ]
    for copy in copies:
        copy.start()
    for copy in copies:
        copy.wait()
    blank = jnp.zeros((1, LANES - 16), F32)
    rows = [jnp.concatenate([high(v[...]).reshape(1, 16), blank], 1) for v in cells]
    rows.append(jnp.concatenate([high(up_cell[...]).reshape(1, 64), blank[:, :64]], 1))
    rows.append(jnp.zeros((7, LANES), F32))
    extra = low(jnp.concatenate(rows, 0))
    own[:, 4 * WIDTH : FIRST] = extra
    give[:, 4 * WIDTH : FIRST] = extra


def stacked_rows(value):
    return jnp.concatenate([value[:, k * WIDTH : (k + 1) * WIDTH] for k in range(4)], 0)


def gather_vectors(extra):
    pieces, ups = [], []
    for g in range(4):
        total = jnp.zeros((8, LANES), F32)
        for p in range(8):
            at = (8 * g + p) * 16
            total += roll_lanes(high(extra[at : at + 16, :])[:8], 16 * p)
        pieces.append(total)
    for g in range(16):
        total = jnp.zeros((8, LANES), F32)
        for p in range(2):
            at = (2 * g + p) * 16
            total += roll_lanes(high(extra[at : at + 16, :])[8:], 64 * p)
        ups.append(total)
    return jnp.concatenate(pieces, 1), jnp.concatenate(ups, 1)


def quad_forward_kernel(layout, mem_rows, slot_len, *refs):
    lengths, near, far, memory, w0, w1, w2, w3 = refs[:8]
    attn, qkv_own, rows, w_own, vectors, up_bias = refs[8:14]
    qkv, weight, extra = refs[14:]
    group = layout.group
    place = lax.axis_index("seq")
    slot, rank = place // group, place % group
    block = layout.block()
    length = lengths[slot]
    parts = (w0, w1, w2, w3)
    place_blocks(weight, parts, GATHER_QKV, block, 16, slice(0, 3 * WIDTH))
    place_blocks(extra, parts, GATHER_QKV, block, 16, slice(4 * WIDTH, FIRST))
    for part, masks in zip((near, far), layout.group_masks()):
        for k, mask in enumerate(masks):
            for part_half in range(2):
                at = aligned((rank ^ mask) * 2 + part_half, 64)
                rows[at, :] = stacked_rows(part[2 * k + part_half])
    rows[slot_len : slot_len + MEM_PAD, :] = memory[...]
    vector_rows, up_rows = gather_vectors(extra)
    vectors[...] = vector_rows
    up_bias[...] = up_rows

    key_rows = slot_len + MEM_KEYS
    filled = slot_len + MEM_PAD
    qkv[filled:key_rows, :] = jnp.zeros((key_rows - filled, 3 * WIDTH), BF)
    for part, shift in enumerate((vector_rows[0:1], None, vector_rows[1:2])):
        lanes = slice(part * WIDTH, (part + 1) * WIDTH)
        value = dot(rows[...], weight[:, lanes])
        qkv[:filled, lanes] = low(value if shift is None else value + shift)
    half = WIDTH // 2
    for part in range(3):
        own = aligned(2 * part + place % 2, half)
        qkv_own[:, part * half : (part + 1) * half] = qkv[:, own]
        w_own[:, part * half : (part + 1) * half] = weight[:, own]

    keep = key_valid((1, key_rows), 1, slot, group, length, slot_len, mem_rows)
    bias = jnp.where(keep, 0.0, -1e30)
    for pair in range(HEADS // 2):
        at = pair * LANES
        own = jnp.concatenate(
            [qkv[aligned(rank, ROWS), at : at + LANES], qkv[slot_len:filled, at : at + LANES]], 0
        )
        keys = qkv[:, WIDTH + at : WIDTH + at + LANES]
        values = qkv[:, 2 * WIDTH + at : 2 * WIDTH + at + LANES]
        scores = dot(both_heads(own, 0.125), keys, NT) + bias
        highest = jnp.max(scores, axis=1, keepdims=True)
        expos = jnp.exp(scores - highest)
        total = jnp.sum(expos, axis=1, keepdims=True)
        attn[:, at : at + LANES] = join_heads(dot(low(expos), values) / total)


STRIP = 32
PACK = 32

ACT_LANES = FF + 2 * WIDTH + WIDTH // 2
LINEAR_LANES = FF // 2 + WIDTH // 2


def hand_out(core, own, give, value, start):
    half = value.shape[1] // 2
    first, second = value[:, :half], value[:, half:]
    mine = core == 0
    own[:, start : start + half] = jnp.where(mine, first, second)
    give[:, start : start + half] = jnp.where(mine, second, first)


def row_weights(group):
    row = lax.broadcasted_iota(jnp.int32, (OWN, 1), 0)
    return jnp.where(row < ROWS, 1.0, 1.0 / group)


def quad_feed_kernel(layout, mem_rows, *refs):
    lengths, tokens, arrived, memory, cots, cot_arrived, cot_memory = refs[:7]
    attn, vectors, up_bias = refs[7:10]
    outs, ups, downs = refs[10:14], refs[14:18], refs[18:22]
    out_own, out_send, own, give, sums, squares_out, w_heads = refs[22:29]
    w_out, w_up, w_down, slope, second_out, normed_out, inverse_out = refs[29:36]
    inputs, cot, feed, linear = refs[36:]
    group = layout.group
    place = lax.axis_index("seq")
    slot, rank = place // group, place % group
    block = layout.block()
    length = lengths[slot]
    place_blocks(w_out, outs, GATHER_QKV, block, 16, slice(3 * WIDTH, 4 * WIDTH))
    place_blocks(w_up, ups, GATHER_UP, block, 16, slice(0, FF))
    place_blocks(w_down, downs, GATHER_DOWN, block, 64, slice(0, WIDTH))
    w_heads[...] = w_out[aligned(place % 2, WIDTH // 2), :]

    vec = vectors[...]
    out_bias, gain_one, shift_one, down_bias, gain_two, shift_two = [
        vec[k : k + 1] for k in range(2, 8)
    ]
    inputs[:64, :] = high(tokens[slot])
    inputs[64:ROWS, :] = high(stacked_rows(arrived[...]))
    inputs[ROWS:, :] = high(memory[...])
    cot[:64, :] = high(cots[slot])
    cot[64:ROWS, :] = high(cot_arrived[...])
    cot[ROWS:, :] = high(cot_memory[...])
    valid_all = jnp.where(own_valid((OWN, 1), slot, group, rank, length, mem_rows), 1.0, 0.0)
    weight_all = row_weights(group)
    strips = [slice(start, start + STRIP) for start in range(0, OWN, STRIP)]

    heads_out = low(attn[...])
    for target in (own, give):
        target[:, FF + WIDTH : FF + 2 * WIDTH] = heads_out
    feed[...] = dot(heads_out, w_out[...])
    for strip in strips:
        normed, inverse = normalize(inputs[strip, :] + (feed[strip, :] + out_bias))
        normed_out[strip, :] = normed
        inverse_out[strip, :] = jnp.broadcast_to(inverse, (STRIP, LANES))
        hidden = normed * gain_one + shift_one
        inputs[strip, :] = hidden
        hidden_low = low(hidden)
        own[strip, FF : FF + WIDTH] = hidden_low
        give[strip, FF : FF + WIDTH] = hidden_low
    for at in range(0, FF, WIDTH):
        cols = slice(at, at + WIDTH)
        linear[:, cols] = dot(own[:, FF : FF + WIDTH], w_up[:, cols])
    for at in range(0, FF, WIDTH):
        cols = slice(at, at + WIDTH)
        for strip in strips:
            t = linear[strip, cols] + up_bias[0:1, cols]
            square = t * t
            bent = jnp.tanh(0.7978845608 * (t + 0.044715 * (square * t)))
            half = 0.5 * (1.0 + bent)
            slope[strip, cols] = half + (0.5 * 0.7978845608) * t * (1.0 - bent * bent) * (
                1.0 + (3 * 0.044715) * square
            )
            act = low(t * half)
            own[strip, cols] = act
            give[strip, cols] = act
        product = dot(own[:, cols], w_down[cols, :])
        feed[...] = product if at == 0 else feed[...] + product
    squares = jnp.zeros((1, WIDTH), F32)
    parts = [jnp.zeros((1, WIDTH), F32)] * 3
    for strip in strips:
        valid, weight = valid_all[strip], weight_all[strip]
        branch = feed[strip, :] + down_bias
        normed, inverse = normalize(inputs[strip, :] + branch)
        output = low((normed * gain_two + shift_two) * valid)
        if strip.start < HEAD_DIM:
            out_own[strip, :] = output
        else:
            out_send[strip.start - HEAD_DIM : strip.stop - HEAD_DIM, :] = output
        if strip.start < ROWS:
            squares += jnp.sum(branch * branch * valid, axis=0, keepdims=True)
        else:
            out_own[HEAD_DIM:, :] = output
        g = cot[strip, :] * valid
        second = norm_back(g * gain_two, normed, inverse)
        second_out[strip, :] = second
        grad_feed = low(second)
        terms = high(grad_feed), g * normed, g
        parts = [
            part + jnp.sum(term * weight, axis=0, keepdims=True)
            for part, term in zip(parts, terms)
        ]
        scaled = grad_feed * low(weight)
        half = WIDTH // 2
        first_core = place % 2 == 0
        own[strip, FF + 2 * WIDTH :] = jnp.where(first_core, scaled[:, :half], scaled[:, half:])
        give[strip, FF + 2 * WIDTH :] = jnp.where(first_core, scaled[:, half:], scaled[:, :half])
    squares_out[...] = low(
        jnp.concatenate([*split_three(squares), jnp.zeros((13, WIDTH), F32)], 0)
    )
    sums[...] = jnp.concatenate([jnp.zeros((5, WIDTH), F32), *parts], 0)


def quad_slope_kernel(layout, *refs):
    vectors, sums, squares, w_out, w_up, w_down, slope, second_in, normed_in, inverse_in = refs[:10]
    pack, grad_mem, first_grad, own, give = refs[10:15]
    grad_linear, product, grad_hidden, halves = refs[15:]
    place = lax.axis_index("seq")
    core = place % 2
    weight = row_weights(layout.group)
    weight_low = low(weight)

    strips = [slice(start, start + STRIP) for start in range(0, OWN, STRIP)]
    grad_feed = low(second_in[...])
    for at in range(0, FF, WIDTH):
        cols = slice(at, at + WIDTH)
        product[:, cols] = dot(grad_feed, w_down[cols, :], NT)
    ups = []
    for at in range(0, FF, WIDTH):
        cols = slice(at, at + WIDTH)
        part = jnp.zeros((1, WIDTH), F32)
        for strip in strips:
            linear = low(product[strip, cols] * slope[strip, cols])
            grad_linear[strip, cols] = linear
            part += jnp.sum(high(linear) * weight[strip], axis=0, keepdims=True)
            halves[at // (FF // 2), strip, at % (FF // 2) : at % (FF // 2) + WIDTH] = (
                linear * weight_low[strip]
            )
        ups.append(part)
    grad_hidden[...] = dot(grad_linear[...], w_up[...], NT)
    own[:, : FF // 2] = halves[core]
    give[:, : FF // 2] = halves[1 - core]
    parts = [jnp.zeros((1, WIDTH), F32)] * 3
    for strip in strips:
        hidden = second_in[strip, :] + grad_hidden[strip, :]
        normed = normed_in[strip, :]
        first = norm_back(hidden * vectors[3:4, :], normed, inverse_in[strip, :1])
        first_grad[strip, :] = first
        grad_branch = low(first)
        terms = high(grad_branch), hidden * normed, hidden
        parts = [
            part + jnp.sum(term * weight[strip], axis=0, keepdims=True)
            for part, term in zip(parts, terms)
        ]
        scaled = grad_branch * weight_low[strip]
        half = WIDTH // 2
        own[strip, FF // 2 :] = jnp.where(core == 0, scaled[:, :half], scaled[:, half:])
        give[strip, FF // 2 :] = jnp.where(core == 0, scaled[:, half:], scaled[:, :half])
        if strip.start < ROWS:
            pack[0, strip, :] = grad_branch
        else:
            grad_mem[...] = grad_branch
    sizes = jnp.concatenate([*parts, sums[5:8, :], *ups], 0)
    first, second, _ = split_three(sizes)
    blank = jnp.zeros((PACK - 23, WIDTH), F32)
    pack[0, ROWS:, :] = low(
        jnp.concatenate([high(squares[...])[:3], first, second, blank], 0)
    )


MAIN_ROWS = 176
REST_ROWS = 112
FEED_ROWS = MAIN_ROWS + REST_ROWS


def quad_weight_kernel(layout, *refs):
    acts, got_acts, linear, got_linear = refs[:4]
    main, rest = refs[4:6], refs[6:8]
    up, down, out = refs[8:]
    core = lax.axis_index("seq") % 2
    pair = layout.block() >> 1
    half = WIDTH // 2

    def both(first, second, start, size):
        cols = slice(start, start + size)
        return jnp.concatenate([first[:, cols], second[:, cols]], 0)

    def emit(source, target, unit, start):
        orders = PAIR_MAIN if target is main else PAIR_REST
        at = slice(start, start + unit)
        emit_pairs(source, *target, orders, pair, core, unit, at)

    grad_feed = both(acts, got_acts, FF + 2 * WIDTH, half)
    for start in range(0, FF, WIDTH):
        act = both(acts, got_acts, start, WIDTH)
        down[start : start + WIDTH, :] = low(dot(act, grad_feed, TN))
    emit(down, main, 128, 0)
    hidden = both(acts, got_acts, FF, WIDTH)
    for start in range(0, FF // 2, WIDTH):
        up[:, start : start + WIDTH] = low(dot(hidden, both(linear, got_linear, start, WIDTH), TN))
    heads_out = both(acts, got_acts, FF + WIDTH, WIDTH)
    value = low(dot(heads_out, both(linear, got_linear, FF // 2, half), TN))
    for p in range(BLOCKS):
        out[p % 2, p // 2 * 16 : p // 2 * 16 + 16, :] = value[16 * p : 16 * p + 16]
    for k in range(4):
        target, start = (main, 128) if k == 0 else (rest, 32 * k - 32)
        emit(up.at[:, half * k : half * (k + 1)], target, 32, start)
    emit(out.at[0], main, 16, 160)
    emit(out.at[1], rest, 16, 96)


def quad_backward_kernel(layout, mem_rows, slot_len, *refs):
    lengths, qkv, rows, w_own, w_heads, near, far, grad_mem = refs[:8]
    keep_out, send_out, in_keep, in_send, tail = refs[8:13]
    grad_rows, sums, packed, grad_weight, extra = refs[13:]
    group = layout.group
    place = lax.axis_index("seq")
    slot, rank = place // group, place % group
    core = place % 2
    pair = layout.block() >> 1
    length = lengths[slot]
    filled = slot_len + MEM_PAD
    key_rows = slot_len + MEM_KEYS
    half = WIDTH // 2
    for part, masks in zip((near, far), layout.group_masks()):
        for k, mask in enumerate(masks):
            at = rank ^ mask
            grad_rows[aligned(at, ROWS), :] = part[k, :ROWS, :]
            sums[at] = high(part[k, ROWS:, :])
    grad_rows[slot_len:filled, :] = grad_mem[...]

    keep = key_valid((1, key_rows), 1, slot, group, length, slot_len, mem_rows)
    bias = jnp.where(keep, 0.0, -1e30)
    grad_attn = low(dot(grad_rows[...], w_heads[...], NT))
    for k in range(2):
        at = [slice(part * half + k * LANES, part * half + (k + 1) * LANES) for part in range(3)]
        queries, keys, values = qkv[:filled, at[0]], qkv[:, at[1]], qkv[:, at[2]]
        d_query = jnp.zeros((filled, LANES), F32)
        d_key = jnp.zeros((key_rows, LANES), F32)
        d_value = jnp.zeros((key_rows, LANES), F32)
        for mask in half_masks():
            query = queries * (mask * 0.125)
            grads = grad_attn[:, k * LANES : (k + 1) * LANES] * mask
            scores = dot(query, keys, NT) + bias
            expos = jnp.exp(scores - jnp.max(scores, axis=1, keepdims=True))
            weights = expos * (1.0 / jnp.sum(expos, axis=1, keepdims=True))
            weights_low = low(weights)
            slopes = dot(grads, values, NT)
            delta = jnp.sum(high(weights_low) * slopes, axis=1, keepdims=True)
            slopes = low(weights * (slopes - delta))
            d_query += dot(slopes, keys) * (high(mask) * 0.125)
            d_key += dot(slopes, query, TN)
            d_value += dot(weights_low, grads, TN)
        packed[:, at[0]] = low(d_query)
        packed[:, at[1]] = low(d_key[:filled])
        packed[:, at[2]] = low(d_value[:filled])

    def emit(source, unit, at):
        emit_pairs(source, keep_out, send_out, PAIR_QKV, pair, core, unit, at)

    for part in range(3):
        lanes = slice(part * half, (part + 1) * half)
        grad_weight[...] = low(dot(rows[...], packed[:, lanes], TN))
        emit(grad_weight, 32, slice(32 * part, 32 * part + 32))
    for target, at in ((in_keep, rank), (in_send, rank ^ 1)):
        target[:ROWS, :] = low(dot(packed[aligned(at, ROWS), :], w_own[...], NT))
    grad_in = low(dot(packed[slot_len:filled, :], w_own[...], NT))
    in_keep[ROWS:, :] = grad_in
    in_send[ROWS:, :] = grad_in

    total = sums[0]
    for k in range(1, group):
        total += sums[k]
    square = total[0:1] + total[1:2] + total[2:3]
    tail[...] = low(jnp.concatenate([*split_three(square), jnp.zeros((13, WIDTH), F32)], 0))
    sizes = total[3:13] + total[13:23]
    first_core = core == 0
    blank = jnp.zeros((1, half), F32)
    biases = []
    for part in (0, 2):
        value = packed[:, part * half : (part + 1) * half]
        value = jnp.sum(high(value), axis=0, keepdims=True)
        first, second = jnp.where(first_core, value, 0.0), jnp.where(first_core, 0.0, value)
        biases.append(jnp.concatenate([first, second], 1))
    vec = jnp.concatenate([*biases, sizes[:6]], 0)
    ups = jnp.concatenate([sizes[6:10], jnp.zeros((4, WIDTH), F32)], 0)
    lanes = lane_index((8, LANES))
    sublane = lax.broadcasted_iota(jnp.int32, (8, LANES), 0)
    for p in range(0, BLOCKS, 2):
        both = []
        for q in (p, p + 1):
            mine = core == q % 2
            g = q // 8
            columns = slice(g * LANES, (g + 1) * LANES)
            cell = roll_lanes(vec[:, columns], -16 * (q % 8))
            cell = jnp.where(sublane < 2, cell, jnp.where(mine, cell, 0.0))
            g = q % 8 // 2
            row = ups[q // 8 : q // 8 + 1, g * LANES : (g + 1) * LANES]
            row = jnp.broadcast_to(jnp.where(mine, row, 0.0), (8, LANES))
            up = jnp.zeros((8, LANES), F32)
            for k in range(4):
                up = jnp.where(sublane == k, roll_lanes(row, 16 - 64 * (q % 2) - 16 * k), up)
            both.append(jnp.where(lanes < 16, cell, jnp.where(lanes < 32, up, 0.0)))
        wide = jnp.concatenate(both, 1)
        extra[p * 8 : p * 8 + 16, :] = low(jnp.concatenate([wide, jnp.zeros_like(wide)], 0))
    emit(extra, 16, slice(96, 112))


def feed_rows(core):
    starts = [128, *(MAIN_ROWS + 32 * k for k in range(3))]
    at = [pl.ds(pl.multiple_of(start + 16 * core, 16), 16) for start in starts]
    at.append(pl.ds(pl.multiple_of(64 * core, 64), 64))
    at.append(pl.ds(pl.multiple_of(160 + 112 * core, 16), 16))
    return at


def qkv_rows(core):
    return [pl.ds(pl.multiple_of(FEED_ROWS + 32 * k + 16 * core, 16), 16) for k in range(3)]


EXTRA_ROWS = pl.ds(FEED_ROWS + 96, 16)


def turn_kernel(keep, other, send):
    start = 0
    core = 1 - lax.axis_index("seq") % 2
    for at in [*feed_rows(core), *qkv_rows(core), EXTRA_ROWS]:
        send[start : start + at.size, :] = low(high(keep[0, at, :]) + high(other[0, at, :]))
        start += at.size


def emit_kernel_quad(keep, other, got, w_up, w_down, w_out, w_qkv, *vectors):
    core = lax.axis_index("seq") % 2
    half = WIDTH // 2
    start = 0
    places = [*feed_rows(core), *qkv_rows(core), EXTRA_ROWS]
    for k, at in enumerate(places):
        total = high(keep[0, at, :]) + high(other[0, at, :])
        arrived = high(got[start : start + at.size, :])
        start += at.size
        if k < 4:
            target, own, theirs = w_up, 4 * core + k, 4 - 4 * core + k
        elif k < 6:
            target, own, theirs = (w_down, w_out)[k - 4], core, 1 - core
        elif k < 9:
            target, own, theirs = w_qkv, 2 * k - 12 + core, 2 * k - 11 - core
        else:
            total += arrived
            continue
        target[:, aligned(own, half)] = total
        target[:, aligned(theirs, half)] = arrived
    total = jnp.where(core == 0, total[:8, :LANES], total[:8, LANES:])
    for k in range(8):
        vectors[k][...] = total[k, :16]
    lanes = lane_index((1, LANES))
    ups = jnp.zeros((1, LANES), F32)
    for k in range(4):
        rolled = roll_lanes(total[k : k + 1], 16 * k - 16)
        ups = jnp.where(jnp.logical_and(lanes >= 16 * k, lanes < 16 * k + 16), rolled, ups)
    vectors[8][...] = ups[0, :64]


def emit_tokens_kernel(layout, *refs):
    lengths, out_own, grad_own, grad_got, tail = refs[:5]
    out_tokens, out_memory, grad_tokens, grad_memory, rms = refs[5:]
    slot = lax.axis_index("seq") // layout.group
    pieces = (
        (out_own, 0, 64, slot, out_tokens, out_memory),
        (grad_got, 112, 176, 1 - slot, out_tokens, out_memory),
        (grad_own, 0, 128, slot, grad_tokens, grad_memory),
        (grad_got, 0, 64, 1 - slot, grad_tokens, grad_memory),
    )
    cells = [[None, None], [None, None]]
    for k, (source, start, mem, at, tokens, _) in enumerate(pieces):
        tokens[at] = source[start : start + 64, :]
        cells[k // 2][k % 2] = high(source[mem : mem + 32, :])
    for (own, got), memory in zip(cells, (out_memory, grad_memory)):
        first = jnp.where(slot == 0, own, got)
        second = jnp.where(slot == 0, got, own)
        rows = memory.shape[0]
        memory[...] = low(jnp.stack([first[:rows], second[:rows]], 1))
    result = []
    for cell, at in ((tail[...], slot), (grad_got[96:112, :], 1 - slot)):
        cell = high(cell)
        square = cell[0:1] + cell[1:2] + cell[2:3]
        result.append(jnp.sqrt(square / lengths[at].astype(F32)))
    row = lax.broadcasted_iota(jnp.int32, (2, WIDTH), 0)
    rms[...] = jnp.where(row == slot, result[0], result[1])


def local_quad(
    layout,
    tokens,
    memory,
    lengths,
    w_qkv,
    b_query,
    b_value,
    w_out,
    b_out,
    gain_one,
    shift_one,
    w_up,
    b_up,
    w_down,
    b_down,
    gain_two,
    shift_two,
    cot_tokens,
    cot_memory,
):
    mem_rows = memory.shape[1]
    slot_len = tokens.shape[1] * layout.seq
    key_rows = slot_len + MEM_KEYS
    filled = slot_len + MEM_PAD
    partner = layout.seq_bits - 1
    slot = lax.axis_index("seq") // layout.group

    def pick(x, at):
        return lax.dynamic_index_in_dim(x, at, 0, False)

    small = (b_query, b_value, b_out, gain_one, shift_one, b_down, gain_two, shift_two)
    own, give = pl.pallas_call(
        functools.partial(prepare_kernel, layout),
        out_shape=[jax.ShapeDtypeStruct((16, FIRST + FF), BF)] * 2,
        in_specs=[pl.BlockSpec(memory_space=pl.ANY)] * 12,
        out_specs=[pl.BlockSpec(memory_space=pltpu.VMEM)] * 2,
        scratch_shapes=[pltpu.VMEM((64,), BF), pltpu.SemaphoreType.DMA((21,))]
        + [pltpu.VMEM((16,), BF)] * 8,
        name="prepare",
    )(tokens, w_qkv, w_out, *small, b_up)

    def after(x, *others):
        return lax.optimization_barrier((x, *others))[0]

    def doubled(held, bit):
        return jnp.concatenate([held, layout.block_swap(held, bit)], 0)

    def finish(held, order, *ready):
        last = after(layout.block_swap(held, order[3]), *ready)
        return held, last, layout.block_swap(held, 0), layout.block_swap(last, 0)

    second = doubled(w_up[None], GATHER_UP[0])
    third = doubled(w_down[None], GATHER_DOWN[0])
    got = layout.swap(give, partner)[None]
    arrived = got[0, :, FIRST:]
    held = jnp.concatenate([own[None], got], 0)
    first = doubled(held[:, :, :FIRST], GATHER_QKV[1])
    near = doubled(after(held[:, :, FIRST:], first), GATHER_QKV[1])
    far = layout.swap(near, 0)
    first = doubled(first, GATHER_QKV[2])
    second = doubled(doubled(second, GATHER_UP[1]), GATHER_UP[2])
    third = doubled(doubled(third, GATHER_DOWN[1]), GATHER_DOWN[2])
    cot_arrived = layout.swap(pick(after(cot_tokens, first), 1 - slot), partner)
    pad_rows = ((0, MEM_PAD - mem_rows), (0, 0))
    own_memory = jnp.pad(pick(memory, slot), pad_rows)
    own_cot_memory = jnp.pad(pick(cot_memory, slot), pad_rows)
    qkv_parts = finish(first, GATHER_QKV, cot_arrived)
    up_parts = finish(second, GATHER_UP)
    down_parts = finish(third, GATHER_DOWN)

    attn, qkv_own, rows, w_own, vector_rows, up_bias = call(
        functools.partial(quad_forward_kernel, layout, mem_rows, slot_len),
        "attention_forward",
        [
            ((OWN, WIDTH), F32),
            ((key_rows, 3 * WIDTH // 2), BF),
            ((filled, WIDTH), BF),
            ((WIDTH, 3 * WIDTH // 2), BF),
            ((8, WIDTH), F32),
            ((8, FF), F32),
        ],
        [((key_rows, 3 * WIDTH), BF), ((WIDTH, 3 * WIDTH), BF), ((WIDTH, LANES), BF)],
        (lengths, near, far, own_memory, *qkv_parts),
        flops=4 * 10**9,
    )
    (
        out_own,
        out_send,
        acts,
        acts_give,
        sums,
        squares,
        w_heads,
        w_out_all,
        w_up_all,
        w_down_all,
        slope,
        second_grad,
        normed_one,
        inverse_one,
    ) = call(
        functools.partial(quad_feed_kernel, layout, mem_rows),
        "feed_forward",
        [
            ((64 + MEM_PAD, WIDTH), BF),
            ((64 + MEM_PAD, WIDTH), BF),
            ((OWN, ACT_LANES), BF),
            ((OWN, ACT_LANES), BF),
            ((8, WIDTH), F32),
            ((16, WIDTH), BF),
            ((WIDTH // 2, WIDTH), BF),
            ((WIDTH, WIDTH), BF),
            ((WIDTH, FF), BF),
            ((FF, WIDTH), BF),
            ((OWN, FF), F32),
            ((OWN, WIDTH), F32),
            ((OWN, WIDTH), F32),
            ((OWN, LANES), F32),
        ],
        [
            ((OWN, WIDTH), F32),
            ((OWN, WIDTH), F32),
            ((OWN, WIDTH), F32),
            ((OWN, FF), F32),
        ],
        (
            lengths,
            tokens,
            arrived,
            own_memory,
            cot_tokens,
            cot_arrived,
            own_cot_memory,
            attn,
            vector_rows,
            up_bias,
            *qkv_parts,
            *up_parts,
            *down_parts,
        ),
        flops=3 * 10**9,
    )
    acts_got = layout.swap(acts_give, 0)
    pack, grad_mem, first_grad, linear, linear_give = call(
        functools.partial(quad_slope_kernel, layout),
        "feed_backward",
        [
            ((1, ROWS + PACK, WIDTH), BF),
            ((MEM_PAD, WIDTH), BF),
            ((OWN, WIDTH), F32),
            ((OWN, LINEAR_LANES), BF),
            ((OWN, LINEAR_LANES), BF),
        ],
        [
            ((OWN, FF), BF),
            ((OWN, FF), F32),
            ((OWN, WIDTH), F32),
            ((2, OWN, FF // 2), BF),
        ],
        (
            vector_rows,
            sums,
            squares,
            w_out_all,
            w_up_all,
            w_down_all,
            slope,
            second_grad,
            normed_one,
            inverse_one,
        ),
        smem=0,
        flops=3 * 10**9,
    )
    linear_got = layout.swap(linear_give, 0)
    grads_next = layout.swap(pack, 1)
    half = PAIRS // 2
    main_keep, main_send, rest_keep, rest_send = call(
        functools.partial(quad_weight_kernel, layout),
        "weight_gradients",
        [((half, MAIN_ROWS, WIDTH // 2), BF)] * 2 + [((half, REST_ROWS, WIDTH // 2), BF)] * 2,
        [((WIDTH, FF // 2), BF), ((FF, WIDTH // 2), BF), ((2, WIDTH // 2, WIDTH // 2), BF)],
        (acts, after(acts_got, pack), linear, linear_got),
        smem=0,
        flops=10**9,
    )
    grads_next = after(grads_next, main_send)
    grads_near = jnp.concatenate([pack, grads_next], 0)
    grads_far = layout.swap(grads_near, 0)
    qkv_keep, qkv_send, in_keep, in_send, tail = call(
        functools.partial(quad_backward_kernel, layout, mem_rows, slot_len),
        "attention_backward",
        [
            ((half // 2, 112, WIDTH // 2), BF),
            ((half // 2, 112, WIDTH // 2), BF),
            ((OWN, WIDTH), BF),
            ((OWN, WIDTH), BF),
            ((16, WIDTH), BF),
        ],
        [
            ((filled, WIDTH), BF),
            ((layout.group, PACK, WIDTH), F32),
            ((filled, 3 * WIDTH // 2), BF),
            ((WIDTH, WIDTH // 2), BF),
            ((8 * BLOCKS, WIDTH // 2), BF),
        ],
        (lengths, qkv_own, rows, w_own, w_heads, grads_near, grads_far, grad_mem),
        flops=0,
    )
    swap = layout.pair_swap_by_core

    def bits(orders, step):
        return tuple(order[step] for order in orders)

    main_other = swap(main_send, bits(PAIR_MAIN, 0))
    rest_other = swap(rest_send, bits(PAIR_REST, 0))
    main_keep, main_send = fold_plain(main_keep, main_other)
    rest_keep, rest_send = fold_plain(rest_keep, rest_other)
    qkv_send = after(qkv_send, main_send, rest_send)
    both_send = jnp.concatenate([main_send, rest_send, qkv_send], 1)
    both_other = swap(both_send, bits(PAIR_QKV, 0))
    main_keep, main_send = fold_plain(main_keep, both_other[:, :MAIN_ROWS])
    both_keep = jnp.concatenate([rest_keep, qkv_keep], 1)
    both_keep, both_send = fold_plain(both_keep, both_other[:, MAIN_ROWS:])
    second_ready = both_send
    main_other = swap(main_send, bits(PAIR_MAIN, 2))
    both_other = swap(both_send, bits(PAIR_QKV, 1))
    main_keep, main_send = fold_plain(main_keep, main_other)
    both_keep, both_send = fold_plain(both_keep, both_other)
    all_keep = jnp.concatenate([main_keep, both_keep], 1)
    all_send = jnp.concatenate([main_send, both_send], 1)

    in_got = layout.swap(in_send, 0)
    grad_own = low(high(in_keep) + high(in_got) + first_grad)
    grad_got = layout.swap(jnp.concatenate([grad_own[64:], tail, out_send], 0), partner)
    grad_got = after(grad_got, all_send)

    out_tokens, out_memory, grad_tokens, grad_memory, rms = call(
        functools.partial(emit_tokens_kernel, layout),
        "emit_tokens",
        [
            (tokens.shape, BF),
            ((mem_rows, 2, WIDTH), BF),
            (tokens.shape, BF),
            ((mem_rows, 2, WIDTH), BF),
            ((2, WIDTH), F32),
        ],
        [],
        (lengths, out_own, grad_own, grad_got, tail),
    )
    all_other = swap(all_send, bits(PAIR_MAIN, 3))
    order = (1, 0, 2)
    all_other, out_memory, grad_memory, rms = lax.optimization_barrier(
        (all_other, out_memory, grad_memory, rms)
    )
    out_memory, grad_memory = jnp.transpose(out_memory, order), jnp.transpose(grad_memory, order)
    (turned,) = call(
        turn_kernel, "turn", [((208, WIDTH // 2), BF)], [], (all_keep, all_other), smem=0
    )
    turned = layout.swap(turned, 0)
    up_sum, down_sum, out_sum, qkv_sum, *vec = call(
        emit_kernel_quad,
        "emit_weights",
        [(w_up.shape, F32), (w_down.shape, F32), (w_out.shape, F32), (w_qkv.shape, F32)]
        + [((16,), F32)] * 8
        + [((64,), F32)],
        [],
        (all_keep, all_other, turned),
        smem=0,
    )
    return (
        out_tokens,
        out_memory,
        grad_tokens,
        grad_memory,
        qkv_sum,
        vec[0],
        vec[1],
        out_sum,
        vec[2],
        vec[3],
        vec[4],
        up_sum,
        vec[8],
        down_sum,
        vec[5],
        vec[6],
        vec[7],
        rms,
    )


def solution(mesh):
    rows = P("dp", "seq", None)
    slots = P("dp", None, None)
    matrix = P(("dp", "seq"), None)
    vector = P(("dp", "seq"))
    weights = (
        matrix,
        vector,
        vector,
        matrix,
        vector,
        vector,
        vector,
        matrix,
        vector,
        matrix,
        vector,
        vector,
        vector,
    )
    layout = Layout(mesh)
    quad = layout.group == 4 and layout.devices == BLOCKS
    return jax.shard_map(
        functools.partial(local_quad if quad else local_wide, layout),
        mesh=mesh,
        in_specs=(rows, slots, P("dp"), *weights, rows, slots),
        out_specs=(rows, slots, rows, slots, *weights, P("dp", None)),
        check_vma=False,
    )
```

```python
import functools

import jax
import jax.numpy as jnp
from jax import lax
from jax.experimental import pallas as pl
from jax.experimental.pallas import tpu as pltpu
from jax.sharding import PartitionSpec as P

HEADS = 8
HEAD_DIM = 64
WIDTH = 512
FF = 2048
BLOCKS = 32
ROWS = 128
MEM_PAD = 32
OWN = ROWS + MEM_PAD
MEM_KEYS = 128
LANES = 128
MIB = 1 << 20

BF = jnp.bfloat16
F32 = jnp.float32
NN = (((1,), (0,)), ((), ()))
NT = (((1,), (1,)), ((), ()))
TN = (((0,), (0,)), ((), ()))

GATHER_QKV = (2, 1, 4, 3, 0)
GATHER_UP = (2, 3, 1, 4, 0)
GATHER_DOWN = (2, 4, 3, 1, 0)
REDUCE_UP = (0, 1, 4, 3, 2)
REDUCE_DOWN = (0, 3, 1, 4, 2)
REDUCE_QKV = (0, 4, 3, 1, 2)
PAIRS = BLOCKS // 2
PAIR_MAIN = ((2, 3, 0, 1), (3, 2, 0, 1))
PAIR_REST = ((0, 3, 2, 1), (0, 2, 3, 1))
PAIR_QKV = ((3, 2, 1), (2, 3, 1))


def dot(a, b, dims=NN):
    return lax.dot_general(a, b, dims, preferred_element_type=F32)


def low(v):
    return v.astype(BF)


def high(v):
    return v.astype(F32)


def split_three(v):
    first = high(low(v))
    second = high(low(v - first))
    return first, second, high(low(v - first - second))


def aligned(index, size):
    return pl.ds(pl.multiple_of(index * size, size), size)


class Layout:
    def __init__(self, mesh):
        self.dp = mesh.shape["dp"]
        self.seq = mesh.shape["seq"]
        self.devices = self.dp * self.seq
        self.low_bits = (self.devices // BLOCKS).bit_length() - 1
        self.group = self.seq // 2
        self.seq_bits = self.seq.bit_length() - 1

    def dim(self, bit):
        if bit < self.seq_bits:
            return "seq", 1 << bit
        return "dp", 1 << (bit - self.seq_bits)

    def swap(self, x, bit):
        axis, mask = self.dim(bit)
        size = self.seq if axis == "seq" else self.dp
        return lax.ppermute(x, axis, [(i, i ^ mask) for i in range(size)])

    def block_swap(self, x, bit):
        return self.swap(x, bit + self.low_bits)

    def pair_swap(self, x, bit):
        return self.swap(x, bit + 1)

    def pair_swap_by_core(self, x, bits):
        pairs = [(i, i ^ (2 << bits[i % 2])) for i in range(self.devices)]
        return lax.ppermute(x, ("dp", "seq"), pairs)

    def device(self):
        return lax.axis_index("dp") * self.seq + lax.axis_index("seq")

    def block(self):
        return self.device() >> self.low_bits

    def join_low(self, x, axis):
        for bit in range(self.low_bits):
            other = self.swap(x, bit)
            first = (self.device() >> bit) % 2 == 0
            x = jnp.where(
                first, jnp.concatenate([x, other], axis), jnp.concatenate([other, x], axis)
            )
        return x

    def reduce_low(self, x, axis):
        for bit in reversed(range(self.low_bits)):
            first = (self.device() >> bit) % 2 == 0
            lower, upper = jnp.split(x, 2, axis)
            other = self.swap(jnp.where(first, upper, lower), bit)
            x = jnp.where(first, lower, upper) + other
        return x

    def gather(self, x, order):
        held = x
        for bit in order[:3]:
            held = jnp.concatenate([held, self.block_swap(held, bit)], 0)
        last = self.block_swap(held, order[3])
        return held, last, self.block_swap(held, order[4]), self.block_swap(last, order[4])

    def reduce(self, keep, send, order, fold, swap=None):
        swap = swap or self.block_swap
        other = swap(send, order[0])
        for bit in order[1:]:
            keep, send = fold(keep, other)
            other = swap(send, bit)
        return keep, other

    def gather_group(self, x):
        near = x
        mask = self.group // 2
        while mask > 1:
            near = jnp.concatenate([near, self.swap(near, mask.bit_length() - 1)], 0)
            mask //= 2
        return near, self.swap(near, 0)

    def group_masks(self):
        near = [0]
        mask = self.group // 2
        while mask > 1:
            near += [m ^ mask for m in near]
            mask //= 2
        return near, [m ^ 1 for m in near]


def gather_masks(order):
    held = [0]
    for bit in order[:3]:
        held = held + [m ^ (1 << bit) for m in held]
    last = [m ^ (1 << order[3]) for m in held]
    swapped = [[m ^ (1 << order[4]) for m in part] for part in (held, last)]
    return held, last, swapped[0], swapped[1]


def reduce_masks(order):
    bits = len(order)
    return [
        sum(((place >> (bits - 1 - k)) & 1) << bit for k, bit in enumerate(order))
        for place in range(1 << bits)
    ]


def place_blocks(target, parts, order, block, unit, lanes):
    for part, masks in zip(parts, gather_masks(order)):
        for place, mask in enumerate(masks):
            target[aligned(block ^ mask, unit), :] = part[place, :, lanes]


def emit_blocks(source, keep, send, order, block, unit, at, lanes):
    masks = reduce_masks(order)
    half = len(masks) // 2
    for place, mask in enumerate(masks):
        target = keep if place < half else send
        target[place % half, at, lanes] = source[aligned(block ^ mask, unit), :]


def emit_pairs(source, keep, send, orders, pair, core, unit, at):
    masks = [reduce_masks(order) for order in orders]
    count = len(masks[0]) // 2
    for spot, (first, second) in enumerate(zip(*masks)):
        target = keep if spot < count else send
        whose = pair ^ jnp.where(core == 0, first, second)
        target[spot % count, at, :] = source[aligned(whose, unit), :]


def roll_lanes(v, shift):
    return pltpu.roll(v, shift % LANES, 1) if shift % LANES else v


def lane_index(shape):
    return lax.broadcasted_iota(jnp.int32, shape, 1)


def normalize(hidden):
    center = hidden - jnp.mean(hidden, axis=-1, keepdims=True)
    inverse = lax.rsqrt(jnp.mean(center * center, axis=-1, keepdims=True) + 1e-05)
    return center * inverse, inverse


def norm_back(grad_normed, normed, inverse):
    mean_grad = jnp.mean(grad_normed, axis=-1, keepdims=True)
    mean_cross = jnp.mean(grad_normed * normed, axis=-1, keepdims=True)
    return inverse * (grad_normed - mean_grad - normed * mean_cross)


def half_masks():
    first = lane_index((1, LANES)) < HEAD_DIM
    return low(jnp.where(first, 1.0, 0.0)), low(jnp.where(first, 0.0, 1.0))


def both_heads(pair, scale=1.0):
    first, second = half_masks()
    return jnp.concatenate([pair * (first * scale), pair * (second * scale)], 0)


def join_heads(pair):
    half = pair.shape[0] // 2
    return jnp.where(lane_index((half, LANES)) < HEAD_DIM, pair[:half], pair[half:])


def head_column(columns, pair):
    lanes = lane_index(columns.shape)
    picked = [
        jnp.sum(jnp.where(lanes == 2 * pair + k, columns, 0.0), axis=1, keepdims=True)
        for k in range(2)
    ]
    return jnp.concatenate(picked, 0)


def key_valid(shape, axis, slot, group, length, slot_len, mem_rows):
    place = lax.broadcasted_iota(jnp.int32, shape, axis)
    half = (place >> 6) & 1
    position = ((half ^ slot) * group + (place >> 7)) * HEAD_DIM + (place & 63)
    token = jnp.logical_and(place < slot_len, position < length)
    mem = jnp.logical_and(place >= slot_len, place < slot_len + mem_rows)
    return jnp.logical_or(token, mem)


def own_valid(shape, slot, group, rank, length, mem_rows):
    place = lax.broadcasted_iota(jnp.int32, shape, 0)
    half = (place >> 6) & 1
    position = ((half ^ slot) * group + rank) * HEAD_DIM + (place & 63)
    token = jnp.logical_and(place < ROWS, position < length)
    mem = jnp.logical_and(place >= ROWS, place < ROWS + mem_rows)
    return jnp.logical_or(token, mem)


def forward_kernel(layout, mem_rows, slot_len, *refs):
    lengths, near, far, memory, w0, w1, w2, w3 = refs[:8]
    qkv, attn, lse_col, vectors, up_bias = refs[8:13]
    rows, weight, extra = refs[13:]
    group = layout.group
    place = lax.axis_index("seq")
    slot, rank = place // group, place % group
    block = layout.block()
    length = lengths[slot]
    parts = (w0, w1, w2, w3)
    place_blocks(weight, parts, GATHER_QKV, block, 16, slice(0, 3 * WIDTH))
    place_blocks(extra, parts, GATHER_QKV, block, 16, slice(4 * WIDTH, FIRST))
    for part, masks in zip((near, far), layout.group_masks()):
        for k, mask in enumerate(masks):
            rows[aligned(rank ^ mask, ROWS), :] = part[k]
    rows[slot_len : slot_len + MEM_PAD, :] = memory[slot]

    pieces, ups = [], []
    for g in range(4):
        total = jnp.zeros((8, LANES), F32)
        for p in range(8):
            total += roll_lanes(high(extra[(8 * g + p) * 16 : (8 * g + p + 1) * 16, :])[:8], 16 * p)
        pieces.append(total)
    for g in range(16):
        total = jnp.zeros((8, LANES), F32)
        for p in range(2):
            at = (2 * g + p) * 16
            total += roll_lanes(high(extra[at : at + 16, :])[8:], 64 * p)
        ups.append(total)
    vector_rows = jnp.concatenate(pieces, 1)
    vectors[...] = vector_rows
    up_bias[...] = jnp.concatenate(ups, 1)

    key_rows = slot_len + MEM_KEYS
    filled = slot_len + MEM_PAD
    qkv[filled:key_rows, :] = jnp.zeros((key_rows - filled, 3 * WIDTH), BF)
    shifts = (vector_rows[0:1], None, vector_rows[1:2])
    step = 544 if filled == 544 else 512
    for start in range(0, filled, step):
        size = min(step, filled - start)
        for part, shift in enumerate(shifts):
            lanes = slice(part * WIDTH, (part + 1) * WIDTH)
            value = dot(rows[start : start + size, :], weight[:, lanes])
            qkv[start : start + size, lanes] = low(value if shift is None else value + shift)

    keep = key_valid((1, key_rows), 1, slot, group, length, slot_len, mem_rows)
    bias = jnp.where(keep, 0.0, -1e30)
    log_columns = jnp.zeros((OWN, LANES), F32)
    for pair in range(HEADS // 2):
        at = pair * LANES
        own = jnp.concatenate(
            [qkv[aligned(rank, ROWS), at : at + LANES], qkv[slot_len:filled, at : at + LANES]], 0
        )
        keys = qkv[:, WIDTH + at : WIDTH + at + LANES]
        values = qkv[:, 2 * WIDTH + at : 2 * WIDTH + at + LANES]
        scores = dot(both_heads(own, 0.125), keys, NT) + bias
        highest = jnp.max(scores, axis=1, keepdims=True)
        expos = jnp.exp(scores - highest)
        total = jnp.sum(expos, axis=1, keepdims=True)
        attn[:, at : at + LANES] = join_heads(dot(low(expos), values) / total)
        log_total = highest + jnp.log(total)
        lanes = lane_index((OWN, LANES))
        log_columns = jnp.where(lanes == 2 * pair, log_total[:OWN], log_columns)
        log_columns = jnp.where(lanes == 2 * pair + 1, log_total[OWN:], log_columns)
    lse_col[...] = log_columns


def feed_kernel(layout, mem_rows, *refs):
    lengths, tokens, arrived, memory, cots, cot_arrived, cot_memory = refs[:7]
    attn, lse_col, vectors, up_bias = refs[7:11]
    outs, ups, downs = refs[11:15], refs[15:19], refs[19:23]
    pack, grad_mem, lse_mem, delta_mem, delta_col, first_grad, out_own, out_send = refs[23:31]
    attn_low, branch_low, hidden_low, grad_linear, active, feed_low, vector_grads, up_grads = refs[
        31:39
    ]
    w_out, w_up, w_down, slope = refs[39:]
    group = layout.group
    place = lax.axis_index("seq")
    slot, rank = place // group, place % group
    block = layout.block()
    length = lengths[slot]
    place_blocks(w_out, outs, GATHER_QKV, block, 16, slice(3 * WIDTH, 4 * WIDTH))
    place_blocks(w_up, ups, GATHER_UP, block, 16, slice(0, FF))
    place_blocks(w_down, downs, GATHER_DOWN, block, 64, slice(0, WIDTH))

    vec = vectors[...]
    out_bias, gain_one, shift_one, down_bias, gain_two, shift_two = [
        vec[k : k + 1] for k in range(2, 8)
    ]
    rows = jnp.concatenate([high(tokens[slot]), high(arrived[...]), high(memory[slot])], 0)
    cot = jnp.concatenate([high(cots[slot]), high(cot_arrived[...]), high(cot_memory[slot])], 0)
    valid = jnp.where(own_valid((OWN, 1), slot, group, rank, length, mem_rows), 1.0, 0.0)
    share = 1.0 / group
    row = lax.broadcasted_iota(jnp.int32, (OWN, 1), 0)
    weight = jnp.where(row < ROWS, 1.0, share)
    weight_low = low(weight)

    def total(v):
        return jnp.sum(v * weight, axis=0, keepdims=True)

    heads_out = attn[...]
    attn_low[...] = low(heads_out)
    branch = dot(attn_low[...], w_out[...]) + out_bias
    normed_one, inverse_one = normalize(rows + branch)
    hidden_one = normed_one * gain_one + shift_one
    hidden_low[...] = low(hidden_one)
    feed = jnp.zeros((OWN, WIDTH), F32) + down_bias
    for at in range(0, FF, WIDTH):
        cols = slice(at, at + WIDTH)
        t = dot(hidden_low[...], w_up[:, cols]) + up_bias[0:1, cols]
        square = t * t
        bent = jnp.tanh(0.7978845608 * (t + 0.044715 * (square * t)))
        half = 0.5 * (1.0 + bent)
        slope[:, cols] = half + (0.5 * 0.7978845608) * t * (1.0 - bent * bent) * (
            1.0 + (3 * 0.044715) * square
        )
        act = low(t * half)
        active[:, cols] = act
        feed += dot(act, w_down[cols, :])
    normed_two, inverse_two = normalize(hidden_one + feed)
    output = (normed_two * gain_two + shift_two) * valid
    out_own[:HEAD_DIM, :] = low(output[:HEAD_DIM])
    out_own[HEAD_DIM:, :] = low(output[ROWS:])
    out_send[...] = low(output[HEAD_DIM:])
    token_valid = jnp.where(row < ROWS, valid, 0.0)
    squares = jnp.sum(feed * feed * token_valid, axis=0, keepdims=True)

    g = cot * valid
    grads = [None] * 8
    grads[6] = total(g * normed_two)
    grads[7] = total(g)
    second = norm_back(g * gain_two, normed_two, inverse_two)
    grad_feed = low(second)
    feed_low[...] = grad_feed * weight_low
    grads[5] = total(high(grad_feed))
    grad_hidden = second
    for at in range(0, FF, WIDTH):
        cols = slice(at, at + WIDTH)
        linear = low(dot(grad_feed, w_down[cols, :], NT) * slope[:, cols])
        grad_linear[:, cols] = linear * weight_low
        up_grads[:, cols] = jnp.broadcast_to(total(high(linear)), (8, WIDTH))
        grad_hidden += dot(linear, w_up[:, cols], NT)
    grads[3] = total(grad_hidden * normed_one)
    grads[4] = total(grad_hidden)
    first = norm_back(grad_hidden * gain_one, normed_one, inverse_one)
    first_grad[...] = first
    grad_branch = low(first)
    branch_low[...] = grad_branch * weight_low
    grads[2] = total(high(grad_branch))
    grads[0] = grads[1] = jnp.zeros((1, WIDTH), F32)
    vector_grads[...] = jnp.concatenate(grads, 0)

    grad_attn = low(dot(grad_branch, w_out[...], NT))
    product = high(grad_attn) * heads_out
    chosen = lax.broadcasted_iota(jnp.int32, (16, WIDTH), 0)
    head = lax.broadcasted_iota(jnp.int32, (16, WIDTH), 1) // HEAD_DIM
    pick = low(jnp.where(chosen == head, 1.0, 0.0))
    down = lax.broadcasted_iota(jnp.int32, (WIDTH, LANES), 0) // HEAD_DIM
    pick_col = low(jnp.where(down == lane_index((WIDTH, LANES)), 1.0, 0.0))
    identity = low(
        jnp.where(
            lax.broadcasted_iota(jnp.int32, (16, LANES), 0) == lane_index((16, LANES)), 1.0, 0.0
        )
    )
    terms = [low(v) for v in split_three(product)]
    delta_col[...] = sum(dot(v, pick_col) for v in terms)
    delta_row = sum(dot(pick, v, NT) for v in terms)[:8]
    log_row = sum(dot(identity, low(v), NT) for v in split_three(lse_col[...]))[:8]
    log_terms = split_three(log_row[:, :ROWS])
    delta_terms = split_three(delta_row[:, :ROWS])
    square_terms = split_three(squares)
    square_rows = jnp.concatenate(
        [v[:, k * LANES : (k + 1) * LANES] for v in square_terms[:2] for k in range(4)], 0
    )
    pack[0, :ROWS, :] = grad_attn[:ROWS]
    pack[0, ROWS:, :] = low(
        jnp.concatenate(
            [
                jnp.concatenate([*log_terms, delta_terms[0]], 1),
                jnp.concatenate(
                    [delta_terms[1], delta_terms[2], square_rows, jnp.zeros((8, LANES), F32)], 1
                ),
            ],
            0,
        )
    )
    grad_mem[...] = grad_attn[ROWS:]
    blank = jnp.zeros((8, LANES - MEM_PAD), F32)
    lse_mem[...] = jnp.concatenate([log_row[:, ROWS:], blank], 1)
    delta_mem[...] = jnp.concatenate([delta_row[:, ROWS:], blank], 1)


def weight_kernel(layout, *refs):
    attn_low, branch_low, hidden_low, grad_linear, active, feed_low = refs[:6]
    up_keep, up_send, down_keep, down_send = refs[6:10]
    up, down, out = refs[10:]
    block = layout.block()
    for at in range(0, FF, WIDTH):
        cols = slice(at, at + WIDTH)
        down[cols, :] = low(dot(active[:, cols], feed_low[...], TN))
    out[...] = low(dot(attn_low[...], branch_low[...], TN))
    every = slice(0, WIDTH)
    emit_blocks(down, down_keep, down_send, REDUCE_DOWN, block, 64, slice(0, 64), every)
    emit_blocks(out, down_keep, down_send, REDUCE_DOWN, block, 16, slice(64, 80), every)
    for at in range(0, FF, WIDTH):
        cols = slice(at, at + WIDTH)
        up[:, cols] = low(dot(hidden_low[...], grad_linear[:, cols], TN))
    emit_blocks(up, up_keep, up_send, REDUCE_UP, block, 16, slice(0, 16), slice(0, FF))


def backward_kernel(layout, mem_rows, slot_len, *refs):
    lengths, tokens, arrived, memory, qkv, near, far, grad_mem, lse_mem, delta_mem = refs[:10]
    lse_col, delta_col, first_grad, vector_grads, up_grads = refs[10:15]
    parts = refs[15:19]
    keep_out, send_out, own_out, give_out = refs[19:23]
    weight, grad_rows, log_row, delta_row, squares, packed, grad_weight, extra = refs[23:]
    group = layout.group
    place = lax.axis_index("seq")
    slot, rank = place // group, place % group
    block = layout.block()
    length = lengths[slot]
    filled = slot_len + MEM_PAD
    key_rows = slot_len + MEM_KEYS
    place_blocks(weight, parts, GATHER_QKV, block, 16, slice(0, 3 * WIDTH))
    for part, masks in zip((near, far), layout.group_masks()):
        for k, mask in enumerate(masks):
            at = rank ^ mask
            grad_rows[aligned(at, ROWS), :] = part[k, :ROWS, :]
            more = high(part[k, ROWS:, :])
            cell = [[more[8 * a : 8 * a + 8, LANES * b : LANES * (b + 1)] for b in range(4)] for a in range(2)]
            log_row[:, aligned(at, LANES)] = cell[0][0] + cell[0][1] + cell[0][2]
            delta_row[:, aligned(at, LANES)] = cell[0][3] + cell[1][0] + cell[1][1]
            squares[at] = cell[1][2]
    grad_rows[slot_len:filled, :] = grad_mem[...]
    grad_rows[filled:, :] = jnp.zeros((key_rows - filled, WIDTH), BF)
    log_row[:, slot_len:] = lse_mem[...]
    delta_row[:, slot_len:] = delta_mem[...]

    own_keep = jnp.where(own_valid((OWN, 1), slot, group, rank, length, mem_rows), 0.0, -1e30)
    own_bias = jnp.concatenate([own_keep, own_keep], 0)
    chunk = min(slot_len, 512)
    spans = [(s, chunk) for s in range(0, slot_len, chunk)]
    spans[-1] = (spans[-1][0], chunk + MEM_KEYS)

    def own_rows(ref, lanes):
        return jnp.concatenate([ref[aligned(rank, ROWS), lanes], ref[slot_len:filled, lanes]], 0)

    for pair in range(HEADS // 2):
        at = pair * LANES
        q_lanes = slice(at, at + LANES)
        k_lanes = slice(WIDTH + at, WIDTH + at + LANES)
        v_lanes = slice(2 * WIDTH + at, 2 * WIDTH + at + LANES)
        own_q = both_heads(own_rows(qkv, q_lanes), 0.125)
        own_k = both_heads(own_rows(qkv, k_lanes), 0.125)
        own_v = both_heads(own_rows(qkv, v_lanes))
        own_g = both_heads(own_rows(grad_rows, q_lanes))
        log_column = head_column(lse_col[...], pair)
        delta_column = head_column(delta_col[...], pair)
        d_query = jnp.zeros((2 * OWN, LANES), F32)
        d_key = jnp.zeros((2 * OWN, LANES), F32)
        d_value = jnp.zeros((2 * OWN, LANES), F32)
        for start, size in spans:
            span = slice(start, start + size)
            keep = (
                lax.broadcasted_iota(jnp.int32, (1, size), 1) + start
            )
            half = (keep >> 6) & 1
            position = ((half ^ slot) * group + (keep >> 7)) * HEAD_DIM + (keep & 63)
            good = jnp.logical_or(
                jnp.logical_and(keep < slot_len, position < length),
                jnp.logical_and(keep >= slot_len, keep < slot_len + mem_rows),
            )
            bias = jnp.where(good, 0.0, -1e30)
            keys, values = qkv[span, k_lanes], qkv[span, v_lanes]
            weights = jnp.exp(dot(own_q, keys, NT) + bias - log_column)
            slopes = dot(own_g, values, NT)
            scores = low(weights * (slopes - delta_column))
            d_query += dot(scores, keys)

            queries, grads = qkv[span, q_lanes], grad_rows[span, q_lanes]

            def row_pair(ref):
                return jnp.concatenate(
                    [
                        jnp.broadcast_to(ref[2 * pair + k : 2 * pair + k + 1, span], (OWN, size))
                        for k in range(2)
                    ],
                    0,
                )

            weights = jnp.exp(dot(own_k, queries, NT) + own_bias - row_pair(log_row))
            slopes = dot(own_v, grads, NT)
            scores = low(weights * (slopes - row_pair(delta_row)))
            d_value += dot(low(weights), grads)
            d_key += dot(scores, queries)
        packed[:, q_lanes] = low(join_heads(d_query) * 0.125)
        packed[:, k_lanes] = low(join_heads(d_key) * 0.125)
        packed[:, v_lanes] = low(join_heads(d_value))

    share = 1.0 / group
    row = lax.broadcasted_iota(jnp.int32, (OWN, 1), 0)
    row_weight = low(jnp.where(row < ROWS, 1.0, share))
    rows = jnp.concatenate([tokens[slot], arrived[...], memory[slot]], 0)
    scaled = packed[...] * row_weight
    for at in range(0, 3 * WIDTH, WIDTH):
        cols = slice(at, at + WIDTH)
        grad_weight[:, cols] = low(dot(rows, scaled[:, cols], TN))
    emit_blocks(
        grad_weight, keep_out, send_out, REDUCE_QKV, block, 16, slice(0, 16), slice(0, 3 * WIDTH)
    )
    query_bias = jnp.sum(high(scaled[:, :WIDTH]), axis=0, keepdims=True)
    value_bias = jnp.sum(high(scaled[:, 2 * WIDTH :]), axis=0, keepdims=True)
    vec = jnp.concatenate([query_bias, value_bias, vector_grads[2:8, :]], 0)
    ups = up_grads[...]
    lane8 = lane_index((8, LANES))
    for p in range(BLOCKS):
        g = p // 8
        top = roll_lanes(vec[:, g * LANES : (g + 1) * LANES], -16 * (p % 8))
        top = jnp.where(lane8 < 16, top, 0.0)
        g = p // 2
        bottom = roll_lanes(ups[:, g * LANES : (g + 1) * LANES], -64 * (p % 2))
        both = jnp.concatenate([top, bottom], 0)
        extra[p * 16 : (p + 1) * 16, :] = split_lanes(both)
    emit_blocks(
        extra,
        keep_out,
        send_out,
        REDUCE_QKV,
        block,
        16,
        slice(0, 16),
        slice(3 * WIDTH, 3 * WIDTH + LANES),
    )

    grad_in = first_grad[...] + dot(packed[...], weight[...], NT)
    square = squares[0]
    for k in range(1, group):
        square += squares[k]
    square = square[:4] + square[4:]
    square = jnp.concatenate([square[k : k + 1] for k in range(4)], 1)
    first, second, _ = split_three(square)
    tail = low(jnp.concatenate([first, second, jnp.zeros((14, WIDTH), F32)], 0))
    own_out[:64, :] = low(grad_in[:64])
    own_out[64:96, :] = low(grad_in[ROWS:])
    own_out[96:, :] = tail
    give_out[:96, :] = low(grad_in[64:])
    give_out[96:, :] = tail


def split_lanes(v):
    first = high(low(v))
    second = pltpu.roll(v - first, 64, v.ndim - 1)
    lanes = lax.broadcasted_iota(jnp.int32, v.shape, v.ndim - 1)
    return low(jnp.where(lanes < 64, first, second))


def fold_kernel(width, keep, other, keep_out, send_out):
    half = keep.shape[0] // 2
    for start, out in ((0, keep_out), (half, send_out)):
        span = slice(start, start + half)
        total = high(keep[span, :, :width]) + high(other[span, :, :width])
        out[:, :, :width] = low(total)
        for k in range(half):
            extra = high(keep[start + k, :, width:]) + high(other[start + k, :, width:])
            out[k, :, width:] = split_lanes(extra + pltpu.roll(extra, 64, 1))


def fold_with_extra(keep, other):
    shape = (keep.shape[0] // 2,) + keep.shape[1:]
    return pl.pallas_call(
        functools.partial(fold_kernel, 3 * WIDTH),
        out_shape=[jax.ShapeDtypeStruct(shape, BF)] * 2,
        name="fold",
    )(keep, other)


def fold_plain(keep, other):
    half = keep.shape[0] // 2
    return tuple(
        low(high(keep[part]) + high(other[part])) for part in (slice(0, half), slice(half, None))
    )


def emit_kernel(layout, mem_rows, *refs):
    lengths, out_own, out_got, grad_own, grad_got = refs[:5]
    out_tokens, out_memory, grad_tokens, grad_memory, rms = refs[5:]
    slot = lax.axis_index("seq") // layout.group
    for own, got, tokens, memory in (
        (out_own, out_got, out_tokens, out_memory),
        (grad_own, grad_got, grad_tokens, grad_memory),
    ):
        for source, at in ((own, slot), (got, 1 - slot)):
            tokens[at] = source[:64, :]
            memory[at] = low(high(source[64:96, :])[:mem_rows])
    result = []
    for source, at in ((grad_own, slot), (grad_got, 1 - slot)):
        tail = high(source[96:112, :])
        square = tail[0:1] + tail[1:2]
        result.append(jnp.sqrt(square / lengths[at].astype(F32)))
    row = lax.broadcasted_iota(jnp.int32, (2, WIDTH), 0)
    rms[...] = jnp.where(row == slot, result[0], result[1])


def call(kernel, name, outs, scratch, args, smem=1, limit=32, flops=0):
    vmem = pl.BlockSpec(memory_space=pltpu.VMEM)
    in_specs = [pl.BlockSpec(memory_space=pltpu.SMEM)] * smem + [vmem] * (len(args) - smem)
    size = sum(a.size * a.dtype.itemsize for a in args)
    return pl.pallas_call(
        kernel,
        out_shape=[jax.ShapeDtypeStruct(shape, kind) for shape, kind in outs],
        in_specs=in_specs,
        out_specs=[vmem] * len(outs),
        scratch_shapes=[pltpu.VMEM(shape, kind) for shape, kind in scratch],
        compiler_params=pltpu.CompilerParams(vmem_limit_bytes=limit * MIB),
        cost_estimate=pl.CostEstimate(flops=flops, bytes_accessed=size, transcendentals=0),
        name=name,
    )(*args)


def local_wide(
    layout,
    tokens,
    memory,
    lengths,
    w_qkv,
    b_query,
    b_value,
    w_out,
    b_out,
    gain_one,
    shift_one,
    w_up,
    b_up,
    w_down,
    b_down,
    gain_two,
    shift_two,
    cot_tokens,
    cot_memory,
):
    mem_rows = memory.shape[1]
    tok_rows = tokens.shape[1]
    slot_len = tok_rows * layout.seq
    key_rows = slot_len + MEM_KEYS
    partner = layout.seq_bits - 1
    slot = lax.axis_index("seq") // layout.group

    def pick(x, at):
        return lax.dynamic_index_in_dim(x, at, 0, False)

    arrived = layout.swap(pick(tokens, 1 - slot), partner)
    near, far = layout.gather_group(jnp.concatenate([pick(tokens, slot), arrived], 0)[None])

    vectors = jnp.stack(
        [b_query, b_value, b_out, gain_one, shift_one, b_down, gain_two, shift_two]
    )
    vectors = layout.join_low(vectors, 1)
    extra = jnp.concatenate(
        [
            jnp.pad(vectors, ((0, 0), (0, LANES - 16))),
            jnp.pad(layout.join_low(b_up, 0)[None], ((0, 7), (0, LANES - 64))),
        ],
        0,
    )
    first = jnp.concatenate([layout.join_low(w_qkv, 0), layout.join_low(w_out, 0), extra], 1)
    qkv_parts = layout.gather(first[None], GATHER_QKV)
    up_parts = layout.gather(layout.join_low(w_up, 0)[None], GATHER_UP)
    down_parts = layout.gather(layout.join_low(w_down, 0)[None], GATHER_DOWN)
    cot_arrived = layout.swap(pick(cot_tokens, 1 - slot), partner)
    pad_rows = ((0, 0), (0, MEM_PAD - mem_rows), (0, 0))
    memory_full = jnp.pad(memory, pad_rows)
    cot_memory_full = jnp.pad(cot_memory, pad_rows)

    qkv, attn, lse_col, vector_rows, up_bias = call(
        functools.partial(forward_kernel, layout, mem_rows, slot_len),
        "attention_forward",
        [
            ((key_rows, 3 * WIDTH), BF),
            ((OWN, WIDTH), F32),
            ((OWN, LANES), F32),
            ((8, WIDTH), F32),
            ((8, FF), F32),
        ],
        [((slot_len + MEM_PAD, WIDTH), BF), ((WIDTH, 3 * WIDTH), BF), ((WIDTH, LANES), BF)],
        (lengths, near, far, memory_full, *qkv_parts),
    )
    (
        pack,
        grad_mem,
        lse_mem,
        delta_mem,
        delta_col,
        first_grad,
        out_own,
        out_send,
        attn_low,
        branch_low,
        hidden_low,
        grad_linear,
        active,
        feed_low,
        vector_grads,
        up_grads,
    ) = call(
        functools.partial(feed_kernel, layout, mem_rows),
        "feed_forward",
        [
            ((1, ROWS + 16, WIDTH), BF),
            ((MEM_PAD, WIDTH), BF),
            ((8, LANES), F32),
            ((8, LANES), F32),
            ((OWN, LANES), F32),
            ((OWN, WIDTH), F32),
            ((64 + MEM_PAD, WIDTH), BF),
            ((64 + MEM_PAD, WIDTH), BF),
            ((OWN, WIDTH), BF),
            ((OWN, WIDTH), BF),
            ((OWN, WIDTH), BF),
            ((OWN, FF), BF),
            ((OWN, FF), BF),
            ((OWN, WIDTH), BF),
            ((8, WIDTH), F32),
            ((8, FF), F32),
        ],
        [((WIDTH, WIDTH), BF), ((WIDTH, FF), BF), ((FF, WIDTH), BF), ((OWN, FF), F32)],
        (
            lengths,
            tokens,
            arrived,
            memory_full,
            cot_tokens,
            cot_arrived,
            cot_memory_full,
            attn,
            lse_col,
            vector_rows,
            up_bias,
            *qkv_parts,
            *up_parts,
            *down_parts,
        ),
    )
    grads_near, grads_far = layout.gather_group(pack)
    out_got = layout.swap(out_send, partner)
    half = BLOCKS // 2
    up_keep, up_send, down_keep, down_send = call(
        functools.partial(weight_kernel, layout),
        "weight_gradients",
        [
            ((half, 16, FF), BF),
            ((half, 16, FF), BF),
            ((half, 80, WIDTH), BF),
            ((half, 80, WIDTH), BF),
        ],
        [((WIDTH, FF), BF), ((FF, WIDTH), BF), ((WIDTH, WIDTH), BF)],
        (attn_low, branch_low, hidden_low, grad_linear, active, feed_low),
        smem=0,
    )
    up_total = layout.reduce(up_keep, up_send, REDUCE_UP, fold_plain)
    down_total = layout.reduce(down_keep, down_send, REDUCE_DOWN, fold_plain)
    qkv_keep, qkv_send, grad_own, grad_send = call(
        functools.partial(backward_kernel, layout, mem_rows, slot_len),
        "attention_backward",
        [
            ((half, 16, 3 * WIDTH + LANES), BF),
            ((half, 16, 3 * WIDTH + LANES), BF),
            ((112, WIDTH), BF),
            ((112, WIDTH), BF),
        ],
        [
            ((WIDTH, 3 * WIDTH), BF),
            ((key_rows, WIDTH), BF),
            ((8, key_rows), F32),
            ((8, key_rows), F32),
            ((layout.group, 8, LANES), F32),
            ((OWN, 3 * WIDTH), BF),
            ((WIDTH, 3 * WIDTH), BF),
            ((WIDTH, LANES), BF),
        ],
        (
            lengths,
            tokens,
            arrived,
            memory_full,
            qkv,
            grads_near,
            grads_far,
            grad_mem,
            lse_mem,
            delta_mem,
            lse_col,
            delta_col,
            first_grad,
            vector_grads,
            up_grads,
            *qkv_parts,
        ),
    )
    qkv_total = layout.reduce(qkv_keep, qkv_send, REDUCE_QKV, fold_with_extra)
    grad_got = layout.swap(grad_send, partner)

    def add(pair):
        return high(pair[0][0]) + high(pair[1][0])

    up_sum = layout.reduce_low(add(up_total), 0)
    down_sum = add(down_total)
    out_sum = layout.reduce_low(down_sum[64:], 0)
    down_sum = layout.reduce_low(down_sum[:64], 0)
    qkv_sum = add(qkv_total)
    extra_sum = qkv_sum[:, 3 * WIDTH :]
    qkv_sum = layout.reduce_low(qkv_sum[:, : 3 * WIDTH], 0)
    vec = layout.reduce_low(extra_sum[:8, :16] + extra_sum[:8, 64:80], 1)
    up_vec = layout.reduce_low(extra_sum[8, :64] + extra_sum[8, 64:], 0)

    out_tokens, out_memory, grad_tokens, grad_memory, rms = call(
        functools.partial(emit_kernel, layout, mem_rows),
        "emit",
        [
            (tokens.shape, BF),
            (memory.shape, BF),
            (tokens.shape, BF),
            (memory.shape, BF),
            ((2, WIDTH), F32),
        ],
        [],
        (lengths, out_own, out_got, grad_own, grad_got),
    )
    return (
        out_tokens,
        out_memory,
        grad_tokens,
        grad_memory,
        qkv_sum,
        vec[0],
        vec[1],
        out_sum,
        vec[2],
        vec[3],
        vec[4],
        up_sum,
        up_vec,
        down_sum,
        vec[5],
        vec[6],
        vec[7],
        rms,
    )


FIRST = 4 * WIDTH + LANES


def prepare_kernel(layout, *refs):
    tokens, w_qkv, w_out = refs[:3]
    vectors, b_up = refs[3:11], refs[11]
    own, give = refs[12:14]
    up_cell, sems = refs[14:16]
    cells = refs[16:]
    slot = lax.axis_index("seq") // layout.group
    moves = [(b_up, up_cell)]
    for target in (own, give):
        moves.append((w_qkv, target.at[:, : 3 * WIDTH]))
        moves.append((w_out, target.at[:, 3 * WIDTH : 4 * WIDTH]))
    for k in range(4):
        rows = slice(16 * k, 16 * k + 16)
        lanes = slice(FIRST + k * WIDTH, FIRST + (k + 1) * WIDTH)
        moves.append((tokens.at[slot, rows], own.at[:, lanes]))
        moves.append((tokens.at[1 - slot, rows], give.at[:, lanes]))
    moves += [(v, cells[k]) for k, v in enumerate(vectors)]
    copies = [
        pltpu.make_async_copy(source, target, sems.at[k])
        for k, (source, target) in enumerate(moves)
    ]
    for copy in copies:
        copy.start()
    for copy in copies:
        copy.wait()
    blank = jnp.zeros((1, LANES - 16), F32)
    rows = [jnp.concatenate([high(v[...]).reshape(1, 16), blank], 1) for v in cells]
    rows.append(jnp.concatenate([high(up_cell[...]).reshape(1, 64), blank[:, :64]], 1))
    rows.append(jnp.zeros((7, LANES), F32))
    extra = low(jnp.concatenate(rows, 0))
    own[:, 4 * WIDTH : FIRST] = extra
    give[:, 4 * WIDTH : FIRST] = extra


def stacked_rows(value):
    return jnp.concatenate([value[:, k * WIDTH : (k + 1) * WIDTH] for k in range(4)], 0)


def gather_vectors(extra):
    pieces, ups = [], []
    for g in range(4):
        total = jnp.zeros((8, LANES), F32)
        for p in range(8):
            at = (8 * g + p) * 16
            total += roll_lanes(high(extra[at : at + 16, :])[:8], 16 * p)
        pieces.append(total)
    for g in range(16):
        total = jnp.zeros((8, LANES), F32)
        for p in range(2):
            at = (2 * g + p) * 16
            total += roll_lanes(high(extra[at : at + 16, :])[8:], 64 * p)
        ups.append(total)
    return jnp.concatenate(pieces, 1), jnp.concatenate(ups, 1)


def quad_forward_kernel(layout, mem_rows, slot_len, *refs):
    lengths, near, far, memory, w0, w1, w2, w3 = refs[:8]
    attn, qkv_own, rows, w_own, vectors, up_bias = refs[8:14]
    qkv, weight, extra = refs[14:]
    group = layout.group
    place = lax.axis_index("seq")
    slot, rank = place // group, place % group
    block = layout.block()
    length = lengths[slot]
    parts = (w0, w1, w2, w3)
    place_blocks(weight, parts, GATHER_QKV, block, 16, slice(0, 3 * WIDTH))
    place_blocks(extra, parts, GATHER_QKV, block, 16, slice(4 * WIDTH, FIRST))
    for part, masks in zip((near, far), layout.group_masks()):
        for k, mask in enumerate(masks):
            for part_half in range(2):
                at = aligned((rank ^ mask) * 2 + part_half, 64)
                rows[at, :] = stacked_rows(part[2 * k + part_half])
    rows[slot_len : slot_len + MEM_PAD, :] = memory[...]
    vector_rows, up_rows = gather_vectors(extra)
    vectors[...] = vector_rows
    up_bias[...] = up_rows

    key_rows = slot_len + MEM_KEYS
    filled = slot_len + MEM_PAD
    qkv[filled:key_rows, :] = jnp.zeros((key_rows - filled, 3 * WIDTH), BF)
    for part, shift in enumerate((vector_rows[0:1], None, vector_rows[1:2])):
        lanes = slice(part * WIDTH, (part + 1) * WIDTH)
        value = dot(rows[...], weight[:, lanes])
        qkv[:filled, lanes] = low(value if shift is None else value + shift)
    half = WIDTH // 2
    for part in range(3):
        own = aligned(2 * part + place % 2, half)
        qkv_own[:, part * half : (part + 1) * half] = qkv[:, own]
        w_own[:, part * half : (part + 1) * half] = weight[:, own]

    keep = key_valid((1, key_rows), 1, slot, group, length, slot_len, mem_rows)
    bias = jnp.where(keep, 0.0, -1e30)
    for pair in range(HEADS // 2):
        at = pair * LANES
        own = jnp.concatenate(
            [qkv[aligned(rank, ROWS), at : at + LANES], qkv[slot_len:filled, at : at + LANES]], 0
        )
        keys = qkv[:, WIDTH + at : WIDTH + at + LANES]
        values = qkv[:, 2 * WIDTH + at : 2 * WIDTH + at + LANES]
        scores = dot(both_heads(own, 0.125), keys, NT) + bias
        highest = jnp.max(scores, axis=1, keepdims=True)
        expos = jnp.exp(scores - highest)
        total = jnp.sum(expos, axis=1, keepdims=True)
        attn[:, at : at + LANES] = join_heads(dot(low(expos), values) / total)


STRIP = 32
PACK = 16

ACT_LANES = FF + 2 * WIDTH + WIDTH // 2
LINEAR_LANES = FF // 2 + WIDTH // 2


def hand_out(core, own, give, value, start):
    half = value.shape[1] // 2
    first, second = value[:, :half], value[:, half:]
    mine = core == 0
    own[:, start : start + half] = jnp.where(mine, first, second)
    give[:, start : start + half] = jnp.where(mine, second, first)


def row_weights(group):
    row = lax.broadcasted_iota(jnp.int32, (OWN, 1), 0)
    return jnp.where(row < ROWS, 1.0, 1.0 / group)


def quad_feed_kernel(layout, mem_rows, *refs):
    lengths, tokens, arrived, memory, cots, cot_arrived, cot_memory = refs[:7]
    attn, vectors, up_bias = refs[7:10]
    outs, ups, downs = refs[10:14], refs[14:18], refs[18:22]
    out_own, out_send, own, give, sums, squares_out, w_heads = refs[22:29]
    w_out, w_up, w_down, slope, second_out, normed_out, inverse_out = refs[29:36]
    inputs, cot, feed, linear = refs[36:]
    group = layout.group
    place = lax.axis_index("seq")
    slot, rank = place // group, place % group
    block = layout.block()
    length = lengths[slot]
    place_blocks(w_out, outs, GATHER_QKV, block, 16, slice(3 * WIDTH, 4 * WIDTH))
    place_blocks(w_up, ups, GATHER_UP, block, 16, slice(0, FF))
    place_blocks(w_down, downs, GATHER_DOWN, block, 64, slice(0, WIDTH))
    w_heads[...] = w_out[aligned(place % 2, WIDTH // 2), :]

    vec = vectors[...]
    out_bias, gain_one, shift_one, down_bias, gain_two, shift_two = [
        vec[k : k + 1] for k in range(2, 8)
    ]
    inputs[:64, :] = high(tokens[slot])
    inputs[64:ROWS, :] = high(stacked_rows(arrived[...]))
    inputs[ROWS:, :] = high(memory[...])
    cot[:64, :] = high(cots[slot])
    cot[64:ROWS, :] = high(cot_arrived[...])
    cot[ROWS:, :] = high(cot_memory[...])
    valid_all = jnp.where(own_valid((OWN, 1), slot, group, rank, length, mem_rows), 1.0, 0.0)
    weight_all = row_weights(group)
    strips = [slice(start, start + STRIP) for start in range(0, OWN, STRIP)]

    heads_out = low(attn[...])
    for target in (own, give):
        target[:, FF + WIDTH : FF + 2 * WIDTH] = heads_out
    feed[...] = dot(heads_out, w_out[...])
    for strip in strips:
        normed, inverse = normalize(inputs[strip, :] + (feed[strip, :] + out_bias))
        normed_out[strip, :] = normed
        inverse_out[strip, :] = jnp.broadcast_to(inverse, (STRIP, LANES))
        hidden = normed * gain_one + shift_one
        inputs[strip, :] = hidden
        hidden_low = low(hidden)
        own[strip, FF : FF + WIDTH] = hidden_low
        give[strip, FF : FF + WIDTH] = hidden_low
    for at in range(0, FF, WIDTH):
        cols = slice(at, at + WIDTH)
        linear[:, cols] = dot(own[:, FF : FF + WIDTH], w_up[:, cols])
    for at in range(0, FF, WIDTH):
        cols = slice(at, at + WIDTH)
        for strip in strips:
            t = linear[strip, cols] + up_bias[0:1, cols]
            square = t * t
            bent = jnp.tanh(0.7978845608 * (t + 0.044715 * (square * t)))
            half = 0.5 * (1.0 + bent)
            slope[strip, cols] = half + (0.5 * 0.7978845608) * t * (1.0 - bent * bent) * (
                1.0 + (3 * 0.044715) * square
            )
            act = low(t * half)
            own[strip, cols] = act
            give[strip, cols] = act
        product = dot(own[:, cols], w_down[cols, :])
        feed[...] = product if at == 0 else feed[...] + product
    squares = jnp.zeros((1, WIDTH), F32)
    parts = [jnp.zeros((1, WIDTH), F32)] * 3
    for strip in strips:
        valid, weight = valid_all[strip], weight_all[strip]
        branch = feed[strip, :] + down_bias
        normed, inverse = normalize(inputs[strip, :] + branch)
        output = low((normed * gain_two + shift_two) * valid)
        if strip.start < HEAD_DIM:
            out_own[strip, :] = output
        else:
            out_send[strip.start - HEAD_DIM : strip.stop - HEAD_DIM, :] = output
        if strip.start < ROWS:
            squares += jnp.sum(branch * branch * valid, axis=0, keepdims=True)
        else:
            out_own[HEAD_DIM:, :] = output
        g = cot[strip, :] * valid
        second = norm_back(g * gain_two, normed, inverse)
        second_out[strip, :] = second
        grad_feed = low(second)
        terms = high(grad_feed), g * normed, g
        parts = [
            part + jnp.sum(term * weight, axis=0, keepdims=True)
            for part, term in zip(parts, terms)
        ]
        scaled = grad_feed * low(weight)
        half = WIDTH // 2
        first_core = place % 2 == 0
        own[strip, FF + 2 * WIDTH :] = jnp.where(first_core, scaled[:, :half], scaled[:, half:])
        give[strip, FF + 2 * WIDTH :] = jnp.where(first_core, scaled[:, half:], scaled[:, :half])
    squares_out[...] = low(
        jnp.concatenate([*split_three(squares), jnp.zeros((13, WIDTH), F32)], 0)
    )
    sums[...] = jnp.concatenate([jnp.zeros((5, WIDTH), F32), *parts], 0)


def quad_slope_kernel(layout, *refs):
    vectors, sums, squares, w_out, w_up, w_down, slope, second_in, normed_in, inverse_in = refs[:10]
    pack, grad_mem, first_grad, own, give = refs[10:15]
    grad_linear, product, grad_hidden, halves = refs[15:]
    place = lax.axis_index("seq")
    core = place % 2
    weight = row_weights(layout.group)
    weight_low = low(weight)

    strips = [slice(start, start + STRIP) for start in range(0, OWN, STRIP)]
    grad_feed = low(second_in[...])
    for at in range(0, FF, WIDTH):
        cols = slice(at, at + WIDTH)
        product[:, cols] = dot(grad_feed, w_down[cols, :], NT)
    ups = []
    for at in range(0, FF, WIDTH):
        cols = slice(at, at + WIDTH)
        part = jnp.zeros((1, WIDTH), F32)
        for strip in strips:
            linear = low(product[strip, cols] * slope[strip, cols])
            grad_linear[strip, cols] = linear
            part += jnp.sum(high(linear) * weight[strip], axis=0, keepdims=True)
            halves[at // (FF // 2), strip, at % (FF // 2) : at % (FF // 2) + WIDTH] = (
                linear * weight_low[strip]
            )
        ups.append(part)
    grad_hidden[...] = dot(grad_linear[...], w_up[...], NT)
    own[:, : FF // 2] = halves[core]
    give[:, : FF // 2] = halves[1 - core]
    parts = [jnp.zeros((1, WIDTH), F32)] * 3
    for strip in strips:
        hidden = second_in[strip, :] + grad_hidden[strip, :]
        normed = normed_in[strip, :]
        first = norm_back(hidden * vectors[3:4, :], normed, inverse_in[strip, :1])
        first_grad[strip, :] = first
        grad_branch = low(first)
        terms = high(grad_branch), hidden * normed, hidden
        parts = [
            part + jnp.sum(term * weight[strip], axis=0, keepdims=True)
            for part, term in zip(parts, terms)
        ]
        scaled = grad_branch * weight_low[strip]
        half = WIDTH // 2
        own[strip, FF // 2 :] = jnp.where(core == 0, scaled[:, :half], scaled[:, half:])
        give[strip, FF // 2 :] = jnp.where(core == 0, scaled[:, half:], scaled[:, :half])
        if strip.start < ROWS:
            pack[0, strip, :] = grad_branch
        else:
            grad_mem[...] = grad_branch
    sizes = jnp.concatenate([*parts, sums[5:8, :], *ups], 0)
    blank = jnp.zeros((PACK - 13, WIDTH), F32)
    pack[0, ROWS:, :] = low(
        jnp.concatenate([high(squares[...])[:3], sizes, blank], 0)
    )


MAIN_ROWS = 176
REST_ROWS = 112
FEED_ROWS = MAIN_ROWS + REST_ROWS


def quad_weight_kernel(layout, *refs):
    acts, got_acts, linear, got_linear = refs[:4]
    main, rest = refs[4:6], refs[6:8]
    up, down, out = refs[8:]
    core = lax.axis_index("seq") % 2
    pair = layout.block() >> 1
    half = WIDTH // 2

    def both(first, second, start, size):
        cols = slice(start, start + size)
        return jnp.concatenate([first[:, cols], second[:, cols]], 0)

    def emit(source, target, unit, start):
        orders = PAIR_MAIN if target is main else PAIR_REST
        at = slice(start, start + unit)
        emit_pairs(source, *target, orders, pair, core, unit, at)

    grad_feed = both(acts, got_acts, FF + 2 * WIDTH, half)
    for start in range(0, FF, WIDTH):
        act = both(acts, got_acts, start, WIDTH)
        down[start : start + WIDTH, :] = low(dot(act, grad_feed, TN))
    emit(down, main, 128, 0)
    hidden = both(acts, got_acts, FF, WIDTH)
    for start in range(0, FF // 2, WIDTH):
        up[:, start : start + WIDTH] = low(dot(hidden, both(linear, got_linear, start, WIDTH), TN))
    heads_out = both(acts, got_acts, FF + WIDTH, WIDTH)
    value = low(dot(heads_out, both(linear, got_linear, FF // 2, half), TN))
    for p in range(BLOCKS):
        out[p % 2, p // 2 * 16 : p // 2 * 16 + 16, :] = value[16 * p : 16 * p + 16]
    for k in range(4):
        target, start = (main, 128) if k == 0 else (rest, 32 * k - 32)
        emit(up.at[:, half * k : half * (k + 1)], target, 32, start)
    emit(out.at[0], main, 16, 160)
    emit(out.at[1], rest, 16, 96)


def quad_backward_kernel(layout, mem_rows, slot_len, *refs):
    lengths, qkv, rows, w_own, w_heads, near, far, grad_mem = refs[:8]
    keep_out, send_out, in_keep, in_send, tail = refs[8:13]
    grad_rows, sums, packed, grad_weight, extra = refs[13:]
    group = layout.group
    place = lax.axis_index("seq")
    slot, rank = place // group, place % group
    core = place % 2
    pair = layout.block() >> 1
    length = lengths[slot]
    filled = slot_len + MEM_PAD
    key_rows = slot_len + MEM_KEYS
    half = WIDTH // 2
    for part, masks in zip((near, far), layout.group_masks()):
        for k, mask in enumerate(masks):
            at = rank ^ mask
            grad_rows[aligned(at, ROWS), :] = part[k, :ROWS, :]
            sums[at] = high(part[k, ROWS:, :])
    grad_rows[slot_len:filled, :] = grad_mem[...]

    keep = key_valid((1, key_rows), 1, slot, group, length, slot_len, mem_rows)
    bias = jnp.where(keep, 0.0, -1e30)
    grad_attn = low(dot(grad_rows[...], w_heads[...], NT))
    for k in range(2):
        at = [slice(part * half + k * LANES, part * half + (k + 1) * LANES) for part in range(3)]
        queries, keys, values = qkv[:filled, at[0]], qkv[:, at[1]], qkv[:, at[2]]
        d_query = jnp.zeros((filled, LANES), F32)
        d_key = jnp.zeros((key_rows, LANES), F32)
        d_value = jnp.zeros((key_rows, LANES), F32)
        for mask in half_masks():
            query = queries * (mask * 0.125)
            grads = grad_attn[:, k * LANES : (k + 1) * LANES] * mask
            scores = dot(query, keys, NT) + bias
            expos = jnp.exp(scores - jnp.max(scores, axis=1, keepdims=True))
            weights = expos * (1.0 / jnp.sum(expos, axis=1, keepdims=True))
            weights_low = low(weights)
            slopes = dot(grads, values, NT)
            delta = jnp.sum(high(weights_low) * slopes, axis=1, keepdims=True)
            slopes = low(weights * (slopes - delta))
            d_query += dot(slopes, keys) * (high(mask) * 0.125)
            d_key += dot(slopes, query, TN)
            d_value += dot(weights_low, grads, TN)
        packed[:, at[0]] = low(d_query)
        packed[:, at[1]] = low(d_key[:filled])
        packed[:, at[2]] = low(d_value[:filled])

    def emit(source, unit, at):
        emit_pairs(source, keep_out, send_out, PAIR_QKV, pair, core, unit, at)

    for part in range(3):
        lanes = slice(part * half, (part + 1) * half)
        grad_weight[...] = low(dot(rows[...], packed[:, lanes], TN))
        emit(grad_weight, 32, slice(32 * part, 32 * part + 32))
    for target, at in ((in_keep, rank), (in_send, rank ^ 1)):
        target[:ROWS, :] = low(dot(packed[aligned(at, ROWS), :], w_own[...], NT))
    grad_in = low(dot(packed[slot_len:filled, :], w_own[...], NT))
    in_keep[ROWS:, :] = grad_in
    in_send[ROWS:, :] = grad_in

    total = sums[0]
    for k in range(1, group):
        total += sums[k]
    square = total[0:1] + total[1:2] + total[2:3]
    tail[...] = low(jnp.concatenate([*split_three(square), jnp.zeros((13, WIDTH), F32)], 0))
    sizes = total[3:13]
    first_core = core == 0
    blank = jnp.zeros((1, half), F32)
    biases = []
    for part in (0, 2):
        value = packed[:, part * half : (part + 1) * half]
        value = jnp.sum(high(value), axis=0, keepdims=True)
        first, second = jnp.where(first_core, value, 0.0), jnp.where(first_core, 0.0, value)
        biases.append(jnp.concatenate([first, second], 1))
    vec = jnp.concatenate([*biases, sizes[:6]], 0)
    ups = jnp.concatenate([sizes[6:10], jnp.zeros((4, WIDTH), F32)], 0)
    lanes = lane_index((8, LANES))
    sublane = lax.broadcasted_iota(jnp.int32, (8, LANES), 0)
    for p in range(0, BLOCKS, 2):
        both = []
        for q in (p, p + 1):
            mine = core == q % 2
            g = q // 8
            columns = slice(g * LANES, (g + 1) * LANES)
            cell = roll_lanes(vec[:, columns], -16 * (q % 8))
            cell = jnp.where(sublane < 2, cell, jnp.where(mine, cell, 0.0))
            g = q % 8 // 2
            row = ups[q // 8 : q // 8 + 1, g * LANES : (g + 1) * LANES]
            row = jnp.broadcast_to(jnp.where(mine, row, 0.0), (8, LANES))
            up = jnp.zeros((8, LANES), F32)
            for k in range(4):
                up = jnp.where(sublane == k, roll_lanes(row, 16 - 64 * (q % 2) - 16 * k), up)
            both.append(jnp.where(lanes < 16, cell, jnp.where(lanes < 32, up, 0.0)))
        wide = jnp.concatenate(both, 1)
        extra[p * 8 : p * 8 + 16, :] = low(jnp.concatenate([wide, jnp.zeros_like(wide)], 0))
    emit(extra, 16, slice(96, 112))


def feed_rows(core):
    starts = [128, *(MAIN_ROWS + 32 * k for k in range(3))]
    at = [pl.ds(pl.multiple_of(start + 16 * core, 16), 16) for start in starts]
    at.append(pl.ds(pl.multiple_of(64 * core, 64), 64))
    at.append(pl.ds(pl.multiple_of(160 + 112 * core, 16), 16))
    return at


def qkv_rows(core):
    return [pl.ds(pl.multiple_of(FEED_ROWS + 32 * k + 16 * core, 16), 16) for k in range(3)]


EXTRA_ROWS = pl.ds(FEED_ROWS + 96, 16)


def turn_kernel(keep, other, send):
    start = 0
    core = 1 - lax.axis_index("seq") % 2
    for at in [*feed_rows(core), *qkv_rows(core), EXTRA_ROWS]:
        send[start : start + at.size, :] = low(high(keep[0, at, :]) + high(other[0, at, :]))
        start += at.size


def emit_kernel_quad(keep, other, got, w_up, w_down, w_out, w_qkv, *vectors):
    core = lax.axis_index("seq") % 2
    half = WIDTH // 2
    start = 0
    places = [*feed_rows(core), *qkv_rows(core), EXTRA_ROWS]
    for k, at in enumerate(places):
        total = high(keep[0, at, :]) + high(other[0, at, :])
        arrived = high(got[start : start + at.size, :])
        start += at.size
        if k < 4:
            target, own, theirs = w_up, 4 * core + k, 4 - 4 * core + k
        elif k < 6:
            target, own, theirs = (w_down, w_out)[k - 4], core, 1 - core
        elif k < 9:
            target, own, theirs = w_qkv, 2 * k - 12 + core, 2 * k - 11 - core
        else:
            total += arrived
            continue
        target[:, aligned(own, half)] = total
        target[:, aligned(theirs, half)] = arrived
    total = jnp.where(core == 0, total[:8, :LANES], total[:8, LANES:])
    for k in range(8):
        vectors[k][...] = total[k, :16]
    lanes = lane_index((1, LANES))
    ups = jnp.zeros((1, LANES), F32)
    for k in range(4):
        rolled = roll_lanes(total[k : k + 1], 16 * k - 16)
        ups = jnp.where(jnp.logical_and(lanes >= 16 * k, lanes < 16 * k + 16), rolled, ups)
    vectors[8][...] = ups[0, :64]


def emit_tokens_kernel(layout, *refs):
    lengths, out_own, grad_own, grad_got, tail = refs[:5]
    out_tokens, out_memory, grad_tokens, grad_memory, rms = refs[5:]
    slot = lax.axis_index("seq") // layout.group
    pieces = (
        (out_own, 0, 64, slot, out_tokens, out_memory),
        (grad_got, 112, 176, 1 - slot, out_tokens, out_memory),
        (grad_own, 0, 128, slot, grad_tokens, grad_memory),
        (grad_got, 0, 64, 1 - slot, grad_tokens, grad_memory),
    )
    cells = [[None, None], [None, None]]
    for k, (source, start, mem, at, tokens, _) in enumerate(pieces):
        tokens[at] = source[start : start + 64, :]
        cells[k // 2][k % 2] = high(source[mem : mem + 32, :])
    for (own, got), memory in zip(cells, (out_memory, grad_memory)):
        first = jnp.where(slot == 0, own, got)
        second = jnp.where(slot == 0, got, own)
        rows = memory.shape[0]
        memory[...] = low(jnp.stack([first[:rows], second[:rows]], 1))
    result = []
    for cell, at in ((tail[...], slot), (grad_got[96:112, :], 1 - slot)):
        cell = high(cell)
        square = cell[0:1] + cell[1:2] + cell[2:3]
        result.append(jnp.sqrt(square / lengths[at].astype(F32)))
    row = lax.broadcasted_iota(jnp.int32, (2, WIDTH), 0)
    rms[...] = jnp.where(row == slot, result[0], result[1])


def local_quad(
    layout,
    tokens,
    memory,
    lengths,
    w_qkv,
    b_query,
    b_value,
    w_out,
    b_out,
    gain_one,
    shift_one,
    w_up,
    b_up,
    w_down,
    b_down,
    gain_two,
    shift_two,
    cot_tokens,
    cot_memory,
):
    mem_rows = memory.shape[1]
    slot_len = tokens.shape[1] * layout.seq
    key_rows = slot_len + MEM_KEYS
    filled = slot_len + MEM_PAD
    partner = layout.seq_bits - 1
    slot = lax.axis_index("seq") // layout.group

    def pick(x, at):
        return lax.dynamic_index_in_dim(x, at, 0, False)

    small = (b_query, b_value, b_out, gain_one, shift_one, b_down, gain_two, shift_two)
    own, give = pl.pallas_call(
        functools.partial(prepare_kernel, layout),
        out_shape=[jax.ShapeDtypeStruct((16, FIRST + FF), BF)] * 2,
        in_specs=[pl.BlockSpec(memory_space=pl.ANY)] * 12,
        out_specs=[pl.BlockSpec(memory_space=pltpu.VMEM)] * 2,
        scratch_shapes=[pltpu.VMEM((64,), BF), pltpu.SemaphoreType.DMA((21,))]
        + [pltpu.VMEM((16,), BF)] * 8,
        name="prepare",
    )(tokens, w_qkv, w_out, *small, b_up)

    def after(x, *others):
        return lax.optimization_barrier((x, *others))[0]

    def doubled(held, bit):
        return jnp.concatenate([held, layout.block_swap(held, bit)], 0)

    def finish(held, order, *ready):
        last = after(layout.block_swap(held, order[3]), *ready)
        return held, last, layout.block_swap(held, 0), layout.block_swap(last, 0)

    second = doubled(w_up[None], GATHER_UP[0])
    third = doubled(w_down[None], GATHER_DOWN[0])
    got = layout.swap(give, partner)[None]
    arrived = got[0, :, FIRST:]
    held = jnp.concatenate([own[None], got], 0)
    first = doubled(held[:, :, :FIRST], GATHER_QKV[1])
    near = doubled(after(held[:, :, FIRST:], first), GATHER_QKV[1])
    far = layout.swap(near, 0)
    first = doubled(first, GATHER_QKV[2])
    second = doubled(doubled(second, GATHER_UP[1]), GATHER_UP[2])
    third = doubled(doubled(third, GATHER_DOWN[1]), GATHER_DOWN[2])
    cot_arrived = layout.swap(pick(after(cot_tokens, first), 1 - slot), partner)
    pad_rows = ((0, MEM_PAD - mem_rows), (0, 0))
    own_memory = jnp.pad(pick(memory, slot), pad_rows)
    own_cot_memory = jnp.pad(pick(cot_memory, slot), pad_rows)
    qkv_parts = finish(first, GATHER_QKV, cot_arrived)
    up_parts = finish(second, GATHER_UP)
    down_parts = finish(third, GATHER_DOWN)

    attn, qkv_own, rows, w_own, vector_rows, up_bias = call(
        functools.partial(quad_forward_kernel, layout, mem_rows, slot_len),
        "attention_forward",
        [
            ((OWN, WIDTH), F32),
            ((key_rows, 3 * WIDTH // 2), BF),
            ((filled, WIDTH), BF),
            ((WIDTH, 3 * WIDTH // 2), BF),
            ((8, WIDTH), F32),
            ((8, FF), F32),
        ],
        [((key_rows, 3 * WIDTH), BF), ((WIDTH, 3 * WIDTH), BF), ((WIDTH, LANES), BF)],
        (lengths, near, far, own_memory, *qkv_parts),
        flops=4 * 10**9,
    )
    (
        out_own,
        out_send,
        acts,
        acts_give,
        sums,
        squares,
        w_heads,
        w_out_all,
        w_up_all,
        w_down_all,
        slope,
        second_grad,
        normed_one,
        inverse_one,
    ) = call(
        functools.partial(quad_feed_kernel, layout, mem_rows),
        "feed_forward",
        [
            ((64 + MEM_PAD, WIDTH), BF),
            ((64 + MEM_PAD, WIDTH), BF),
            ((OWN, ACT_LANES), BF),
            ((OWN, ACT_LANES), BF),
            ((8, WIDTH), F32),
            ((16, WIDTH), BF),
            ((WIDTH // 2, WIDTH), BF),
            ((WIDTH, WIDTH), BF),
            ((WIDTH, FF), BF),
            ((FF, WIDTH), BF),
            ((OWN, FF), F32),
            ((OWN, WIDTH), F32),
            ((OWN, WIDTH), F32),
            ((OWN, LANES), F32),
        ],
        [
            ((OWN, WIDTH), F32),
            ((OWN, WIDTH), F32),
            ((OWN, WIDTH), F32),
            ((OWN, FF), F32),
        ],
        (
            lengths,
            tokens,
            arrived,
            own_memory,
            cot_tokens,
            cot_arrived,
            own_cot_memory,
            attn,
            vector_rows,
            up_bias,
            *qkv_parts,
            *up_parts,
            *down_parts,
        ),
        flops=3 * 10**9,
    )
    acts_got = layout.swap(acts_give, 0)
    pack, grad_mem, first_grad, linear, linear_give = call(
        functools.partial(quad_slope_kernel, layout),
        "feed_backward",
        [
            ((1, ROWS + PACK, WIDTH), BF),
            ((MEM_PAD, WIDTH), BF),
            ((OWN, WIDTH), F32),
            ((OWN, LINEAR_LANES), BF),
            ((OWN, LINEAR_LANES), BF),
        ],
        [
            ((OWN, FF), BF),
            ((OWN, FF), F32),
            ((OWN, WIDTH), F32),
            ((2, OWN, FF // 2), BF),
        ],
        (
            vector_rows,
            sums,
            squares,
            w_out_all,
            w_up_all,
            w_down_all,
            slope,
            second_grad,
            normed_one,
            inverse_one,
        ),
        smem=0,
        flops=3 * 10**9,
    )
    linear_got = layout.swap(linear_give, 0)
    grads_next = layout.swap(pack, 1)
    half = PAIRS // 2
    main_keep, main_send, rest_keep, rest_send = call(
        functools.partial(quad_weight_kernel, layout),
        "weight_gradients",
        [((half, MAIN_ROWS, WIDTH // 2), BF)] * 2 + [((half, REST_ROWS, WIDTH // 2), BF)] * 2,
        [((WIDTH, FF // 2), BF), ((FF, WIDTH // 2), BF), ((2, WIDTH // 2, WIDTH // 2), BF)],
        (acts, after(acts_got, pack), linear, linear_got),
        smem=0,
        flops=10**9,
    )
    grads_next = after(grads_next, main_send)
    grads_near = jnp.concatenate([pack, grads_next], 0)
    grads_far = layout.swap(grads_near, 0)
    qkv_keep, qkv_send, in_keep, in_send, tail = call(
        functools.partial(quad_backward_kernel, layout, mem_rows, slot_len),
        "attention_backward",
        [
            ((half // 2, 112, WIDTH // 2), BF),
            ((half // 2, 112, WIDTH // 2), BF),
            ((OWN, WIDTH), BF),
            ((OWN, WIDTH), BF),
            ((16, WIDTH), BF),
        ],
        [
            ((filled, WIDTH), BF),
            ((layout.group, PACK, WIDTH), F32),
            ((filled, 3 * WIDTH // 2), BF),
            ((WIDTH, WIDTH // 2), BF),
            ((8 * BLOCKS, WIDTH // 2), BF),
        ],
        (lengths, qkv_own, rows, w_own, w_heads, grads_near, grads_far, grad_mem),
        flops=0,
    )
    swap = layout.pair_swap_by_core

    def bits(orders, step):
        return tuple(order[step] for order in orders)

    main_other = swap(main_send, bits(PAIR_MAIN, 0))
    rest_other = swap(rest_send, bits(PAIR_REST, 0))
    main_keep, main_send = fold_plain(main_keep, main_other)
    rest_keep, rest_send = fold_plain(rest_keep, rest_other)
    qkv_send = after(qkv_send, main_send, rest_send)
    both_send = jnp.concatenate([main_send, rest_send, qkv_send], 1)
    both_other = swap(both_send, bits(PAIR_QKV, 0))
    main_keep, main_send = fold_plain(main_keep, both_other[:, :MAIN_ROWS])
    both_keep = jnp.concatenate([rest_keep, qkv_keep], 1)
    both_keep, both_send = fold_plain(both_keep, both_other[:, MAIN_ROWS:])
    second_ready = both_send
    main_other = swap(main_send, bits(PAIR_MAIN, 2))
    both_other = swap(both_send, bits(PAIR_QKV, 1))
    main_keep, main_send = fold_plain(main_keep, main_other)
    both_keep, both_send = fold_plain(both_keep, both_other)
    all_keep = jnp.concatenate([main_keep, both_keep], 1)
    all_send = jnp.concatenate([main_send, both_send], 1)

    in_got = layout.swap(in_send, 0)
    grad_own = low(high(in_keep) + high(in_got) + first_grad)
    grad_got = layout.swap(jnp.concatenate([grad_own[64:], tail, out_send], 0), partner)
    grad_got = after(grad_got, all_send)

    out_tokens, out_memory, grad_tokens, grad_memory, rms = call(
        functools.partial(emit_tokens_kernel, layout),
        "emit_tokens",
        [
            (tokens.shape, BF),
            ((mem_rows, 2, WIDTH), BF),
            (tokens.shape, BF),
            ((mem_rows, 2, WIDTH), BF),
            ((2, WIDTH), F32),
        ],
        [],
        (lengths, out_own, grad_own, grad_got, tail),
    )
    all_other = swap(all_send, bits(PAIR_MAIN, 3))
    order = (1, 0, 2)
    all_other, out_memory, grad_memory, rms = lax.optimization_barrier(
        (all_other, out_memory, grad_memory, rms)
    )
    out_memory, grad_memory = jnp.transpose(out_memory, order), jnp.transpose(grad_memory, order)
    (turned,) = call(
        turn_kernel, "turn", [((208, WIDTH // 2), BF)], [], (all_keep, all_other), smem=0
    )
    turned = layout.swap(turned, 0)
    up_sum, down_sum, out_sum, qkv_sum, *vec = call(
        emit_kernel_quad,
        "emit_weights",
        [(w_up.shape, F32), (w_down.shape, F32), (w_out.shape, F32), (w_qkv.shape, F32)]
        + [((16,), F32)] * 8
        + [((64,), F32)],
        [],
        (all_keep, all_other, turned),
        smem=0,
    )
    return (
        out_tokens,
        out_memory,
        grad_tokens,
        grad_memory,
        qkv_sum,
        vec[0],
        vec[1],
        out_sum,
        vec[2],
        vec[3],
        vec[4],
        up_sum,
        vec[8],
        down_sum,
        vec[5],
        vec[6],
        vec[7],
        rms,
    )


def solution(mesh):
    rows = P("dp", "seq", None)
    slots = P("dp", None, None)
    matrix = P(("dp", "seq"), None)
    vector = P(("dp", "seq"))
    weights = (
        matrix,
        vector,
        vector,
        matrix,
        vector,
        vector,
        vector,
        matrix,
        vector,
        matrix,
        vector,
        vector,
        vector,
    )
    layout = Layout(mesh)
    quad = layout.group == 4 and layout.devices == BLOCKS
    return jax.shard_map(
        functools.partial(local_quad if quad else local_wide, layout),
        mesh=mesh,
        in_specs=(rows, slots, P("dp"), *weights, rows, slots),
        out_specs=(rows, slots, rows, slots, *weights, P("dp", None)),
        check_vma=False,
    )
```
